512 devices in a mesh: sweep: 16 (over x_lo, y), cx: 16 (over x_hi, z), cy: 2 (over core).
Axes of the slice: x: 4 (x_hi: 2, x_lo: 2; x = x_hi * 2 + x_lo), y: 8, z: 8, core: 2. Of those that a mesh axis runs over, the one named last changes fastest.
Arguments:
- rhs_vectors: float32 [48, 32, 4, 16, 320], P('sweep', 'cx', 'cy'), may hold values from -6 to 6
- old_iterate: float32 [48, 32, 4, 16, 320], P('sweep', 'cx', 'cy'), may hold values from -6 to 6
- diag_inverse: bfloat16 [48, 32, 4, 320, 320], P('sweep', 'cx', 'cy'), may hold values from -0.051 to 1.051
- coupling: bfloat16 [48, 32, 4, 80, 480], P('sweep', 'cx', 'cy'), may hold values from -0.09 to 1.01
- lift_table: bfloat16 [480, 320], replicated, may hold values from -1 to 1, as said below
- upstream: int32 [48, 32, 4], P('sweep', 'cx', 'cy'), may hold values from 0 to 3, as said below
Outputs:
- new_iterate: float32 [48, 32, 4, 16, 320], P('sweep', 'cx', 'cy')
- residual: float32 [48, 32, 4, 16, 320], P('sweep', 'cx', 'cy')
The draws below stay inside these ranges and needn't reach their ends.
Inputs may be any that keep to these rules, and one draw needn't show every extreme that they name: `upstream`: for every layer and every aligned patch of 2 x 2 elements of the two cross dimensions, the values form a permutation of the positions p * 2 + q of the patch. `lift_table`: row f * 80 + t is nonzero only at the 4 element rows of trace entry t's variable whose two node indices along face f equal those of entry t.
All inputs are finite; a program needn't handle non-finite values.
Results may differ from the reference program's by a relative error of at most 0.0003.
Values sent between devices are 32-bit elements; how exact they have to be, the bound alone decides.
No kernel may reach another device: no remote copies, remote signals or barrier semaphores. Data moves between devices by JAX's collectives and lax.ppermute only.
A program may use at most 64 MiB of HBM per device.

```python
import math
import jax
import jax.numpy as jnp
import numpy as np
from jax import lax

NVAR = 5
NPOINT = 4
ROWS = 320
TRACE = 80
VECS = 16
LAYERS = 3
EX = 2
EY = 2
NLAYER = 48
NEX = 32
NEY = 4


def draw_diag_inverse(key, part):
    key = jax.random.fold_in(key, 11)
    jitter = jax.random.uniform(key, (NLAYER, NEX, NEY, ROWS, ROWS), jnp.float32, -0.05, 0.05)
    return (jitter + jnp.eye(ROWS, dtype=jnp.float32)).astype(jnp.bfloat16)


def draw_coupling(key, part):
    key = jax.random.fold_in(key, 23)
    jitter = jax.random.uniform(key, (NLAYER, NEX, NEY, TRACE, 6 * TRACE), jnp.float32, -1.0, 1.0)
    face_gains = jnp.repeat(jnp.array([0.92, 0.3, 0.3, 0.3, 0.3, 0.3], jnp.float32), TRACE)
    spread = jnp.repeat(jnp.array([0.085, 0.026, 0.026, 0.026, 0.026, 0.026], jnp.float32), TRACE)
    diagonal_part = jnp.tile(jnp.eye(TRACE, dtype=jnp.float32), (1, 6)) * face_gains
    return (diagonal_part + jitter * spread).astype(jnp.bfloat16)


def draw_lift_table(key, part):
    key = jax.random.fold_in(key, 53)
    key_size, key_sign, key_far = jax.random.split(key, 3)
    points = NPOINT
    row_ids = jnp.arange(ROWS, dtype=jnp.int32)
    variable_ids = row_ids // points ** 3
    index_i = row_ids // points ** 2 % points
    index_j = row_ids // points % points
    index_k = row_ids % points
    along_k = (variable_ids * points + index_i) * points + index_j
    along_i = (variable_ids * points + index_j) * points + index_k
    along_j = (variable_ids * points + index_i) * points + index_k
    trace_of = jnp.stack([along_k, along_k, along_i, along_i, along_j, along_j])
    normal_of = jnp.stack([index_k, index_k, index_i, index_i, index_j, index_j])
    magnitude = jax.random.uniform(key_size, (6, TRACE, points), jnp.float32, 0.3, 1.0)
    sign_flip = jnp.where(jax.random.bernoulli(key_sign, 0.5, (6, TRACE, points)), 1.0, -1.0).astype(jnp.float32)
    gain_square = 0.88 ** (2.0 / LAYERS)
    face_energy = 0.92 ** 2 + TRACE * 0.085 ** 2 / 3.0
    jitter_energy = TRACE * 0.1 ** 2 / 12.0
    far_square = (gain_square / face_energy - jitter_energy * (points - 1) * 0.4633) / (1.0 + jitter_energy)
    far_level = min(math.sqrt(max(far_square, 0.25)), 0.98)
    far_entry = far_level * (1.0 + 0.01 * jax.random.uniform(key_far, (TRACE,), jnp.float32, -1.0, 1.0))
    face_ids = jnp.arange(6, dtype=jnp.int32)[:, None, None]
    node_ids = jnp.arange(points, dtype=jnp.int32)[None, None, :]
    profile = jnp.where((face_ids == 0) & (node_ids == points - 1), far_entry[None, :, None], magnitude * sign_flip)
    picked = jnp.take_along_axis(profile, jnp.broadcast_to(normal_of[:, None, :], (6, TRACE, ROWS)), axis=2)
    matched = trace_of[:, None, :] == jnp.arange(TRACE, dtype=jnp.int32)[None, :, None]
    return jnp.where(matched, picked, 0.0).reshape(6 * TRACE, ROWS).astype(jnp.bfloat16)


def draw_upstream(key, part):
    key = jax.random.fold_in(key, 37)
    patch_size = EX * EY
    within = jnp.arange(EX, dtype=jnp.int32)[:, None] * EY + jnp.arange(EY, dtype=jnp.int32)[None, :]
    scores = jax.random.randint(key, (NLAYER, NEX // EX, EX, NEY // EY, EY), 0, 1 << 20, dtype=jnp.int32)
    scores = scores * patch_size + within[None, None, :, None, :]
    grouped = scores.transpose(0, 1, 3, 2, 4).reshape(NLAYER, NEX // EX, NEY // EY, patch_size)
    ordering = jnp.argsort(grouped, axis=-1).astype(jnp.int32)
    ordering = ordering.reshape(NLAYER, NEX // EX, NEY // EY, EX, EY).transpose(0, 1, 3, 2, 4)
    return ordering.reshape(NLAYER, NEX, NEY)


def levels(stream_key, shape, shards, least, high):
    factor_of, own = 1.0, jax.random.fold_in(stream_key, 6)
    for dim, blocks in shards:
        draws = jnp.exp(jax.random.uniform(jax.random.fold_in(own, dim), (blocks,), jnp.float32, least / len(shards), high / len(shards)))
        factor_of = factor_of * jnp.repeat(draws, shape[dim] // blocks).reshape([-1 if axis == dim else 1 for axis in range(len(shape))])
    return factor_of


def bell_draw(own_key, extent, deviation, most, cuts=(), kind=jnp.bfloat16):
    factor_of = levels(own_key, extent, cuts, -0.22, 0.18) if cuts else 1.0
    result = jax.random.normal(own_key, extent, jnp.float32) * deviation * factor_of
    return jnp.minimum(jnp.maximum(result, -most), most).astype(kind)


def setup_inputs(seed: int = 0) -> dict:
    key_of = jax.random.split(jax.random.key(seed), 7)
    return {
        "rhs_vectors": bell_draw(key_of[0], (NLAYER, NEX, NEY, VECS, ROWS), 1.0, 6.0, ((0, 16), (1, 16), (2, 2)), jnp.float32),
        "old_iterate": bell_draw(key_of[1], (NLAYER, NEX, NEY, VECS, ROWS), 1.0, 6.0, ((0, 16), (1, 16), (2, 2)), jnp.float32),
        "diag_inverse": draw_diag_inverse(jax.random.fold_in(key_of[6], 71), 0),
        "coupling": draw_coupling(jax.random.fold_in(key_of[6], 71), 0),
        "lift_table": draw_lift_table(jax.random.fold_in(key_of[6], 71), 0),
        "upstream": draw_upstream(jax.random.fold_in(key_of[6], 71), 0),
    }


HIGHEST = lax.Precision.HIGHEST


def face_table(components, points):
    height = components * points ** 3
    stride = components * points ** 2
    edge_at = points - 1
    selector = np.zeros((height, 6 * stride), np.float32)
    for c in range(components):
        for i in range(points):
            for j in range(points):
                for k in range(points):
                    source = ((c * points + i) * points + j) * points + k
                    placed = ((0, k == 0, i, j), (1, k == edge_at, i, j), (2, i == 0, j, k), (3, i == edge_at, j, k), (4, j == 0, i, k), (5, j == edge_at, i, k))
                    for f, inside, a, b in placed:
                        if inside:
                            selector[source, f * stride + (c * points + a) * points + b] = 1.0
    return selector


def lifted(stacked, coupling, lift_full):
    blocks = coupling.astype(jnp.float32).reshape(coupling.shape[:-1] + (6, TRACE))
    shaped = stacked.reshape(stacked.shape[:-1] + (6, TRACE))
    fluxes = jnp.einsum('...vfi,...ifo->...vfo', shaped, blocks, precision=HIGHEST)
    return jnp.dot(fluxes.reshape(stacked.shape), lift_full, precision=HIGHEST)


def neighbours(traces, up_x, up_y):
    zero_face = jnp.zeros(traces.shape[:-1] + (TRACE,), jnp.float32)
    inflow = traces[..., 0:TRACE]
    layer_ids = jnp.broadcast_to(jnp.arange(NLAYER - 1, dtype=jnp.int32)[:, None, None], up_x[1:].shape)
    from_below = zero_face.at[layer_ids, up_x[1:], up_y[1:]].set(inflow[1:])
    edge_x = zero_face[:, 0:1]
    from_west = jnp.concatenate([edge_x, traces[:, :-1, :, :, 3 * TRACE:4 * TRACE]], 1)
    from_east = jnp.concatenate([traces[:, 1:, :, :, 2 * TRACE:3 * TRACE], edge_x], 1)
    edge_y = zero_face[:, :, 0:1]
    from_south = jnp.concatenate([edge_y, traces[:, :, :-1, :, 5 * TRACE:6 * TRACE]], 2)
    from_north = jnp.concatenate([traces[:, :, 1:, :, 4 * TRACE:5 * TRACE], edge_y], 2)
    return jnp.concatenate([zero_face, from_below, from_west, from_east, from_south, from_north], -1)


def reference(rhs_vectors, old_iterate, diag_inverse, coupling, lift_table, upstream):
    selector = jnp.asarray(face_table(NVAR, NPOINT))
    lift_full = lift_table.astype(jnp.float32)
    index_x = jnp.arange(NEX, dtype=jnp.int32)[None, :, None]
    index_y = jnp.arange(NEY, dtype=jnp.int32)[None, None, :]
    up_x = ((index_x // EX) * EX + upstream // EY).astype(jnp.int32)
    up_y = ((index_y // EY) * EY + upstream % EY).astype(jnp.int32)
    old_stack = neighbours(jnp.dot(old_iterate, selector, precision=HIGHEST), up_x, up_y)

    def layer_step(previous, inputs):
        rhs_layer, stack_layer, inverse_layer, coupling_layer, across_x, across_y = inputs
        upwind_trace = previous[across_x, across_y]
        stack_full = stack_layer.at[..., 0:TRACE].set(upwind_trace)
        rhs_full = rhs_layer - lifted(stack_full, coupling_layer, lift_full)
        solved = jnp.einsum('...vk,...kj->...vj', rhs_full, inverse_layer.astype(jnp.float32), precision=HIGHEST)
        return solved[..., NPOINT - 1::NPOINT], solved

    inflow_zero = jnp.zeros((NEX, NEY, VECS, TRACE), jnp.float32)
    unused, new_iterate = lax.scan(layer_step, inflow_zero, (rhs_vectors, old_stack, diag_inverse, coupling, up_x, up_y))
    new_stack = neighbours(jnp.dot(new_iterate, selector, precision=HIGHEST), up_x, up_y)

    def layer_residual(pieces):
        return lifted(pieces[0], pieces[1], lift_full)

    residual = lax.map(layer_residual, (old_stack - new_stack, coupling))
    return new_iterate, residual
```

```python
import jax
import jax.numpy as jnp
from jax import lax
from jax.experimental import pallas as pl
from jax.experimental.pallas import tpu as pltpu
from jax.sharding import PartitionSpec as P

NPOINT = 4
ROWS = 320
TRACE = 80
VECS = 16
LAYERS = 3
EX = 2
EY = 2
PATCH = EX * EY
CELLS = LAYERS * PATCH
LANES = 128
DEEP = 2 * LANES
GROUP = 4
NODES = NPOINT**3
MAP_ROWS = TRACE + VECS
BF16 = jnp.bfloat16
F32 = jnp.float32

FACE_ROWS = ((0, 16, 4), (3, 16, 4), (0, 4, 1), (48, 4, 1), (0, 16, 1), (12, 16, 1))
SLOT_FACES = (0, 3, 2, 5, 4)


def split(x):
    high = x.astype(BF16)
    low = (x - high.astype(F32)).astype(BF16)
    return high, low


def stacked(x):
    return jnp.concatenate(split(x), axis=0)


def dot(a, b):
    return jnp.dot(a, b, preferred_element_type=F32)


def dot_rows(a, b):
    return lax.dot_general(a, b, (((1,), (1,)), ((), ())), preferred_element_type=F32)


def halves(x):
    rows = x.shape[0] // 2
    return x[:rows] + x[rows:]


def deep_rows(table):
    high, low = split(table)
    gap = jnp.zeros((LANES - TRACE, table.shape[1]), BF16)
    return jnp.concatenate([high, gap, low, gap], axis=0)


def deep_lhs(x):
    high, low = split(x)
    return jnp.concatenate(
        [jnp.concatenate([high, high], axis=1), jnp.concatenate([low, low], axis=1)], axis=0
    )


def times(x, deep):
    return halves(dot(deep_lhs(x), deep))


def lane_take(x, index):
    return jnp.take_along_axis(x, index, axis=1)


def lane_ids(rows):
    return lax.broadcasted_iota(jnp.int32, (rows, LANES), 1)


def blocks_of(x):
    rest = ROWS - 2 * LANES
    tail = jnp.concatenate([x[:, 2 * LANES :], jnp.zeros((x.shape[0], LANES - rest), x.dtype)], axis=1)
    return x[:, :LANES], x[:, LANES : 2 * LANES], tail


def face_of(blocks, face):
    start, a_step, b_step = FACE_ROWS[face]
    lane = lane_ids(blocks[0].shape[0])
    entry = lane & 15
    index = (lane >> 4 & 1) * NODES + start + (entry >> 2) * a_step + (entry & 3) * b_step
    first, second, third = [lane_take(block, index) for block in blocks]
    third = jnp.where(lane < TRACE, third, 0.0)
    return jnp.where(lane < 32, first, jnp.where(lane < 64, second, third))


def put_faces(layer, cells, up, traces, inner, outer, across, below):
    core = lax.axis_index("cy")
    even = lax.rem(lax.axis_index("cx"), 2) == 0
    blocks = blocks_of(jnp.concatenate(cells, axis=0))
    faces = [face_of(blocks, face) for face in SLOT_FACES]
    block = lambda e, s: faces[s][VECS * e : VECS * (e + 1)]
    for e in range(PATCH):
        for s in range(len(SLOT_FACES)):
            traces[layer * PATCH + e, :, s * LANES : (s + 1) * LANES] = stacked(block(e, s))
    for b in range(EY):
        east, west = block(EY + b, 1), block(b, 2)
        inner[layer * EY + b] = jnp.where(even, east, west)
        outer[layer * EY + b] = jnp.where(even, west, east)
    for a in range(EX):
        across[layer * EX + a] = jnp.where(core == 0, block(a * EY + 1, 3), block(a * EY, 4))
    if layer == 0:
        for e in range(PATCH):
            below[up[e]] = block(e, 0)


def open_kernel(links, old, up, traces, inner, outer, across, below):
    for at in range(CELLS):
        up[at] = links[at % PATCH // EY, at % EY, at // PATCH]
    for layer in range(LAYERS):
        cells = [old[layer * PATCH + e] for e in range(PATCH)]
        put_faces(layer, cells, up, traces, inner, outer, across, below)


def place_downstream(up, traces, from_above, down):
    for layer in range(1, LAYERS):
        for e in range(PATCH):
            down[(layer - 1) * PATCH + up[layer * PATCH + e]] = traces[layer * PATCH + e, :, 0:LANES]
    for e in range(PATCH):
        down[(LAYERS - 1) * PATCH + e] = stacked(from_above[e])


def lifted_layer(layer, traces, down, inner, outer, from_across, coupling, lift):
    core = lax.axis_index("cy")
    even = lax.rem(lax.axis_index("cx"), 2) == 0
    lane = lax.broadcasted_iota(jnp.int32, (2 * VECS, DEEP), 1)
    left, right = [], []
    for e in range(PATCH):
        a, b = e // EY, e % EY
        own = lambda cell, s: traces[layer * PATCH + cell, :, s * LANES : (s + 1) * LANES]
        near, far = inner[layer * EY + b], outer[layer * EY + b]
        slot1 = down[layer * PATCH + e]
        slot2 = own(b, 1) if a == 1 else stacked(jnp.where(even, far, near))
        slot3 = own(EY + b, 2) if a == 0 else stacked(jnp.where(even, near, far))
        other = from_across[layer * EX + a]
        slot4 = own(a * EY, 3) if b == 1 else stacked(jnp.where(core == 1, other, 0.0))
        slot5 = own(a * EY + 1, 4) if b == 0 else stacked(jnp.where(core == 0, other, 0.0))
        first = jnp.concatenate([slot1, slot2, slot3], axis=0)[:, :TRACE]
        second = jnp.concatenate([slot3, slot4, slot5], axis=0)[:, :TRACE]
        block = coupling[layer * PATCH + e]
        y = dot(first, block[:, :DEEP])
        r = 2 * VECS
        kept = jnp.where(
            lane < TRACE,
            0.0,
            jnp.where(lane < 2 * TRACE, y[:r], jnp.where(lane < 3 * TRACE, y[r : 2 * r], y[2 * r :])),
        )
        left.append(stacked(halves(kept)))
        z = dot(second, block[:, DEEP:])
        tail = lane[:, : 6 * TRACE - DEEP] + DEEP
        kept = jnp.where(
            tail < 4 * TRACE, z[:r], jnp.where(tail < 5 * TRACE, z[r : 2 * r], z[2 * r :])
        )
        right.append(stacked(halves(kept)))
    out = dot_rows(jnp.concatenate(left, axis=0), lift[:, :DEEP]) + dot_rows(
        jnp.concatenate(right, axis=0), lift[:, DEEP:]
    )
    return [halves(out[2 * VECS * e : 2 * VECS * (e + 1)]) for e in range(PATCH)]


def left_of(deep):
    high, low = deep[:TRACE], deep[LANES : LANES + TRACE]
    return jnp.concatenate(
        [jnp.concatenate([high, high], axis=1), jnp.concatenate([low, low], axis=1)], axis=0
    )


def transfer_kernel(up, diag, coupling, lift, weights, passing, composed, first_two):
    one = lax.broadcasted_iota(jnp.int32, (TRACE, TRACE), 0)
    two = lax.broadcasted_iota(jnp.int32, (TRACE, TRACE), 1)
    inflow = dot_rows((one == two).astype(F32).astype(BF16), lift[:, :TRACE]).astype(BF16)
    upper, lower = inflow[:NODES, :DEEP], inflow[NODES:, DEEP:]
    for at in range(CELLS):
        block = diag[at]
        lifted_rows = jnp.concatenate([dot(upper, block[:DEEP]), dot(lower, block[DEEP:])], axis=0)
        upwind = coupling[at][:, :LANES]
        weight = dot(jnp.concatenate([upwind, upwind], axis=1), deep_rows(lifted_rows))
        weights[at] = deep_rows(weight)
        passing[at] = deep_rows(face_of(blocks_of(weight), 1))
    for e in range(PATCH):
        first_two[e] = halves(dot(left_of(passing[up[PATCH + e]]), passing[PATCH + e]))
    for e in range(PATCH):
        composed[e] = -times(first_two[up[2 * PATCH + e]], passing[2 * PATCH + e])


def pack(maps, ends):
    lane = lane_ids(MAP_ROWS)
    fourth = maps[3]
    one = jnp.where(lane < TRACE, maps[0], pltpu.roll(fourth, TRACE, 1))
    two = jnp.where(lane < TRACE, maps[1], pltpu.roll(fourth, 2 * TRACE - LANES, 1))
    return jnp.concatenate([one, two, maps[2], ends], axis=0)


def unpack(packed):
    lane = lane_ids(MAP_ROWS)
    one, two, three = [packed[MAP_ROWS * at : MAP_ROWS * (at + 1)] for at in range(3)]
    fourth = jnp.where(
        lane < LANES - TRACE, pltpu.roll(one, LANES - TRACE, 1), pltpu.roll(two, 2 * LANES - 2 * TRACE, 1)
    )
    used = lane < TRACE
    maps = [jnp.where(used, x, 0.0) for x in (one, two, three, fourth)]
    return maps, packed[3 * MAP_ROWS : 3 * MAP_ROWS + 8]


def chosen(items, at):
    out = items[0]
    for number in range(1, PATCH):
        out = jnp.where(at == number, items[number], out)
    return out


def rows_of(ends):
    return [ends[at : at + 1] for at in range(PATCH)]


def ends_of(rows):
    return jnp.concatenate(list(rows) + [jnp.zeros((8 - PATCH, LANES), F32)], axis=0)


def placed(states, ends):
    out = []
    for position in range(PATCH):
        total = jnp.where(ends[0] == position, states[0], 0.0)
        for at in range(1, PATCH):
            total = total + jnp.where(ends[at] == position, states[at], 0.0)
        out.append(total)
    return out


def after(first, second):
    nothing = jnp.zeros((TRACE, LANES), F32)
    added = jnp.concatenate([nothing, second[TRACE:]], axis=0) if first.shape[0] > VECS else second[TRACE:]
    return times(first, deep_rows(second[:TRACE])) + added


def source_kernel(
    up, rhs, traces, outer, from_above, inner, from_across, diag, coupling, lift, passing, composed,
    solved, sources, packed, down, current, maps,
):
    place_downstream(up, traces, from_above, down)
    for layer in range(LAYERS):
        lifts = lifted_layer(layer, traces, down, inner, outer, from_across, coupling, lift)
        for e in range(PATCH):
            at = layer * PATCH + e
            y = halves(dot(stacked(rhs[at] - lifts[e]), diag[at]))
            solved[at] = y
            sources[at] = face_of(blocks_of(y), 1)
    for e in range(PATCH):
        current[e] = sources[e]
    for layer in range(1, LAYERS):
        moved = []
        for e in range(PATCH):
            at = layer * PATCH + e
            moved.append(sources[at] - times(current[up[at]], passing[at]))
        for e in range(PATCH):
            current[e] = moved[e]
    row = lax.broadcasted_iota(jnp.int32, (8, LANES), 0)
    ends = jnp.zeros((8, LANES), F32)
    for e in range(PATCH):
        start = up[up[PATCH + up[2 * PATCH + e]]]
        maps[start, 0:TRACE] = composed[e]
        maps[start, TRACE:MAP_ROWS] = current[e]
        ends = jnp.where(row == start, float(e), ends)
    packed[...] = pack([maps[e] for e in range(PATCH)], ends)


def joined(mine, theirs, bit):
    later = (lax.axis_index("sweep") >> bit & 1) == 1
    first, first_ends = unpack(jnp.where(later, theirs, mine))
    second, second_ends = unpack(jnp.where(later, mine, theirs))
    first_ends, second_ends = rows_of(first_ends), rows_of(second_ends)
    maps = [after(first[at], chosen(second, first_ends[at])) for at in range(PATCH)]
    return maps, [chosen(second_ends, first_ends[at]) for at in range(PATCH)], first, first_ends, later


def pair_kernel(mine, theirs, packed):
    maps, ends, *unused = joined(mine[...], theirs[...], 0)
    packed[...] = pack(maps, ends_of(ends))


def group_kernel(mine, theirs, packed, leaving):
    maps, ends, *unused = joined(mine[...], theirs[...], 1)
    packed[...] = pack(maps, ends_of(ends))
    for at, state in enumerate(placed([x[TRACE:] for x in maps], ends)):
        leaving[at] = state


def prefix_kernel(pair, theirs, prefixes, ends):
    me = lax.axis_index("sweep")
    partner, partner_ends = unpack(pair[...])
    row = lax.broadcasted_iota(jnp.int32, (MAP_ROWS, LANES), 0)
    same = (row == lane_ids(MAP_ROWS)).astype(F32)
    later = (me & 1) == 1
    own = [jnp.where(later, x, same) for x in partner]
    own_ends = [jnp.where(later, x, float(at)) for at, x in enumerate(rows_of(partner_ends))]
    first, first_ends = unpack(theirs[...])
    first_ends = rows_of(first_ends)
    later = (me >> 1 & 1) == 1
    out = []
    for at in range(PATCH):
        whole = after(first[at], chosen(own, first_ends[at]))
        prefixes[at] = jnp.where(later, whole, own[at])
        out.append(jnp.where(later, chosen(own_ends, first_ends[at]), own_ends[at]))
    ends[...] = ends_of(out)


def onward_kernel(entering, packed, leaving):
    maps, ends = unpack(packed[...])
    states = [after(entering[at], maps[at]) for at in range(PATCH)]
    for at, state in enumerate(placed(states, rows_of(ends))):
        leaving[at] = state


def finish_kernel(
    up, second, third, fourth, before, prefixes, ends, old, solved, sources, weights, passing,
    new, traces, inner, outer, across, below, arrived, current,
):
    maps, map_ends = unpack(before[...])
    states = [after(fourth[at], maps[at]) for at in range(PATCH)]
    last = placed(states, rows_of(map_ends))
    entering = [second[at] + third[at] + last[at] for at in range(PATCH)]
    states = [after(entering[at], prefixes[at]) for at in range(PATCH)]
    for at, state in enumerate(placed(states, rows_of(ends))):
        arrived[at] = state
    for layer in range(LAYERS):
        inflow = []
        for e in range(PATCH):
            link = up[layer * PATCH + e]
            inflow.append(arrived[link] if layer == 0 else current[link])
        if layer < LAYERS - 1:
            for e in range(PATCH):
                at = layer * PATCH + e
                current[e] = sources[at] - times(inflow[e], passing[at])
        changes = []
        for e in range(PATCH):
            at = layer * PATCH + e
            x = solved[at] - times(inflow[e], weights[at])
            new[at] = x
            changes.append(old[at] - x)
        put_faces(layer, changes, up, traces, inner, outer, across, below)


def residual_kernel(up, traces, outer, from_above, inner, from_across, coupling, lift, out, down):
    place_downstream(up, traces, from_above, down)
    for layer in range(LAYERS):
        lifts = lifted_layer(layer, traces, down, inner, outer, from_across, coupling, lift)
        for e in range(PATCH):
            out[layer * PATCH + e] = lifts[e]


VMEM = pl.BlockSpec(memory_space=pltpu.VMEM)
SMEM = pl.BlockSpec(memory_space=pltpu.SMEM)


def call(kernel, scalars, outs, scratch=(), scalar_outs=(), micros=1):
    def run(*args):
        return pl.pallas_call(
            kernel,
            in_specs=[SMEM] * scalars + [VMEM] * (len(args) - scalars),
            out_specs=[SMEM if i in scalar_outs else VMEM for i in range(len(outs))],
            out_shape=[jax.ShapeDtypeStruct(shape, kind) for shape, kind in outs],
            scratch_shapes=list(scratch),
            compiler_params=pltpu.CompilerParams(vmem_limit_bytes=16 * 1024 * 1024),
            cost_estimate=pl.CostEstimate(
                flops=micros * 1_000_000_000, bytes_accessed=micros * 3_600_000, transcendentals=0
            ),
        )(*args)

    return run


FACE_OUTS = [
    ((CELLS, 2 * VECS, len(SLOT_FACES) * LANES), BF16),
    ((LAYERS * EY, VECS, LANES), F32),
    ((LAYERS * EY, VECS, LANES), F32),
    ((LAYERS * EX, VECS, LANES), F32),
    ((PATCH, VECS, LANES), F32),
]
FIELD = ((CELLS, VECS, ROWS), F32)
STATES = ((PATCH, VECS, LANES), F32)
PACKED = ((3 * MAP_ROWS + 8, LANES), F32)
DOWN = pltpu.VMEM((CELLS, 2 * VECS, LANES), BF16)
HELD = pltpu.VMEM((PATCH, VECS, LANES), F32)


def exchange_sides(inner, outer, across, below):
    wide, deep = lax.axis_size("cx"), lax.axis_size("sweep")
    outer = lax.ppermute(outer, "cx", [(i, i + 1 if i % 2 else i - 1) for i in range(1, wide - 1)])
    below = lax.ppermute(below, "sweep", [(i + 1, i) for i in range(deep - 1)])
    inner = lax.ppermute(inner, "cx", [(i, i ^ 1) for i in range(wide)])
    across = lax.ppermute(across, "cy", [(0, 1), (1, 0)])
    return outer, below, inner, across


def swapped(packed, by):
    return lax.ppermute(packed, "sweep", [(i, i ^ by) for i in range(lax.axis_size("sweep"))])


def passed(states, source, target):
    return lax.ppermute(states, "sweep", [(GROUP * source + p, GROUP * target + p) for p in range(GROUP)])


def local(rhs_vectors, old_iterate, diag_inverse, coupling, lift_table, upstream):
    old = old_iterate.reshape(CELLS, VECS, ROWS)
    rhs = rhs_vectors.reshape(CELLS, VECS, ROWS)
    diag = diag_inverse.reshape(CELLS, ROWS, ROWS)
    blocks = coupling.reshape(CELLS, TRACE, 6 * TRACE)
    lift = lift_table.T
    up, traces, *sends = call(open_kernel, 1, [((CELLS,), jnp.int32)] + FACE_OUTS, scalar_outs=(0,), micros=2)(
        upstream.transpose(1, 2, 0), old
    )
    halos = exchange_sides(*sends)
    weights, passing, composed = call(
        transfer_kernel,
        1,
        [((CELLS, DEEP, ROWS), BF16), ((CELLS, DEEP, LANES), BF16), ((PATCH, TRACE, LANES), F32)],
        [pltpu.VMEM((PATCH, TRACE, LANES), F32)],
    )(up, diag, blocks, lift)
    solved, sources, single = call(
        source_kernel,
        1,
        [FIELD, ((CELLS, VECS, LANES), F32), PACKED],
        [DOWN, HELD, pltpu.VMEM((PATCH, MAP_ROWS, LANES), F32)],
    )(up, rhs, traces, *halos, diag, blocks, lift, passing, composed)
    partner = swapped(single, 1)
    (pair,) = call(pair_kernel, 0, [PACKED])(single, partner)
    partner_pair = swapped(pair, 2)
    group, leaving = call(group_kernel, 0, [PACKED, STATES])(pair, partner_pair)
    second = passed(leaving, 0, 1)
    before = passed(group, 2, 3)
    prefixes, ends = call(prefix_kernel, 0, [((PATCH, MAP_ROWS, LANES), F32), ((8, LANES), F32)])(
        partner, partner_pair
    )
    (leaving,) = call(onward_kernel, 0, [STATES])(second, group)
    third = passed(leaving, 1, 2)
    fourth = passed(leaving, 1, 3)
    new, traces, *sends = call(finish_kernel, 1, [FIELD] + FACE_OUTS, [HELD, HELD])(
        up, second, third, fourth, before, prefixes, ends, old, solved, sources, weights, passing
    )
    halos = exchange_sides(*sends)
    (residual,) = call(residual_kernel, 1, [FIELD], [DOWN])(up, traces, *halos, blocks, lift)
    shape = rhs_vectors.shape
    return new.reshape(shape), residual.reshape(shape)


def solution(mesh):
    field = P("sweep", "cx", "cy", None, None)
    return jax.shard_map(
        local,
        mesh=mesh,
        in_specs=(field, field, field, field, P(), P("sweep", "cx", "cy")),
        out_specs=(field, field),
        check_vma=False,
    )
```

```python
import jax
import jax.numpy as jnp
from jax import lax
from jax.experimental import pallas as pl
from jax.experimental.pallas import tpu as pltpu
from jax.sharding import PartitionSpec as P

NPOINT = 4
ROWS = 320
TRACE = 80
VECS = 16
LAYERS = 3
EX = 2
EY = 2
PATCH = EX * EY
CELLS = LAYERS * PATCH
LANES = 128
DEEP = 2 * LANES
GROUP = 4
NODES = NPOINT**3
MAP_ROWS = TRACE + VECS
BF16 = jnp.bfloat16
F32 = jnp.float32

FACE_ROWS = ((0, 16, 4), (3, 16, 4), (0, 4, 1), (48, 4, 1), (0, 16, 1), (12, 16, 1))
SLOT_FACES = (0, 3, 2, 5, 4)


def split(x):
    high = x.astype(BF16)
    low = (x - high.astype(F32)).astype(BF16)
    return high, low


def stacked(x):
    return jnp.concatenate(split(x), axis=0)


def dot(a, b):
    return jnp.dot(a, b, preferred_element_type=F32)


def dot_rows(a, b):
    return lax.dot_general(a, b, (((1,), (1,)), ((), ())), preferred_element_type=F32)


def halves(x):
    rows = x.shape[0] // 2
    return x[:rows] + x[rows:]


def deep_rows(table):
    high, low = split(table)
    gap = jnp.zeros((LANES - TRACE, table.shape[1]), BF16)
    return jnp.concatenate([high, gap, low, gap], axis=0)


def deep_lhs(x):
    high, low = split(x)
    return jnp.concatenate(
        [jnp.concatenate([high, high], axis=1), jnp.concatenate([low, low], axis=1)], axis=0
    )


def times(x, deep):
    return halves(dot(deep_lhs(x), deep))


def lane_take(x, index):
    return jnp.take_along_axis(x, index, axis=1)


def lane_ids(rows):
    return lax.broadcasted_iota(jnp.int32, (rows, LANES), 1)


def blocks_of(x):
    rest = ROWS - 2 * LANES
    tail = jnp.concatenate([x[:, 2 * LANES :], jnp.zeros((x.shape[0], LANES - rest), x.dtype)], axis=1)
    return x[:, :LANES], x[:, LANES : 2 * LANES], tail


def face_of(blocks, face):
    start, a_step, b_step = FACE_ROWS[face]
    lane = lane_ids(blocks[0].shape[0])
    entry = lane & 15
    index = (lane >> 4 & 1) * NODES + start + (entry >> 2) * a_step + (entry & 3) * b_step
    first, second, third = [lane_take(block, index) for block in blocks]
    third = jnp.where(lane < TRACE, third, 0.0)
    return jnp.where(lane < 32, first, jnp.where(lane < 64, second, third))


def side_table():
    row = lax.broadcasted_iota(jnp.int32, (ROWS, LANES), 0)
    lane = lane_ids(1)
    blocks = []
    for face in SLOT_FACES:
        start, a_step, b_step = FACE_ROWS[face]
        source = (lane >> 4) * NODES + start + (lane >> 2 & 3) * a_step + (lane & 3) * b_step
        source = jnp.where(lane < TRACE, source, -1)
        blocks.append(jnp.where(row == source, 1.0, 0.0).astype(BF16))
    return jnp.concatenate(blocks, axis=1)


def put_faces(cells, up, traces, inner, outer, across, below):
    core = lax.axis_index("cy")
    even = lax.rem(lax.axis_index("cx"), 2) == 0
    picked = dot(jnp.concatenate([stacked(x) for x in cells], axis=0), side_table())
    whole = []
    for at in range(CELLS):
        piece = picked[2 * VECS * at : 2 * VECS * (at + 1)]
        traces[at] = piece.astype(BF16)
        whole.append(halves(piece))
    for layer in range(LAYERS):
        block = lambda e, s: whole[layer * PATCH + e][:, s * LANES : (s + 1) * LANES]
        for b in range(EY):
            east, west = block(EY + b, 1), block(b, 2)
            inner[layer * EY + b] = jnp.where(even, east, west)
            outer[layer * EY + b] = jnp.where(even, west, east)
        for a in range(EX):
            across[layer * EX + a] = jnp.where(core == 0, block(a * EY + 1, 3), block(a * EY, 4))
    for e in range(PATCH):
        below[up[e]] = whole[e][:, :LANES]
    for e in range(PATCH, LAYERS * EY):
        below[e] = jnp.zeros((VECS, LANES), F32)


def open_kernel(links, old, up, traces, inner, outer, across, below):
    for at in range(CELLS):
        up[at] = links[at % PATCH // EY, at % EY, at // PATCH]
    put_faces([old[at] for at in range(CELLS)], up, traces, inner, outer, across, below)


def place_downstream(up, traces, from_above, down):
    for layer in range(1, LAYERS):
        for e in range(PATCH):
            down[(layer - 1) * PATCH + up[layer * PATCH + e]] = traces[layer * PATCH + e, :, 0:LANES]
    for e in range(PATCH):
        down[(LAYERS - 1) * PATCH + e] = stacked(from_above[e])


def lifted_layer(layer, traces, down, inner, outer, from_across, coupling, lift):
    core = lax.axis_index("cy")
    even = lax.rem(lax.axis_index("cx"), 2) == 0
    lane = lax.broadcasted_iota(jnp.int32, (2 * VECS, DEEP), 1)
    left, right = [], []
    for e in range(PATCH):
        a, b = e // EY, e % EY
        own = lambda cell, s: traces[layer * PATCH + cell, :, s * LANES : (s + 1) * LANES]
        near, far = inner[layer * EY + b], outer[layer * EY + b]
        slot1 = down[layer * PATCH + e]
        slot2 = own(b, 1) if a == 1 else stacked(jnp.where(even, far, near))
        slot3 = own(EY + b, 2) if a == 0 else stacked(jnp.where(even, near, far))
        other = from_across[layer * EX + a]
        slot4 = own(a * EY, 3) if b == 1 else stacked(jnp.where(core == 1, other, 0.0))
        slot5 = own(a * EY + 1, 4) if b == 0 else stacked(jnp.where(core == 0, other, 0.0))
        first = jnp.concatenate([slot1, slot2, slot3], axis=0)[:, :TRACE]
        second = jnp.concatenate([slot3, slot4, slot5], axis=0)[:, :TRACE]
        block = coupling[layer * PATCH + e]
        y = dot(first, block[:, :DEEP])
        r = 2 * VECS
        kept = jnp.where(
            lane < TRACE,
            0.0,
            jnp.where(lane < 2 * TRACE, y[:r], jnp.where(lane < 3 * TRACE, y[r : 2 * r], y[2 * r :])),
        )
        left.append(stacked(halves(kept)))
        z = dot(second, block[:, DEEP:])
        tail = lane[:, : 6 * TRACE - DEEP] + DEEP
        kept = jnp.where(
            tail < 4 * TRACE, z[:r], jnp.where(tail < 5 * TRACE, z[r : 2 * r], z[2 * r :])
        )
        right.append(stacked(halves(kept)))
    out = dot_rows(jnp.concatenate(left, axis=0), lift[:, :DEEP]) + dot_rows(
        jnp.concatenate(right, axis=0), lift[:, DEEP:]
    )
    return [halves(out[2 * VECS * e : 2 * VECS * (e + 1)]) for e in range(PATCH)]


def left_of(deep):
    high, low = deep[:TRACE], deep[LANES : LANES + TRACE]
    return jnp.concatenate(
        [jnp.concatenate([high, high], axis=1), jnp.concatenate([low, low], axis=1)], axis=0
    )


def transfer_kernel(up, diag, coupling, lift, weights, passing, composed, first_two):
    one = lax.broadcasted_iota(jnp.int32, (TRACE, TRACE), 0)
    two = lax.broadcasted_iota(jnp.int32, (TRACE, TRACE), 1)
    inflow = dot_rows((one == two).astype(F32).astype(BF16), lift[:, :TRACE]).astype(BF16)
    upper, lower = inflow[:NODES, :DEEP], inflow[NODES:, DEEP:]
    for at in range(CELLS):
        block = diag[at]
        lifted_rows = jnp.concatenate([dot(upper, block[:DEEP]), dot(lower, block[DEEP:])], axis=0)
        upwind = coupling[at][:, :LANES]
        weight = dot(jnp.concatenate([upwind, upwind], axis=1), deep_rows(lifted_rows))
        weights[at] = deep_rows(weight)
        passing[at] = deep_rows(face_of(blocks_of(weight), 1))
    for e in range(PATCH):
        first_two[e] = halves(dot(left_of(passing[up[PATCH + e]]), passing[PATCH + e]))
    for e in range(PATCH):
        composed[e] = -times(first_two[up[2 * PATCH + e]], passing[2 * PATCH + e])


def turned(x, by):
    return pltpu.roll(x, by % LANES, 1)


def pack(maps, ends):
    lane = lane_ids(TRACE)
    square = [x[:TRACE] for x in maps]
    source = [x[TRACE:] for x in maps]
    all_sources = jnp.concatenate(source, axis=0)
    part = lane_ids(VECS) >> 4
    last = jnp.where(part == 5, turned(source[0], 16), jnp.where(part == 6, turned(source[1], 32), turned(source[2], 48)))
    one = jnp.where(lane < TRACE, square[0], turned(square[3], TRACE))
    rest = jnp.concatenate([turned(all_sources, 64), turned(source[3], 48)], axis=0)
    two = jnp.where(lane < TRACE, square[1], jnp.where(lane < 112, turned(square[3], 32), rest))
    three = jnp.where(lane < TRACE, square[2], jnp.concatenate([turned(all_sources, TRACE), last], axis=0))
    return jnp.concatenate([one, two, three, ends], axis=0)


def unpack(packed):
    lane = lane_ids(TRACE)
    one, two, three = [packed[TRACE * at : TRACE * (at + 1)] for at in range(3)]
    four = jnp.where(lane < 48, turned(one, 48), turned(two, 96))
    square = [jnp.where(lane < TRACE, x, 0.0) for x in (one, two, three, four)]
    lane = lane_ids(PATCH * VECS)
    most = jnp.where(lane < 48, turned(three[: PATCH * VECS], 48), turned(two[: PATCH * VECS], 64))
    ends = [turned(three[PATCH * VECS :], by) for by in (112, 96, 80)] + [turned(two[PATCH * VECS :], 80)]
    lane = lane_ids(VECS)
    maps = []
    for at in range(PATCH):
        source = jnp.where(lane < 64, most[VECS * at : VECS * (at + 1)], jnp.where(lane < TRACE, ends[at], 0.0))
        maps.append(jnp.concatenate([square[at], source], axis=0))
    return maps, packed[3 * TRACE : 3 * TRACE + 8]


def pack_states(states):
    lane = lane_ids(VECS)
    one = jnp.where(lane < TRACE, states[0], turned(states[3], TRACE))
    two = jnp.where(lane < TRACE, states[1], turned(states[3], 32))
    return jnp.concatenate([one, two, states[2]], axis=0)


def unpack_states(packed):
    lane = lane_ids(VECS)
    one, two, three = [packed[VECS * at : VECS * (at + 1)] for at in range(3)]
    four = jnp.where(lane < 48, turned(one, 48), turned(two, 96))
    return [jnp.where(lane < TRACE, x, 0.0) for x in (one, two, three, four)]


def rows_of(ends):
    return [ends[at : at + 1] for at in range(PATCH)]


def ends_of(rows):
    return jnp.concatenate(list(rows) + [jnp.zeros((8 - PATCH, LANES), F32)], axis=0)


def chosen(items, at):
    out = items[0]
    for number in range(1, PATCH):
        out = jnp.where(at == number, items[number], out)
    return out


def placed(states, ends):
    out = []
    for position in range(PATCH):
        total = jnp.where(ends[0] == position, states[0], 0.0)
        for at in range(1, PATCH):
            total = total + jnp.where(ends[at] == position, states[at], 0.0)
        out.append(total)
    return out


def after(first, second):
    nothing = jnp.zeros((TRACE, LANES), F32)
    added = jnp.concatenate([nothing, second[TRACE:]], axis=0) if first.shape[0] > VECS else second[TRACE:]
    return times(first, deep_rows(second[:TRACE])) + added


def source_kernel(
    up, rhs, traces, from_above, outer, inner, from_across, diag, coupling, lift, passing, composed,
    solved, sources, packed, down, current, maps,
):
    place_downstream(up, traces, from_above, down)
    for layer in range(LAYERS):
        lifts = lifted_layer(layer, traces, down, inner, outer, from_across, coupling, lift)
        for e in range(PATCH):
            at = layer * PATCH + e
            y = halves(dot(stacked(rhs[at] - lifts[e]), diag[at]))
            solved[at] = y
            sources[at] = face_of(blocks_of(y), 1)
    for e in range(PATCH):
        current[e] = sources[e]
    for layer in range(1, LAYERS):
        moved = []
        for e in range(PATCH):
            at = layer * PATCH + e
            moved.append(sources[at] - times(current[up[at]], passing[at]))
        for e in range(PATCH):
            current[e] = moved[e]
    row = lax.broadcasted_iota(jnp.int32, (8, LANES), 0)
    ends = jnp.zeros((8, LANES), F32)
    for e in range(PATCH):
        start = up[up[PATCH + up[2 * PATCH + e]]]
        maps[start, 0:TRACE] = composed[e]
        maps[start, TRACE:MAP_ROWS] = current[e]
        ends = jnp.where(row == start, float(e), ends)
    packed[...] = pack([maps[e] for e in range(PATCH)], ends)


def joined(mine, theirs, bit):
    later = (lax.axis_index("sweep") >> bit & 1) == 1
    first, first_ends = unpack(jnp.where(later, theirs, mine))
    second, second_ends = unpack(jnp.where(later, mine, theirs))
    first_ends, second_ends = rows_of(first_ends), rows_of(second_ends)
    maps = [after(first[at], chosen(second, first_ends[at])) for at in range(PATCH)]
    return maps, [chosen(second_ends, first_ends[at]) for at in range(PATCH)], first, first_ends, later


def pair_kernel(mine, theirs, packed):
    maps, ends, *unused = joined(mine[...], theirs[...], 0)
    packed[...] = pack(maps, ends_of(ends))


def group_kernel(mine, theirs, packed, leaving):
    maps, ends, *unused = joined(mine[...], theirs[...], 1)
    packed[...] = pack(maps, ends_of(ends))
    leaving[...] = pack_states(placed([x[TRACE:] for x in maps], ends))


def prefix_kernel(pair, theirs, prefixes, ends):
    me = lax.axis_index("sweep")
    partner, partner_ends = unpack(pair[...])
    row = lax.broadcasted_iota(jnp.int32, (MAP_ROWS, LANES), 0)
    same = (row == lane_ids(MAP_ROWS)).astype(F32)
    later = (me & 1) == 1
    own = [jnp.where(later, x, same) for x in partner]
    own_ends = [jnp.where(later, x, float(at)) for at, x in enumerate(rows_of(partner_ends))]
    first, first_ends = unpack(theirs[...])
    first_ends = rows_of(first_ends)
    later = (me >> 1 & 1) == 1
    out = []
    for at in range(PATCH):
        whole = after(first[at], chosen(own, first_ends[at]))
        prefixes[at] = jnp.where(later, whole, own[at])
        out.append(jnp.where(later, chosen(own_ends, first_ends[at]), own_ends[at]))
    ends[...] = ends_of(out)


def onward_kernel(entering, packed, leaving):
    maps, ends = unpack(packed[...])
    states = unpack_states(entering[...])
    states = [after(states[at], maps[at]) for at in range(PATCH)]
    leaving[...] = pack_states(placed(states, rows_of(ends)))


def finish_kernel(
    up, second, fourth, third, before, prefixes, ends, old, solved, sources, weights, passing,
    new, traces, inner, outer, across, below, arrived, current, made, sems,
):
    maps, map_ends = unpack(before[...])
    second, fourth, third = [unpack_states(x[...]) for x in (second, fourth, third)]
    states = [after(fourth[at], maps[at]) for at in range(PATCH)]
    last = placed(states, rows_of(map_ends))
    entering = [second[at] + third[at] + last[at] for at in range(PATCH)]
    states = [after(entering[at], prefixes[at]) for at in range(PATCH)]
    for at, state in enumerate(placed(states, rows_of(ends))):
        arrived[at] = state
    changes, copies = [], []
    for layer in range(LAYERS):
        inflow = []
        for e in range(PATCH):
            link = up[layer * PATCH + e]
            inflow.append(arrived[link] if layer == 0 else current[link])
        if layer < LAYERS - 1:
            for e in range(PATCH):
                at = layer * PATCH + e
                current[e] = sources[at] - times(inflow[e], passing[at])
        for e in range(PATCH):
            at = layer * PATCH + e
            x = solved[at] - times(inflow[e], weights[at])
            made[at] = x
            changes.append(old[at] - x)
    copy = pltpu.make_async_copy(made, new, sems.at[0])
    copy.start()
    put_faces(changes, up, traces, inner, outer, across, below)
    copy.wait()


def residual_kernel(up, traces, from_above, outer, inner, from_across, coupling, lift, out, down):
    place_downstream(up, traces, from_above, down)
    for layer in range(LAYERS):
        lifts = lifted_layer(layer, traces, down, inner, outer, from_across, coupling, lift)
        for e in range(PATCH):
            out[layer * PATCH + e] = lifts[e]


VMEM = pl.BlockSpec(memory_space=pltpu.VMEM)
SMEM = pl.BlockSpec(memory_space=pltpu.SMEM)
FAR = pl.BlockSpec(memory_space=pl.ANY)


def call(kernel, scalars, outs, scratch=(), scalar_outs=(), far_outs=(), micros=1):
    def run(*args):
        return pl.pallas_call(
            kernel,
            in_specs=[SMEM] * scalars + [VMEM] * (len(args) - scalars),
            out_specs=[SMEM if i in scalar_outs else FAR if i in far_outs else VMEM for i in range(len(outs))],
            out_shape=[jax.ShapeDtypeStruct(shape, kind) for shape, kind in outs],
            scratch_shapes=list(scratch),
            compiler_params=pltpu.CompilerParams(vmem_limit_bytes=16 * 1024 * 1024),
            cost_estimate=pl.CostEstimate(
                flops=micros * 1_000_000_000, bytes_accessed=micros * 3_600_000, transcendentals=0
            ),
        )(*args)

    return run


FACE_OUTS = [
    ((CELLS, 2 * VECS, len(SLOT_FACES) * LANES), BF16),
    ((LAYERS * EY, VECS, LANES), F32),
    ((LAYERS * EY, VECS, LANES), F32),
    ((LAYERS * EX, VECS, LANES), F32),
    ((LAYERS * EY, VECS, LANES), F32),
]
FIELD = ((CELLS, VECS, ROWS), F32)
STATES = ((3 * VECS, LANES), F32)
PACKED = ((3 * TRACE + 8, LANES), F32)
DOWN = pltpu.VMEM((CELLS, 2 * VECS, LANES), BF16)
HELD = pltpu.VMEM((PATCH, VECS, LANES), F32)


def exchange_sides(inner, outer, across, below):
    wide, deep = lax.axis_size("cx"), lax.axis_size("sweep")
    outer = lax.ppermute(outer, "cx", [(i, i + 1 if i % 2 else i - 1) for i in range(1, wide - 1)])
    below = lax.ppermute(below, "sweep", [(i + 1, i) for i in range(deep - 1)])
    inner = lax.ppermute(inner, "cx", [(i, i ^ 1) for i in range(wide)])
    across = lax.ppermute(across, "cy", [(0, 1), (1, 0)])
    return below, outer, inner, across


def swapped(packed, by):
    return lax.ppermute(packed, "sweep", [(i, i ^ by) for i in range(lax.axis_size("sweep"))])


def passed(states, source, target, shift):
    pairs = [(GROUP * source + p, GROUP * target + (p + shift) % GROUP) for p in range(GROUP)]
    return lax.ppermute(states, "sweep", pairs)


def local(rhs_vectors, old_iterate, diag_inverse, coupling, lift_table, upstream):
    old = old_iterate.reshape(CELLS, VECS, ROWS)
    rhs = rhs_vectors.reshape(CELLS, VECS, ROWS)
    diag = diag_inverse.reshape(CELLS, ROWS, ROWS)
    blocks = coupling.reshape(CELLS, TRACE, 6 * TRACE)
    lift = lift_table.T
    up, traces, *sends = call(open_kernel, 1, [((CELLS,), jnp.int32)] + FACE_OUTS, scalar_outs=(0,), micros=2)(
        upstream.transpose(1, 2, 0), old
    )
    halos = exchange_sides(*sends)
    weights, passing, composed = call(
        transfer_kernel,
        1,
        [((CELLS, DEEP, ROWS), BF16), ((CELLS, DEEP, LANES), BF16), ((PATCH, TRACE, LANES), F32)],
        [pltpu.VMEM((PATCH, TRACE, LANES), F32)],
    )(up, diag, blocks, lift)
    solved, sources, single = call(
        source_kernel,
        1,
        [FIELD, ((CELLS, VECS, LANES), F32), PACKED],
        [DOWN, HELD, pltpu.VMEM((PATCH, MAP_ROWS, LANES), F32)],
    )(up, rhs, traces, *halos, diag, blocks, lift, passing, composed)
    partner = swapped(single, 1)
    (pair,) = call(pair_kernel, 0, [PACKED])(single, partner)
    partner_pair = swapped(pair, 2)
    group, leaving = call(group_kernel, 0, [PACKED, STATES])(pair, partner_pair)
    second = passed(leaving, 0, 1, 2)
    before = passed(group, 2, 3, 2)
    prefixes, ends = call(prefix_kernel, 0, [((PATCH, MAP_ROWS, LANES), F32), ((8, LANES), F32)])(
        partner, partner_pair
    )
    (leaving,) = call(onward_kernel, 0, [STATES])(second, group)
    third = passed(leaving, 1, 2, 2)
    fourth = passed(leaving, 1, 3, 0)
    new, traces, *sends = call(
        finish_kernel,
        1,
        [FIELD] + FACE_OUTS,
        [HELD, HELD, pltpu.VMEM((CELLS, VECS, ROWS), F32), pltpu.SemaphoreType.DMA((1,))],
        far_outs=(0,),
    )(
        up, second, fourth, third, before, prefixes, ends, old, solved, sources, weights, passing
    )
    halos = exchange_sides(*sends)
    (residual,) = call(residual_kernel, 1, [FIELD], [DOWN])(up, traces, *halos, blocks, lift)
    shape = rhs_vectors.shape
    return new.reshape(shape), residual.reshape(shape)


def solution(mesh):
    field = P("sweep", "cx", "cy", None, None)
    return jax.shard_map(
        local,
        mesh=mesh,
        in_specs=(field, field, field, field, P(), P("sweep", "cx", "cy")),
        out_specs=(field, field),
        check_vma=False,
    )
```

```python
import jax
import jax.numpy as jnp
from jax import lax
from jax.experimental import pallas as pl
from jax.experimental.pallas import tpu as pltpu
from jax.sharding import PartitionSpec as P

NPOINT = 4
ROWS = 320
TRACE = 80
VECS = 16
LAYERS = 3
EX = 2
EY = 2
PATCH = EX * EY
CELLS = LAYERS * PATCH
LANES = 128
DEEP = 2 * LANES
GROUP = 4
NODES = NPOINT**3
MAP_ROWS = TRACE + VECS
BF16 = jnp.bfloat16
F32 = jnp.float32

FACE_ROWS = ((0, 16, 4), (3, 16, 4), (0, 4, 1), (48, 4, 1), (0, 16, 1), (12, 16, 1))
SLOT_FACES = (0, 3, 2, 5, 4)


def split(x):
    high = x.astype(BF16)
    low = (x - high.astype(F32)).astype(BF16)
    return high, low


def stacked(x):
    return jnp.concatenate(split(x), axis=0)


def dot(a, b):
    return jnp.dot(a, b, preferred_element_type=F32)


def dot_rows(a, b):
    return lax.dot_general(a, b, (((1,), (1,)), ((), ())), preferred_element_type=F32)


def halves(x):
    rows = x.shape[0] // 2
    return x[:rows] + x[rows:]


def deep_rows(table):
    high, low = split(table)
    gap = jnp.zeros((LANES - TRACE, table.shape[1]), BF16)
    return jnp.concatenate([high, gap, low, gap], axis=0)


def deep_lhs(x):
    high, low = split(x)
    return jnp.concatenate(
        [jnp.concatenate([high, high], axis=1), jnp.concatenate([low, low], axis=1)], axis=0
    )


def times(x, deep):
    return halves(dot(deep_lhs(x), deep))


def lane_take(x, index):
    return jnp.take_along_axis(x, index, axis=1)


def lane_ids(rows):
    return lax.broadcasted_iota(jnp.int32, (rows, LANES), 1)


def blocks_of(x):
    rest = ROWS - 2 * LANES
    tail = jnp.concatenate([x[:, 2 * LANES :], jnp.zeros((x.shape[0], LANES - rest), x.dtype)], axis=1)
    return x[:, :LANES], x[:, LANES : 2 * LANES], tail


def face_of(blocks, face):
    start, a_step, b_step = FACE_ROWS[face]
    lane = lane_ids(blocks[0].shape[0])
    entry = lane & 15
    index = (lane >> 4 & 1) * NODES + start + (entry >> 2) * a_step + (entry & 3) * b_step
    first, second, third = [lane_take(block, index) for block in blocks]
    third = jnp.where(lane < TRACE, third, 0.0)
    return jnp.where(lane < 32, first, jnp.where(lane < 64, second, third))


def side_table():
    row = lax.broadcasted_iota(jnp.int32, (ROWS, LANES), 0)
    lane = lane_ids(1)
    blocks = []
    for face in SLOT_FACES:
        start, a_step, b_step = FACE_ROWS[face]
        source = (lane >> 4) * NODES + start + (lane >> 2 & 3) * a_step + (lane & 3) * b_step
        source = jnp.where(lane < TRACE, source, -1)
        blocks.append(jnp.where(row == source, 1.0, 0.0).astype(BF16))
    return jnp.concatenate(blocks, axis=1)


def rows_of(ends):
    return [ends[at : at + 1] for at in range(PATCH)]


def ends_of(rows):
    return jnp.concatenate(list(rows) + [jnp.zeros((8 - PATCH, LANES), F32)], axis=0)


def chosen(items, at):
    out = items[0]
    for number in range(1, PATCH):
        out = jnp.where(at == number, items[number], out)
    return out


def placed(states, ends):
    out = []
    for position in range(PATCH):
        total = jnp.where(ends[0] == position, states[0], 0.0)
        for at in range(1, PATCH):
            total = total + jnp.where(ends[at] == position, states[at], 0.0)
        out.append(total)
    return out


def ups_of(ups):
    return [[ups[layer * PATCH + e : layer * PATCH + e + 1] for e in range(PATCH)] for layer in range(LAYERS)]


def position_kernel(links, ups):
    found = []
    lane = lax.broadcasted_iota(jnp.int32, (EY, LAYERS), 1)
    for layer in range(LAYERS):
        for a in range(EX):
            value = jnp.sum(jnp.where(lane == layer, links[a], 0).astype(F32), axis=1, keepdims=True)
            found.append(jnp.broadcast_to(value, (EY, LANES)))
    ups[...] = jnp.concatenate(found + [jnp.zeros((16 - CELLS, LANES), F32)], axis=0)


def put_faces(cells, ups, traces, inner, outer, across, below):
    core = lax.axis_index("cy")
    even = lax.rem(lax.axis_index("cx"), 2) == 0
    picked = dot(jnp.concatenate([stacked(x) for x in cells], axis=0), side_table())
    pieces = [picked[2 * VECS * at : 2 * VECS * (at + 1)] for at in range(CELLS)]
    whole = [halves(piece) for piece in pieces]
    for layer in range(LAYERS):
        block = lambda e, s: whole[layer * PATCH + e][:, s * LANES : (s + 1) * LANES]
        for e in range(PATCH):
            traces[layer * PATCH + e, :, LANES:] = pieces[layer * PATCH + e][:, LANES:].astype(BF16)
        for b in range(EY):
            east, west = block(EY + b, 1), block(b, 2)
            inner[layer * EY + b] = jnp.where(even, east, west)
            outer[layer * EY + b] = jnp.where(even, west, east)
        for a in range(EX):
            across[layer * EX + a] = jnp.where(core == 0, block(a * EY + 1, 3), block(a * EY, 4))
        if layer == 0:
            for e, state in enumerate(placed([block(e, 0) for e in range(PATCH)], ups[layer])):
                below[e] = state
        else:
            inflows = [pieces[layer * PATCH + e][:, :LANES] for e in range(PATCH)]
            for e, piece in enumerate(placed(inflows, ups[layer])):
                traces[(layer - 1) * PATCH + e, :, :LANES] = piece.astype(BF16)
    for e in range(PATCH, LAYERS * EY):
        below[e] = jnp.zeros((VECS, LANES), F32)


def open_kernel(ups, old, traces, inner, outer, across, below):
    put_faces([old[at] for at in range(CELLS)], ups_of(ups), traces, inner, outer, across, below)


def near_slots(layer, e, traces):
    a, b = e // EY, e % EY
    own = lambda cell, s: traces[layer * PATCH + cell, :, s * LANES : (s + 1) * LANES]
    slots = {}
    if layer < LAYERS - 1:
        slots[1] = own(e, 0)
    slots[2 if a == 1 else 3] = own(b, 1) if a == 1 else own(EY + b, 2)
    slots[4 if b == 1 else 5] = own(a * EY, 3) if b == 1 else own(a * EY + 1, 4)
    return slots


def far_slots(layer, e, from_above, outer, inner, from_across):
    core = lax.axis_index("cy")
    even = lax.rem(lax.axis_index("cx"), 2) == 0
    a, b = e // EY, e % EY
    close, wide = inner[layer * EY + b], outer[layer * EY + b]
    other = from_across[layer * EX + a]
    slots = {}
    if layer == LAYERS - 1:
        slots[1] = stacked(from_above[e])
    slots[2 if a == 0 else 3] = stacked(jnp.where(even, wide, close) if a == 0 else jnp.where(even, close, wide))
    slots[4 if b == 0 else 5] = stacked(jnp.where(core == (1 if b == 0 else 0), other, 0.0))
    return slots


def lifted_layer(layer, stacks, coupling, lift):
    lane = lax.broadcasted_iota(jnp.int32, (2 * VECS, DEEP), 1)
    halfs = ((0, (1, 2, 3)), (DEEP, (3, 4, 5)))
    sides = [[], []]
    r = 2 * VECS
    for e, slots in enumerate(stacks):
        block = coupling[layer * PATCH + e]
        for side, (begin, numbers) in zip(sides, halfs):
            present = [slot for slot in numbers if slot in slots]
            y = dot(
                jnp.concatenate([slots[slot] for slot in present], axis=0)[:, :TRACE],
                block[:, begin : begin + DEEP],
            )
            at = lane[:, : y.shape[1]] + begin
            kept = jnp.zeros((r, y.shape[1]), F32)
            for i, slot in enumerate(present):
                inside = (at >= slot * TRACE) & (at < (slot + 1) * TRACE)
                kept = jnp.where(inside, y[r * i : r * (i + 1)], kept)
            side.append(stacked(halves(kept)))
    out = dot_rows(jnp.concatenate(sides[0], axis=0), lift[:, :DEEP]) + dot_rows(
        jnp.concatenate(sides[1], axis=0), lift[:, DEEP:]
    )
    return [halves(out[r * e : r * (e + 1)]) for e in range(PATCH)]


def transfer_kernel(ups, diag, coupling, lift, weights, passing, composed):
    ups = ups_of(ups)
    one = lax.broadcasted_iota(jnp.int32, (TRACE, TRACE), 0)
    two = lax.broadcasted_iota(jnp.int32, (TRACE, TRACE), 1)
    inflow = dot_rows((one == two).astype(F32).astype(BF16), lift[:, :TRACE]).astype(BF16)
    upper, lower = inflow[:NODES, :DEEP], inflow[NODES:, DEEP:]
    first = []
    for at in range(CELLS):
        block = diag[at]
        lifted_rows = jnp.concatenate([dot(upper, block[:DEEP]), dot(lower, block[DEEP:])], axis=0)
        upwind = coupling[at][:, :LANES]
        weight = dot(jnp.concatenate([upwind, upwind], axis=1), deep_rows(lifted_rows))
        weights[at] = deep_rows(weight)
        passed_on = face_of(blocks_of(weight), 1)
        passing[at] = deep_rows(passed_on)
        if at < PATCH:
            first.append(passed_on)
    both = [times(chosen(first, ups[1][e]), passing[PATCH + e]) for e in range(PATCH)]
    for e in range(PATCH):
        composed[e] = -times(chosen(both, ups[2][e]), passing[2 * PATCH + e])


def turned(x, by):
    return pltpu.roll(x, by % LANES, 1)


def pack(maps, ends):
    lane = lane_ids(TRACE)
    square = [x[:TRACE] for x in maps]
    source = [x[TRACE:] for x in maps]
    all_sources = jnp.concatenate(source, axis=0)
    part = lane_ids(VECS) >> 4
    last = jnp.where(part == 5, turned(source[0], 16), jnp.where(part == 6, turned(source[1], 32), turned(source[2], 48)))
    one = jnp.where(lane < TRACE, square[0], turned(square[3], TRACE))
    rest = jnp.concatenate([turned(all_sources, 64), turned(source[3], 48)], axis=0)
    two = jnp.where(lane < TRACE, square[1], jnp.where(lane < 112, turned(square[3], 32), rest))
    three = jnp.where(lane < TRACE, square[2], jnp.concatenate([turned(all_sources, TRACE), last], axis=0))
    return jnp.concatenate([one, two, three, ends], axis=0)


def unpack(packed):
    lane = lane_ids(TRACE)
    one, two, three = [packed[TRACE * at : TRACE * (at + 1)] for at in range(3)]
    four = jnp.where(lane < 48, turned(one, 48), turned(two, 96))
    square = [jnp.where(lane < TRACE, x, 0.0) for x in (one, two, three, four)]
    lane = lane_ids(PATCH * VECS)
    most = jnp.where(lane < 48, turned(three[: PATCH * VECS], 48), turned(two[: PATCH * VECS], 64))
    ends = [turned(three[PATCH * VECS :], by) for by in (112, 96, 80)] + [turned(two[PATCH * VECS :], 80)]
    lane = lane_ids(VECS)
    maps = []
    for at in range(PATCH):
        source = jnp.where(lane < 64, most[VECS * at : VECS * (at + 1)], jnp.where(lane < TRACE, ends[at], 0.0))
        maps.append(jnp.concatenate([square[at], source], axis=0))
    return maps, packed[3 * TRACE : 3 * TRACE + 8]


def pack_states(states):
    lane = lane_ids(VECS)
    one = jnp.where(lane < TRACE, states[0], turned(states[3], TRACE))
    two = jnp.where(lane < TRACE, states[1], turned(states[3], 32))
    return jnp.concatenate([one, two, states[2]], axis=0)


def unpack_states(packed):
    lane = lane_ids(VECS)
    one, two, three = [packed[VECS * at : VECS * (at + 1)] for at in range(3)]
    four = jnp.where(lane < 48, turned(one, 48), turned(two, 96))
    return [jnp.where(lane < TRACE, x, 0.0) for x in (one, two, three, four)]


def after(first, second):
    nothing = jnp.zeros((TRACE, LANES), F32)
    added = jnp.concatenate([nothing, second[TRACE:]], axis=0) if first.shape[0] > VECS else second[TRACE:]
    return times(first, deep_rows(second[:TRACE])) + added


def source_kernel(
    ups, rhs, traces, from_above, outer, inner, from_across, diag, coupling, lift, passing, composed,
    solved, sources, packed,
):
    ups = ups_of(ups)
    outflows = []
    for layer in range(LAYERS):
        stacks = [
            near_slots(layer, e, traces) | far_slots(layer, e, from_above, outer, inner, from_across)
            for e in range(PATCH)
        ]
        lifts = lifted_layer(layer, stacks, coupling, lift)
        for e in range(PATCH):
            at = layer * PATCH + e
            y = halves(dot(stacked(rhs[at] - lifts[e]), diag[at]))
            solved[at] = y
            outflows.append(face_of(blocks_of(y), 1))
            sources[at] = outflows[at]
    current = outflows[:PATCH]
    for layer in range(1, LAYERS):
        current = [
            outflows[layer * PATCH + e] - times(chosen(current, ups[layer][e]), passing[layer * PATCH + e])
            for e in range(PATCH)
        ]
    starts = [chosen(ups[0], chosen(ups[1], ups[2][e])) for e in range(PATCH)]
    maps = placed([jnp.concatenate([composed[e], current[e]], axis=0) for e in range(PATCH)], starts)
    ends = placed([jnp.full((1, LANES), float(e), F32) for e in range(PATCH)], starts)
    packed[...] = pack(maps, ends_of(ends))


def joined(mine, theirs, bit):
    later = (lax.axis_index("sweep") >> bit & 1) == 1
    first, first_ends = unpack(jnp.where(later, theirs, mine))
    second, second_ends = unpack(jnp.where(later, mine, theirs))
    first_ends, second_ends = rows_of(first_ends), rows_of(second_ends)
    maps = [after(first[at], chosen(second, first_ends[at])) for at in range(PATCH)]
    return maps, [chosen(second_ends, first_ends[at]) for at in range(PATCH)], first, first_ends, later


def pair_kernel(mine, theirs, packed):
    maps, ends, *unused = joined(mine[...], theirs[...], 0)
    packed[...] = pack(maps, ends_of(ends))


def group_kernel(mine, theirs, packed, leaving):
    maps, ends, *unused = joined(mine[...], theirs[...], 1)
    packed[...] = pack(maps, ends_of(ends))
    leaving[...] = pack_states(placed([x[TRACE:] for x in maps], ends))


def prefix_kernel(pair, theirs, prefixes, ends):
    me = lax.axis_index("sweep")
    partner, partner_ends = unpack(pair[...])
    row = lax.broadcasted_iota(jnp.int32, (MAP_ROWS, LANES), 0)
    same = (row == lane_ids(MAP_ROWS)).astype(F32)
    later = (me & 1) == 1
    own = [jnp.where(later, x, same) for x in partner]
    own_ends = [jnp.where(later, x, float(at)) for at, x in enumerate(rows_of(partner_ends))]
    first, first_ends = unpack(theirs[...])
    first_ends = rows_of(first_ends)
    later = (me >> 1 & 1) == 1
    out = []
    for at in range(PATCH):
        whole = after(first[at], chosen(own, first_ends[at]))
        prefixes[at] = jnp.where(later, whole, own[at])
        out.append(jnp.where(later, chosen(own_ends, first_ends[at]), own_ends[at]))
    ends[...] = ends_of(out)


def onward_kernel(entering, packed, leaving):
    maps, ends = unpack(packed[...])
    states = unpack_states(entering[...])
    states = [after(states[at], maps[at]) for at in range(PATCH)]
    leaving[...] = pack_states(placed(states, rows_of(ends)))


def finish_kernel(
    ups, second, fourth, third, before, prefixes, ends, old, solved, sources, weights, passing,
    new, traces, inner, outer, across, below, made, sems,
):
    maps, map_ends = unpack(before[...])
    second, fourth, third = [unpack_states(x[...]) for x in (second, fourth, third)]
    states = [after(fourth[at], maps[at]) for at in range(PATCH)]
    last = placed(states, rows_of(map_ends))
    entering = [second[at] + third[at] + last[at] for at in range(PATCH)]
    states = [after(entering[at], prefixes[at]) for at in range(PATCH)]
    current = placed(states, rows_of(ends))
    ups = ups_of(ups)
    changes = []
    for layer in range(LAYERS):
        inflow = [chosen(current, ups[layer][e]) for e in range(PATCH)]
        current = [
            sources[layer * PATCH + e] - times(inflow[e], passing[layer * PATCH + e]) for e in range(PATCH)
        ]
        for e in range(PATCH):
            at = layer * PATCH + e
            x = solved[at] - times(inflow[e], weights[at])
            made[at] = x
            changes.append(old[at] - x)
    copy = pltpu.make_async_copy(made, new, sems.at[0])
    copy.start()
    put_faces(changes, ups, traces, inner, outer, across, below)
    copy.wait()


def near_residual_kernel(traces, coupling, lift, out):
    for layer in range(LAYERS):
        stacks = [near_slots(layer, e, traces) for e in range(PATCH)]
        for e, x in enumerate(lifted_layer(layer, stacks, coupling, lift)):
            out[layer * PATCH + e] = x


def residual_kernel(near, from_above, outer, inner, from_across, coupling, lift, out):
    for layer in range(LAYERS):
        stacks = [far_slots(layer, e, from_above, outer, inner, from_across) for e in range(PATCH)]
        for e, x in enumerate(lifted_layer(layer, stacks, coupling, lift)):
            out[layer * PATCH + e] = near[layer * PATCH + e] + x


VMEM = pl.BlockSpec(memory_space=pltpu.VMEM)
FAR = pl.BlockSpec(memory_space=pl.ANY)


def call(kernel, outs, scratch=(), far_outs=(), micros=1):
    def run(*args):
        return pl.pallas_call(
            kernel,
            in_specs=[VMEM] * len(args),
            out_specs=[FAR if i in far_outs else VMEM for i in range(len(outs))],
            out_shape=[jax.ShapeDtypeStruct(shape, kind) for shape, kind in outs],
            scratch_shapes=list(scratch),
            compiler_params=pltpu.CompilerParams(vmem_limit_bytes=16 * 1024 * 1024),
            cost_estimate=pl.CostEstimate(
                flops=micros * 1_000_000_000, bytes_accessed=micros * 3_600_000, transcendentals=0
            ),
        )(*args)

    return run


FACE_OUTS = [
    ((CELLS, 2 * VECS, len(SLOT_FACES) * LANES), BF16),
    ((LAYERS * EY, VECS, LANES), F32),
    ((LAYERS * EY, VECS, LANES), F32),
    ((LAYERS * EX, VECS, LANES), F32),
    ((LAYERS * EY, VECS, LANES), F32),
]
FIELD = ((CELLS, VECS, ROWS), F32)
STATES = ((3 * VECS, LANES), F32)
PACKED = ((3 * TRACE + 8, LANES), F32)


def exchange_sides(inner, outer, across, below):
    wide, deep = lax.axis_size("cx"), lax.axis_size("sweep")
    outer = lax.ppermute(outer, "cx", [(i, i + 1 if i % 2 else i - 1) for i in range(1, wide - 1)])
    below = lax.ppermute(below, "sweep", [(i + 1, i) for i in range(deep - 1)])
    inner = lax.ppermute(inner, "cx", [(i, i ^ 1) for i in range(wide)])
    across = lax.ppermute(across, "cy", [(0, 1), (1, 0)])
    return below, outer, inner, across


def swapped(packed, by):
    return lax.ppermute(packed, "sweep", [(i, i ^ by) for i in range(lax.axis_size("sweep"))])


def passed(states, source, target, shift):
    pairs = [(GROUP * source + p, GROUP * target + (p + shift) % GROUP) for p in range(GROUP)]
    return lax.ppermute(states, "sweep", pairs)


def local(rhs_vectors, old_iterate, diag_inverse, coupling, lift_table, upstream):
    old = old_iterate.reshape(CELLS, VECS, ROWS)
    rhs = rhs_vectors.reshape(CELLS, VECS, ROWS)
    diag = diag_inverse.reshape(CELLS, ROWS, ROWS)
    blocks = coupling.reshape(CELLS, TRACE, 6 * TRACE)
    lift = lift_table.T
    (ups,) = call(position_kernel, [((16, LANES), F32)], micros=2)(upstream.transpose(1, 2, 0))
    traces, *sends = call(open_kernel, FACE_OUTS, micros=2)(ups, old)
    halos = exchange_sides(*sends)
    weights, passing, composed = call(
        transfer_kernel,
        [((CELLS, DEEP, ROWS), BF16), ((CELLS, DEEP, LANES), BF16), ((PATCH, TRACE, LANES), F32)],
    )(ups, diag, blocks, lift)
    solved, sources, single = call(source_kernel, [FIELD, ((CELLS, VECS, LANES), F32), PACKED])(
        ups, rhs, traces, *halos, diag, blocks, lift, passing, composed
    )
    partner = swapped(single, 1)
    (pair,) = call(pair_kernel, [PACKED])(single, partner)
    partner_pair = swapped(pair, 2)
    group, leaving = call(group_kernel, [PACKED, STATES])(pair, partner_pair)
    second = passed(leaving, 0, 1, 2)
    before = passed(group, 2, 3, 2)
    prefixes, ends = call(prefix_kernel, [((PATCH, MAP_ROWS, LANES), F32), ((8, LANES), F32)])(
        partner, partner_pair
    )
    (leaving,) = call(onward_kernel, [STATES])(second, group)
    third = passed(leaving, 1, 2, 2)
    fourth = passed(leaving, 1, 3, 0)
    new, traces, *sends = call(
        finish_kernel,
        [FIELD] + FACE_OUTS,
        [pltpu.VMEM((CELLS, VECS, ROWS), F32), pltpu.SemaphoreType.DMA((1,))],
        far_outs=(0,),
    )(ups, second, fourth, third, before, prefixes, ends, old, solved, sources, weights, passing)
    halos = exchange_sides(*sends)
    (near,) = call(near_residual_kernel, [FIELD])(traces, blocks, lift)
    (residual,) = call(residual_kernel, [FIELD])(near, *halos, blocks, lift)
    shape = rhs_vectors.shape
    return new.reshape(shape), residual.reshape(shape)


def solution(mesh):
    field = P("sweep", "cx", "cy", None, None)
    return jax.shard_map(
        local,
        mesh=mesh,
        in_specs=(field, field, field, field, P(), P("sweep", "cx", "cy")),
        out_specs=(field, field),
        check_vma=False,
    )
```

```python
import jax
import jax.numpy as jnp
from jax import lax
from jax.experimental import pallas as pl
from jax.experimental.pallas import tpu as pltpu
from jax.sharding import PartitionSpec as P

NPOINT = 4
ROWS = 320
TRACE = 80
VECS = 16
LAYERS = 3
EX = 2
EY = 2
PATCH = EX * EY
CELLS = LAYERS * PATCH
LANES = 128
DEEP = 2 * LANES
GROUP = 4
NODES = NPOINT**3
MAP_ROWS = TRACE + VECS
BF16 = jnp.bfloat16
F32 = jnp.float32

FACE_ROWS = ((0, 16, 4), (3, 16, 4), (0, 4, 1), (48, 4, 1), (0, 16, 1), (12, 16, 1))
SLOT_FACES = (0, 3, 2, 5, 4)


def split(x):
    high = x.astype(BF16)
    low = (x - high.astype(F32)).astype(BF16)
    return high, low


def stacked(x):
    return jnp.concatenate(split(x), axis=0)


def dot(a, b):
    return jnp.dot(a, b, preferred_element_type=F32)


def dot_rows(a, b):
    return lax.dot_general(a, b, (((1,), (1,)), ((), ())), preferred_element_type=F32)


def halves(x):
    rows = x.shape[0] // 2
    return x[:rows] + x[rows:]


def deep_rows(table):
    high, low = split(table)
    gap = jnp.zeros((LANES - TRACE, table.shape[1]), BF16)
    return jnp.concatenate([high, gap, low, gap], axis=0)


def deep_lhs(x):
    high, low = split(x)
    return jnp.concatenate(
        [jnp.concatenate([high, high], axis=1), jnp.concatenate([low, low], axis=1)], axis=0
    )


def times(x, deep):
    return halves(dot(deep_lhs(x), deep))


def lane_take(x, index):
    return jnp.take_along_axis(x, index, axis=1)


def lane_ids(rows):
    return lax.broadcasted_iota(jnp.int32, (rows, LANES), 1)


def blocks_of(x):
    rest = ROWS - 2 * LANES
    tail = jnp.concatenate([x[:, 2 * LANES :], jnp.zeros((x.shape[0], LANES - rest), x.dtype)], axis=1)
    return x[:, :LANES], x[:, LANES : 2 * LANES], tail


def face_of(blocks, face):
    start, a_step, b_step = FACE_ROWS[face]
    lane = lane_ids(blocks[0].shape[0])
    entry = lane & 15
    index = (lane >> 4 & 1) * NODES + start + (entry >> 2) * a_step + (entry & 3) * b_step
    first, second, third = [lane_take(block, index) for block in blocks]
    third = jnp.where(lane < TRACE, third, 0.0)
    return jnp.where(lane < 32, first, jnp.where(lane < 64, second, third))


def side_table():
    row = lax.broadcasted_iota(jnp.int32, (ROWS, LANES), 0)
    lane = lane_ids(1)
    blocks = []
    for face in SLOT_FACES:
        start, a_step, b_step = FACE_ROWS[face]
        source = (lane >> 4) * NODES + start + (lane >> 2 & 3) * a_step + (lane & 3) * b_step
        source = jnp.where(lane < TRACE, source, -1)
        blocks.append(jnp.where(row == source, 1.0, 0.0).astype(BF16))
    return jnp.concatenate(blocks, axis=1)


def rows_of(ends):
    return [ends[at : at + 1] for at in range(PATCH)]


def ends_of(rows):
    return jnp.concatenate(list(rows) + [jnp.zeros((8 - PATCH, LANES), F32)], axis=0)


def chosen(items, at):
    out = items[0]
    for number in range(1, PATCH):
        out = jnp.where(at == number, items[number], out)
    return out


def placed(states, ends):
    out = []
    for position in range(PATCH):
        total = jnp.where(ends[0] == position, states[0], 0.0)
        for at in range(1, PATCH):
            total = total + jnp.where(ends[at] == position, states[at], 0.0)
        out.append(total)
    return out


def ups_of(ups):
    return [[ups[layer * PATCH + e : layer * PATCH + e + 1] for e in range(PATCH)] for layer in range(LAYERS)]


def position_rows(links):
    found = []
    lane = lax.broadcasted_iota(jnp.int32, (EY, LAYERS), 1)
    for layer in range(LAYERS):
        for a in range(EX):
            value = jnp.sum(jnp.where(lane == layer, links[a], 0).astype(F32), axis=1, keepdims=True)
            found.append(jnp.broadcast_to(value, (EY, LANES)))
    return jnp.concatenate(found + [jnp.zeros((16 - CELLS, LANES), F32)], axis=0)


def put_sides(cells, traces, inner, outer, across):
    core = lax.axis_index("cy")
    even = lax.rem(lax.axis_index("cx"), 2) == 0
    picked = dot(jnp.concatenate([stacked(x) for x in cells], axis=0), side_table())
    pieces = [picked[2 * VECS * at : 2 * VECS * (at + 1)] for at in range(CELLS)]
    whole = [halves(piece[:, LANES:]) for piece in pieces]
    for layer in range(LAYERS):
        block = lambda e, s: whole[layer * PATCH + e][:, (s - 1) * LANES : s * LANES]
        for e in range(PATCH):
            traces[layer * PATCH + e] = pieces[layer * PATCH + e][:, LANES:].astype(BF16)
        for b in range(EY):
            east, west = block(EY + b, 1), block(b, 2)
            inner[layer * EY + b] = jnp.where(even, east, west)
            outer[layer * EY + b] = jnp.where(even, west, east)
        for a in range(EX):
            across[layer * EX + a] = jnp.where(core == 0, block(a * EY + 1, 3), block(a * EY, 4))
    return [piece[:, :LANES] for piece in pieces]


def put_inflows(pieces, ups, down, below):
    for e, state in enumerate(placed([halves(pieces[e]) for e in range(PATCH)], ups[0])):
        below[e] = state
    for e in range(PATCH, LAYERS * EY):
        below[e] = jnp.zeros((VECS, LANES), F32)
    for layer in range(1, LAYERS):
        for e, piece in enumerate(placed(pieces[layer * PATCH : (layer + 1) * PATCH], ups[layer])):
            down[(layer - 1) * PATCH + e] = piece.astype(BF16)


def open_kernel(old, traces, inner, outer, across, faces):
    for at, piece in enumerate(put_sides([old[at] for at in range(CELLS)], traces, inner, outer, across)):
        faces[at] = piece


def position_kernel(links, faces, ups, down, below):
    rows = position_rows(links)
    ups[...] = rows
    put_inflows([faces[at] for at in range(CELLS)], ups_of(rows), down, below)


def near_slots(layer, e, traces, down):
    a, b = e // EY, e % EY
    own = lambda cell, s: traces[layer * PATCH + cell, :, (s - 1) * LANES : s * LANES]
    slots = {}
    if layer < LAYERS - 1:
        slots[1] = down[layer * PATCH + e]
    slots[2 if a == 1 else 3] = own(b, 1) if a == 1 else own(EY + b, 2)
    slots[4 if b == 1 else 5] = own(a * EY, 3) if b == 1 else own(a * EY + 1, 4)
    return slots


def far_slots(layer, e, from_above, outer, inner, from_across):
    core = lax.axis_index("cy")
    even = lax.rem(lax.axis_index("cx"), 2) == 0
    a, b = e // EY, e % EY
    close, wide = inner[layer * EY + b], outer[layer * EY + b]
    other = from_across[layer * EX + a]
    slots = {}
    if layer == LAYERS - 1:
        slots[1] = stacked(from_above[e])
    slots[2 if a == 0 else 3] = stacked(jnp.where(even, wide, close) if a == 0 else jnp.where(even, close, wide))
    slots[4 if b == 0 else 5] = stacked(jnp.where(core == (1 if b == 0 else 0), other, 0.0))
    return slots


def lift_all(stacks, coupling, lift, left, right):
    lane = lax.broadcasted_iota(jnp.int32, (2 * VECS, DEEP), 1)
    r = 2 * VECS
    for at, slots in enumerate(stacks):
        for begin, numbers, kept_rows in ((0, (1, 2, 3), left), (DEEP, (3, 4, 5), right)):
            present = [slot for slot in numbers if slot in slots]
            y = dot(
                jnp.concatenate([slots[slot] for slot in present], axis=0)[:, :TRACE],
                coupling[at, :, begin : min(begin + DEEP, 6 * TRACE)],
            )
            place = lane[:, : y.shape[1]] + begin
            kept = jnp.zeros((r, y.shape[1]), F32)
            for i, slot in enumerate(present):
                inside = (place >= slot * TRACE) & (place < (slot + 1) * TRACE)
                kept = jnp.where(inside, y[r * i : r * (i + 1)], kept)
            kept_rows[r * at : r * (at + 1)] = stacked(halves(kept))
    out = dot_rows(left[...], lift[:, :DEEP]) + dot_rows(right[...], lift[:, DEEP:])
    return [halves(out[r * at : r * (at + 1)]) for at in range(CELLS)]


def transfer_kernel(ups, diag, coupling, lift, lifted_rows, passing, composed, outflows, first):
    ups = ups_of(ups)
    one = lax.broadcasted_iota(jnp.int32, (TRACE, TRACE), 0)
    two = lax.broadcasted_iota(jnp.int32, (TRACE, TRACE), 1)
    inflow = dot_rows((one == two).astype(F32).astype(BF16), lift[:, :TRACE]).astype(BF16)
    upper, lower = inflow[:NODES, :DEEP], inflow[NODES:, DEEP:]
    for at in range(CELLS):
        lifts = jnp.concatenate([dot(upper, diag[at, :DEEP]), dot(lower, diag[at, DEEP:])], axis=0)
        lifted_rows[at] = deep_rows(lifts)
        outflows[at] = deep_rows(face_of(blocks_of(lifts), 1))
    for at in range(CELLS):
        upwind = coupling[at, :, :LANES]
        passed_on = dot(jnp.concatenate([upwind, upwind], axis=1), outflows[at])
        passing[at] = deep_rows(passed_on)
        if at < PATCH:
            first[at] = passed_on
    source = [first[e] for e in range(PATCH)]
    both = [times(chosen(source, ups[1][e]), passing[PATCH + e]) for e in range(PATCH)]
    for e in range(PATCH):
        composed[e] = -times(chosen(both, ups[2][e]), passing[2 * PATCH + e])


def weight_kernel(coupling, lifted_rows, unused, weights):
    for at in range(CELLS):
        upwind = coupling[at][:, :LANES]
        weights[at] = deep_rows(dot(jnp.concatenate([upwind, upwind], axis=1), lifted_rows[at]))


def turned(x, by):
    return pltpu.roll(x, by % LANES, 1)


def pack(maps, ends):
    lane = lane_ids(TRACE)
    square = [x[:TRACE] for x in maps]
    source = [x[TRACE:] for x in maps]
    all_sources = jnp.concatenate(source, axis=0)
    part = lane_ids(VECS) >> 4
    last = jnp.where(part == 5, turned(source[0], 16), jnp.where(part == 6, turned(source[1], 32), turned(source[2], 48)))
    one = jnp.where(lane < TRACE, square[0], turned(square[3], TRACE))
    rest = jnp.concatenate([turned(all_sources, 64), turned(source[3], 48)], axis=0)
    two = jnp.where(lane < TRACE, square[1], jnp.where(lane < 112, turned(square[3], 32), rest))
    three = jnp.where(lane < TRACE, square[2], jnp.concatenate([turned(all_sources, TRACE), last], axis=0))
    return jnp.concatenate([one, two, three, ends], axis=0)


def unpack(packed):
    lane = lane_ids(TRACE)
    one, two, three = [packed[TRACE * at : TRACE * (at + 1)] for at in range(3)]
    four = jnp.where(lane < 48, turned(one, 48), turned(two, 96))
    square = [jnp.where(lane < TRACE, x, 0.0) for x in (one, two, three, four)]
    lane = lane_ids(PATCH * VECS)
    most = jnp.where(lane < 48, turned(three[: PATCH * VECS], 48), turned(two[: PATCH * VECS], 64))
    ends = [turned(three[PATCH * VECS :], by) for by in (112, 96, 80)] + [turned(two[PATCH * VECS :], 80)]
    lane = lane_ids(VECS)
    maps = []
    for at in range(PATCH):
        source = jnp.where(lane < 64, most[VECS * at : VECS * (at + 1)], jnp.where(lane < TRACE, ends[at], 0.0))
        maps.append(jnp.concatenate([square[at], source], axis=0))
    return maps, packed[3 * TRACE : 3 * TRACE + 8]


def pack_states(states):
    lane = lane_ids(VECS)
    one = jnp.where(lane < TRACE, states[0], turned(states[3], TRACE))
    two = jnp.where(lane < TRACE, states[1], turned(states[3], 32))
    return jnp.concatenate([one, two, states[2]], axis=0)


def unpack_states(packed):
    lane = lane_ids(VECS)
    one, two, three = [packed[VECS * at : VECS * (at + 1)] for at in range(3)]
    four = jnp.where(lane < 48, turned(one, 48), turned(two, 96))
    return [jnp.where(lane < TRACE, x, 0.0) for x in (one, two, three, four)]


def after(first, second):
    nothing = jnp.zeros((TRACE, LANES), F32)
    added = jnp.concatenate([nothing, second[TRACE:]], axis=0) if first.shape[0] > VECS else second[TRACE:]
    return times(first, deep_rows(second[:TRACE])) + added


def source_kernel(
    ups, rhs, traces, down, from_above, outer, inner, from_across, diag, coupling, lift, passing, composed,
    solved, sources, packed, left, right,
):
    ups = ups_of(ups)
    stacks = [
        near_slots(layer, e, traces, down) | far_slots(layer, e, from_above, outer, inner, from_across)
        for layer in range(LAYERS)
        for e in range(PATCH)
    ]
    outflows = []
    for at, x in enumerate(lift_all(stacks, coupling, lift, left, right)):
        y = halves(dot(stacked(rhs[at] - x), diag[at]))
        solved[at] = y
        outflows.append(face_of(blocks_of(y), 1))
        sources[at] = outflows[at]
    current = outflows[:PATCH]
    for layer in range(1, LAYERS):
        current = [
            outflows[layer * PATCH + e] - times(chosen(current, ups[layer][e]), passing[layer * PATCH + e])
            for e in range(PATCH)
        ]
    starts = [chosen(ups[0], chosen(ups[1], ups[2][e])) for e in range(PATCH)]
    maps = placed([jnp.concatenate([composed[e], current[e]], axis=0) for e in range(PATCH)], starts)
    ends = placed([jnp.full((1, LANES), float(e), F32) for e in range(PATCH)], starts)
    packed[...] = pack(maps, ends_of(ends))


def ordered(mine, theirs, bit):
    later = (lax.axis_index("sweep") >> bit & 1) == 1
    first, first_ends = unpack(jnp.where(later, theirs, mine))
    second, second_ends = unpack(jnp.where(later, mine, theirs))
    return first, rows_of(first_ends), second, rows_of(second_ends)


def joined(mine, theirs, bit):
    first, first_ends, second, second_ends = ordered(mine, theirs, bit)
    maps = [after(first[at], chosen(second, first_ends[at])) for at in range(PATCH)]
    return pack(maps, ends_of([chosen(second_ends, at) for at in first_ends]))


def pair_kernel(mine, theirs, packed):
    packed[...] = joined(mine[...], theirs[...], 0)


def group_kernel(mine, theirs, unused, packed):
    packed[...] = joined(mine[...], theirs[...], 1)


def leaving_kernel(mine, theirs, leaving):
    first, first_ends, second, second_ends = ordered(mine[...], theirs[...], 1)
    states = [after(first[at][TRACE:], chosen(second, first_ends[at])) for at in range(PATCH)]
    leaving[...] = pack_states(placed(states, [chosen(second_ends, at) for at in first_ends]))


def prefix_kernel(pair, theirs, prefixes, ends):
    me = lax.axis_index("sweep")
    partner, partner_ends = unpack(pair[...])
    row = lax.broadcasted_iota(jnp.int32, (MAP_ROWS, LANES), 0)
    same = (row == lane_ids(MAP_ROWS)).astype(F32)
    later = (me & 1) == 1
    own = [jnp.where(later, x, same) for x in partner]
    own_ends = [jnp.where(later, x, float(at)) for at, x in enumerate(rows_of(partner_ends))]
    first, first_ends = unpack(theirs[...])
    first_ends = rows_of(first_ends)
    later = (me >> 1 & 1) == 1
    out = []
    for at in range(PATCH):
        whole = after(first[at], chosen(own, first_ends[at]))
        prefixes[at] = jnp.where(later, whole, own[at])
        out.append(jnp.where(later, chosen(own_ends, first_ends[at]), own_ends[at]))
    ends[...] = ends_of(out)


def onward_kernel(entering, packed, leaving):
    maps, ends = unpack(packed[...])
    states = unpack_states(entering[...])
    states = [after(states[at], maps[at]) for at in range(PATCH)]
    leaving[...] = pack_states(placed(states, rows_of(ends)))


def finish_kernel(
    ups, second, fourth, third, before, prefixes, ends, old, solved, sources, weights, passing,
    new, traces, inner, outer, across, below, down, made, sems,
):
    maps, map_ends = unpack(before[...])
    second, fourth, third = [unpack_states(x[...]) for x in (second, fourth, third)]
    states = [after(fourth[at], maps[at]) for at in range(PATCH)]
    last = placed(states, rows_of(map_ends))
    entering = [second[at] + third[at] + last[at] for at in range(PATCH)]
    states = [after(entering[at], prefixes[at]) for at in range(PATCH)]
    current = placed(states, rows_of(ends))
    ups = ups_of(ups)
    changes = []
    for layer in range(LAYERS):
        inflow = [chosen(current, ups[layer][e]) for e in range(PATCH)]
        current = [
            sources[layer * PATCH + e] - times(inflow[e], passing[layer * PATCH + e]) for e in range(PATCH)
        ]
        for e in range(PATCH):
            at = layer * PATCH + e
            x = solved[at] - times(inflow[e], weights[at])
            made[at] = x
            changes.append(old[at] - x)
    copy = pltpu.make_async_copy(made, new, sems.at[0])
    copy.start()
    put_inflows(put_sides(changes, traces, inner, outer, across), ups, down, below)
    copy.wait()


def near_residual_kernel(traces, down, coupling, lift, out, left, right):
    stacks = [near_slots(layer, e, traces, down) for layer in range(LAYERS) for e in range(PATCH)]
    for at, x in enumerate(lift_all(stacks, coupling, lift, left, right)):
        out[at] = x


def residual_kernel(near, from_above, outer, inner, from_across, coupling, lift, out, left, right):
    stacks = [
        far_slots(layer, e, from_above, outer, inner, from_across) for layer in range(LAYERS) for e in range(PATCH)
    ]
    for at, x in enumerate(lift_all(stacks, coupling, lift, left, right)):
        out[at] = near[at] + x


VMEM = pl.BlockSpec(memory_space=pltpu.VMEM)
FAR = pl.BlockSpec(memory_space=pl.ANY)


def call(kernel, outs, scratch=(), far_outs=(), micros=1):
    def run(*args):
        return pl.pallas_call(
            kernel,
            in_specs=[VMEM] * len(args),
            out_specs=[FAR if i in far_outs else VMEM for i in range(len(outs))],
            out_shape=[jax.ShapeDtypeStruct(shape, kind) for shape, kind in outs],
            scratch_shapes=list(scratch),
            compiler_params=pltpu.CompilerParams(vmem_limit_bytes=16 * 1024 * 1024),
            cost_estimate=pl.CostEstimate(
                flops=micros * 1_000_000_000, bytes_accessed=micros * 3_600_000, transcendentals=0
            ),
        )(*args)

    return run


SIDE_OUTS = [
    ((CELLS, 2 * VECS, (len(SLOT_FACES) - 1) * LANES), BF16),
    ((LAYERS * EY, VECS, LANES), F32),
    ((LAYERS * EY, VECS, LANES), F32),
    ((LAYERS * EX, VECS, LANES), F32),
]
BELOW = ((LAYERS * EY, VECS, LANES), F32)
DOWN = (((LAYERS - 1) * PATCH, 2 * VECS, LANES), BF16)
ROW_TILE = ((16, LANES), F32)
FLUXES = [pltpu.VMEM((CELLS * 2 * VECS, DEEP), BF16), pltpu.VMEM((CELLS * 2 * VECS, 6 * TRACE - DEEP), BF16)]
FIELD = ((CELLS, VECS, ROWS), F32)
STATES = ((3 * VECS, LANES), F32)
PACKED = ((3 * TRACE + 8, LANES), F32)


def exchange_sides(below, outer, inner, across):
    wide, deep = lax.axis_size("cx"), lax.axis_size("sweep")
    outer = lax.ppermute(outer, "cx", [(i, i + 1 if i % 2 else i - 1) for i in range(1, wide - 1)])
    below = lax.ppermute(below, "sweep", [(i + 1, i) for i in range(deep - 1)])
    inner = lax.ppermute(inner, "cx", [(i, i ^ 1) for i in range(wide)])
    across = lax.ppermute(across, "cy", [(0, 1), (1, 0)])
    return below, outer, inner, across


def swapped(packed, by):
    return lax.ppermute(packed, "sweep", [(i, i ^ by) for i in range(lax.axis_size("sweep"))])


def passed(states, source, target, shift):
    pairs = [(GROUP * source + p, GROUP * target + (p + shift) % GROUP) for p in range(GROUP)]
    return lax.ppermute(states, "sweep", pairs)


def local(rhs_vectors, old_iterate, diag_inverse, coupling, lift_table, upstream):
    old = old_iterate.reshape(CELLS, VECS, ROWS)
    rhs = rhs_vectors.reshape(CELLS, VECS, ROWS)
    diag = diag_inverse.reshape(CELLS, ROWS, ROWS)
    blocks = coupling.reshape(CELLS, TRACE, 6 * TRACE)
    lift = lift_table.T
    traces, inner, outer, across, faces = call(
        open_kernel, SIDE_OUTS + [((CELLS, 2 * VECS, LANES), F32)], micros=2
    )(old)
    ups, down, below = call(position_kernel, [ROW_TILE, DOWN, BELOW])(upstream.transpose(1, 2, 0), faces)
    halos = exchange_sides(below, outer, inner, across)
    lifted_rows, passing, composed = call(
        transfer_kernel,
        [((CELLS, DEEP, ROWS), BF16), ((CELLS, DEEP, LANES), BF16), ((PATCH, TRACE, LANES), F32)],
        [pltpu.VMEM((CELLS, DEEP, LANES), BF16), pltpu.VMEM((PATCH, TRACE, LANES), F32)],
    )(ups, diag, blocks, lift)
    solved, sources, single = call(source_kernel, [FIELD, ((CELLS, VECS, LANES), F32), PACKED], FLUXES)(
        ups, rhs, traces, down, *halos, diag, blocks, lift, passing, composed
    )
    partner = swapped(single, 1)
    (weights,) = call(weight_kernel, [((CELLS, DEEP, ROWS), BF16)])(blocks, lifted_rows, single)
    (pair,) = call(pair_kernel, [PACKED])(single, partner)
    partner_pair = swapped(pair, 2)
    (leaving,) = call(leaving_kernel, [STATES])(pair, partner_pair)
    second = passed(leaving, 0, 1, 2)
    (group,) = call(group_kernel, [PACKED])(pair, partner_pair, leaving)
    before = passed(group, 2, 3, 2)
    (leaving,) = call(onward_kernel, [STATES])(second, group)
    third = passed(leaving, 1, 2, 2)
    fourth = passed(leaving, 1, 3, 0)
    prefixes, ends = call(prefix_kernel, [((PATCH, MAP_ROWS, LANES), F32), ((8, LANES), F32)])(
        partner, partner_pair
    )
    new, traces, inner, outer, across, below, down = call(
        finish_kernel,
        [FIELD] + SIDE_OUTS + [BELOW, DOWN],
        [pltpu.VMEM((CELLS, VECS, ROWS), F32), pltpu.SemaphoreType.DMA((1,))],
        far_outs=(0,),
    )(ups, second, fourth, third, before, prefixes, ends, old, solved, sources, weights, passing)
    halos = exchange_sides(below, outer, inner, across)
    (near,) = call(near_residual_kernel, [FIELD], FLUXES)(traces, down, blocks, lift)
    (residual,) = call(residual_kernel, [FIELD], FLUXES)(near, *halos, blocks, lift)
    shape = rhs_vectors.shape
    return new.reshape(shape), residual.reshape(shape)


def solution(mesh):
    field = P("sweep", "cx", "cy", None, None)
    return jax.shard_map(
        local,
        mesh=mesh,
        in_specs=(field, field, field, field, P(), P("sweep", "cx", "cy")),
        out_specs=(field, field),
        check_vma=False,
    )
```

```python
import jax
import jax.numpy as jnp
from jax import lax
from jax.experimental import pallas as pl
from jax.experimental.pallas import tpu as pltpu
from jax.sharding import PartitionSpec as P

NPOINT = 4
ROWS = 320
TRACE = 80
VECS = 16
LAYERS = 3
EX = 2
EY = 2
PATCH = EX * EY
CELLS = LAYERS * PATCH
LANES = 128
DEEP = 2 * LANES
GROUP = 4
NODES = NPOINT**3
MAP_ROWS = TRACE + VECS
BF16 = jnp.bfloat16
F32 = jnp.float32

FACE_ROWS = ((0, 16, 4), (3, 16, 4), (0, 4, 1), (48, 4, 1), (0, 16, 1), (12, 16, 1))
SLOT_FACES = (0, 3, 2, 5, 4)


def split(x):
    high = x.astype(BF16)
    low = (x - high.astype(F32)).astype(BF16)
    return high, low


def stacked(x):
    return jnp.concatenate(split(x), axis=0)


def dot(a, b):
    return jnp.dot(a, b, preferred_element_type=F32)


def dot_rows(a, b):
    return lax.dot_general(a, b, (((1,), (1,)), ((), ())), preferred_element_type=F32)


def halves(x):
    rows = x.shape[0] // 2
    return x[:rows] + x[rows:]


def deep_rows(table):
    high, low = split(table)
    gap = jnp.zeros((LANES - TRACE, table.shape[1]), BF16)
    return jnp.concatenate([high, gap, low, gap], axis=0)


def deep_lhs(x):
    high, low = split(x)
    return jnp.concatenate(
        [jnp.concatenate([high, high], axis=1), jnp.concatenate([low, low], axis=1)], axis=0
    )


def times(x, deep):
    return halves(dot(deep_lhs(x), deep))


def lane_take(x, index):
    return jnp.take_along_axis(x, index, axis=1)


def lane_ids(rows):
    return lax.broadcasted_iota(jnp.int32, (rows, LANES), 1)


def blocks_of(x):
    rest = ROWS - 2 * LANES
    tail = jnp.concatenate([x[:, 2 * LANES :], jnp.zeros((x.shape[0], LANES - rest), x.dtype)], axis=1)
    return x[:, :LANES], x[:, LANES : 2 * LANES], tail


def face_of(blocks, face):
    start, a_step, b_step = FACE_ROWS[face]
    lane = lane_ids(blocks[0].shape[0])
    entry = lane & 15
    index = (lane >> 4 & 1) * NODES + start + (entry >> 2) * a_step + (entry & 3) * b_step
    first, second, third = [lane_take(block, index) for block in blocks]
    third = jnp.where(lane < TRACE, third, 0.0)
    return jnp.where(lane < 32, first, jnp.where(lane < 64, second, third))


def side_table():
    row = lax.broadcasted_iota(jnp.int32, (ROWS, LANES), 0)
    lane = lane_ids(1)
    blocks = []
    for face in SLOT_FACES:
        start, a_step, b_step = FACE_ROWS[face]
        source = (lane >> 4) * NODES + start + (lane >> 2 & 3) * a_step + (lane & 3) * b_step
        source = jnp.where(lane < TRACE, source, -1)
        blocks.append(jnp.where(row == source, 1.0, 0.0).astype(BF16))
    return jnp.concatenate(blocks, axis=1)


def rows_of(ends):
    return [ends[at : at + 1] for at in range(PATCH)]


def ends_of(rows):
    return jnp.concatenate(list(rows) + [jnp.zeros((8 - PATCH, LANES), F32)], axis=0)


def chosen(items, at):
    out = items[0]
    for number in range(1, PATCH):
        out = jnp.where(at == number, items[number], out)
    return out


def placed(states, ends):
    out = []
    for position in range(PATCH):
        total = jnp.where(ends[0] == position, states[0], 0.0)
        for at in range(1, PATCH):
            total = total + jnp.where(ends[at] == position, states[at], 0.0)
        out.append(total)
    return out


def ups_of(ups):
    return [[ups[layer * PATCH + e : layer * PATCH + e + 1] for e in range(PATCH)] for layer in range(LAYERS)]


def position_rows(links):
    found = []
    lane = lax.broadcasted_iota(jnp.int32, (EY, LAYERS), 1)
    for layer in range(LAYERS):
        for a in range(EX):
            value = jnp.sum(jnp.where(lane == layer, links[a], 0).astype(F32), axis=1, keepdims=True)
            found.append(jnp.broadcast_to(value, (EY, LANES)))
    return jnp.concatenate(found + [jnp.zeros((16 - CELLS, LANES), F32)], axis=0)


def put_sides(rows, traces, inner, outer, across):
    core = lax.axis_index("cy")
    even = lax.rem(lax.axis_index("cx"), 2) == 0
    picked = dot(rows[...], side_table())
    pieces = [picked[2 * VECS * at : 2 * VECS * (at + 1)] for at in range(CELLS)]
    whole = [halves(piece[:, LANES:]) for piece in pieces]
    for layer in range(LAYERS):
        block = lambda e, s: whole[layer * PATCH + e][:, (s - 1) * LANES : s * LANES]
        for e in range(PATCH):
            traces[layer * PATCH + e] = pieces[layer * PATCH + e][:, LANES:].astype(BF16)
        for b in range(EY):
            east, west = block(EY + b, 1), block(b, 2)
            inner[layer * EY + b] = jnp.where(even, east, west)
            outer[layer * EY + b] = jnp.where(even, west, east)
        for a in range(EX):
            across[layer * EX + a] = jnp.where(core == 0, block(a * EY + 1, 3), block(a * EY, 4))
    return [piece[:, :LANES] for piece in pieces]


def put_inflows(pieces, ups, down, below):
    for e, state in enumerate(placed([halves(pieces[e]) for e in range(PATCH)], ups[0])):
        below[e] = state
    for e in range(PATCH, LAYERS * EY):
        below[e] = jnp.zeros((VECS, LANES), F32)
    for layer in range(1, LAYERS):
        for e, piece in enumerate(placed(pieces[layer * PATCH : (layer + 1) * PATCH], ups[layer])):
            down[(layer - 1) * PATCH + e] = piece.astype(BF16)


def open_kernel(old, traces, inner, outer, across, faces, rows):
    for at in range(CELLS):
        rows[2 * VECS * at : 2 * VECS * (at + 1)] = stacked(old[at])
    for at, piece in enumerate(put_sides(rows, traces, inner, outer, across)):
        faces[at] = piece


def position_kernel(links, faces, ups, down, below):
    rows = position_rows(links)
    ups[...] = rows
    put_inflows([faces[at] for at in range(CELLS)], ups_of(rows), down, below)


def near_slots(layer, e, traces, down):
    a, b = e // EY, e % EY
    own = lambda cell, s: traces[layer * PATCH + cell, :, (s - 1) * LANES : s * LANES]
    slots = {}
    if layer < LAYERS - 1:
        slots[1] = down[layer * PATCH + e]
    slots[2 if a == 1 else 3] = own(b, 1) if a == 1 else own(EY + b, 2)
    slots[4 if b == 1 else 5] = own(a * EY, 3) if b == 1 else own(a * EY + 1, 4)
    return slots


def far_slots(layer, e, from_above, outer, inner, from_across):
    core = lax.axis_index("cy")
    even = lax.rem(lax.axis_index("cx"), 2) == 0
    a, b = e // EY, e % EY
    close, wide = inner[layer * EY + b], outer[layer * EY + b]
    other = from_across[layer * EX + a]
    slots = {}
    if layer == LAYERS - 1:
        slots[1] = stacked(from_above[e])
    slots[2 if a == 0 else 3] = stacked(jnp.where(even, wide, close) if a == 0 else jnp.where(even, close, wide))
    slots[4 if b == 0 else 5] = stacked(jnp.where(core == (1 if b == 0 else 0), other, 0.0))
    return slots


def lift_all(stacks, coupling, lift, left, right):
    lane = lax.broadcasted_iota(jnp.int32, (2 * VECS, DEEP), 1)
    r = 2 * VECS
    for at, slots in enumerate(stacks):
        for begin, numbers, kept_rows in ((0, (1, 2, 3), left), (DEEP, (3, 4, 5), right)):
            present = [slot for slot in numbers if slot in slots]
            y = dot(
                jnp.concatenate([slots[slot] for slot in present], axis=0)[:, :TRACE],
                coupling[at, :, begin : min(begin + DEEP, 6 * TRACE)],
            )
            place = lane[:, : y.shape[1]] + begin
            kept = jnp.zeros((r, y.shape[1]), F32)
            for i, slot in enumerate(present):
                inside = (place >= slot * TRACE) & (place < (slot + 1) * TRACE)
                kept = jnp.where(inside, y[r * i : r * (i + 1)], kept)
            kept_rows[r * at : r * (at + 1)] = stacked(halves(kept))
    out = dot_rows(left[...], lift[:, :DEEP]) + dot_rows(right[...], lift[:, DEEP:])
    return [halves(out[r * at : r * (at + 1)]) for at in range(CELLS)]


def transfer_kernel(ups, diag, coupling, lift, lifted_rows, passing, composed, outflows, first):
    ups = ups_of(ups)
    one = lax.broadcasted_iota(jnp.int32, (TRACE, TRACE), 0)
    two = lax.broadcasted_iota(jnp.int32, (TRACE, TRACE), 1)
    inflow = dot_rows((one == two).astype(F32).astype(BF16), lift[:, :TRACE]).astype(BF16)
    upper, lower = inflow[:NODES, :DEEP], inflow[NODES:, DEEP:]
    for at in range(CELLS):
        lifts = jnp.concatenate([dot(upper, diag[at, :DEEP]), dot(lower, diag[at, DEEP:])], axis=0)
        lifted_rows[at] = deep_rows(lifts)
        outflows[at] = deep_rows(face_of(blocks_of(lifts), 1))
    for at in range(CELLS):
        upwind = coupling[at, :, :LANES]
        passed_on = dot(jnp.concatenate([upwind, upwind], axis=1), outflows[at])
        passing[at] = deep_rows(passed_on)
        if at < PATCH:
            first[at] = passed_on
    source = [first[e] for e in range(PATCH)]
    both = [times(chosen(source, ups[1][e]), passing[PATCH + e]) for e in range(PATCH)]
    for e in range(PATCH):
        composed[e] = -times(chosen(both, ups[2][e]), passing[2 * PATCH + e])


def weight_kernel(coupling, lifted_rows, unused, weights):
    for at in range(CELLS):
        upwind = coupling[at][:, :LANES]
        weights[at] = deep_rows(dot(jnp.concatenate([upwind, upwind], axis=1), lifted_rows[at]))


def turned(x, by):
    return pltpu.roll(x, by % LANES, 1)


def pack(maps, ends):
    lane = lane_ids(TRACE)
    square = [x[:TRACE] for x in maps]
    source = [x[TRACE:] for x in maps]
    all_sources = jnp.concatenate(source, axis=0)
    part = lane_ids(VECS) >> 4
    last = jnp.where(part == 5, turned(source[0], 16), jnp.where(part == 6, turned(source[1], 32), turned(source[2], 48)))
    one = jnp.where(lane < TRACE, square[0], turned(square[3], TRACE))
    rest = jnp.concatenate([turned(all_sources, 64), turned(source[3], 48)], axis=0)
    two = jnp.where(lane < TRACE, square[1], jnp.where(lane < 112, turned(square[3], 32), rest))
    three = jnp.where(lane < TRACE, square[2], jnp.concatenate([turned(all_sources, TRACE), last], axis=0))
    return jnp.concatenate([one, two, three, ends], axis=0)


def unpack(packed):
    lane = lane_ids(TRACE)
    one, two, three = [packed[TRACE * at : TRACE * (at + 1)] for at in range(3)]
    four = jnp.where(lane < 48, turned(one, 48), turned(two, 96))
    square = [jnp.where(lane < TRACE, x, 0.0) for x in (one, two, three, four)]
    lane = lane_ids(PATCH * VECS)
    most = jnp.where(lane < 48, turned(three[: PATCH * VECS], 48), turned(two[: PATCH * VECS], 64))
    ends = [turned(three[PATCH * VECS :], by) for by in (112, 96, 80)] + [turned(two[PATCH * VECS :], 80)]
    lane = lane_ids(VECS)
    maps = []
    for at in range(PATCH):
        source = jnp.where(lane < 64, most[VECS * at : VECS * (at + 1)], jnp.where(lane < TRACE, ends[at], 0.0))
        maps.append(jnp.concatenate([square[at], source], axis=0))
    return maps, packed[3 * TRACE : 3 * TRACE + 8]


def pack_states(states):
    lane = lane_ids(VECS)
    one = jnp.where(lane < TRACE, states[0], turned(states[3], TRACE))
    two = jnp.where(lane < TRACE, states[1], turned(states[3], 32))
    return jnp.concatenate([one, two, states[2]], axis=0)


def unpack_states(packed):
    lane = lane_ids(VECS)
    one, two, three = [packed[VECS * at : VECS * (at + 1)] for at in range(3)]
    four = jnp.where(lane < 48, turned(one, 48), turned(two, 96))
    return [jnp.where(lane < TRACE, x, 0.0) for x in (one, two, three, four)]


def after(first, second):
    nothing = jnp.zeros((TRACE, LANES), F32)
    added = jnp.concatenate([nothing, second[TRACE:]], axis=0) if first.shape[0] > VECS else second[TRACE:]
    return times(first, deep_rows(second[:TRACE])) + added


def source_kernel(
    ups, rest, from_above, outer, inner, from_across, diag, coupling, lift, passing, composed,
    solved, sources, packed, left, right,
):
    ups = ups_of(ups)
    stacks = [
        far_slots(layer, e, from_above, outer, inner, from_across) for layer in range(LAYERS) for e in range(PATCH)
    ]
    outflows = []
    for at, x in enumerate(lift_all(stacks, coupling, lift, left, right)):
        y = halves(dot(stacked(rest[at] - x), diag[at]))
        solved[at] = y
        outflows.append(face_of(blocks_of(y), 1))
        sources[at] = outflows[at]
    current = outflows[:PATCH]
    for layer in range(1, LAYERS):
        current = [
            outflows[layer * PATCH + e] - times(chosen(current, ups[layer][e]), passing[layer * PATCH + e])
            for e in range(PATCH)
        ]
    starts = [chosen(ups[0], chosen(ups[1], ups[2][e])) for e in range(PATCH)]
    maps = placed([jnp.concatenate([composed[e], current[e]], axis=0) for e in range(PATCH)], starts)
    ends = placed([jnp.full((1, LANES), float(e), F32) for e in range(PATCH)], starts)
    packed[...] = pack(maps, ends_of(ends))


def ordered(mine, theirs, bit):
    later = (lax.axis_index("sweep") >> bit & 1) == 1
    first, first_ends = unpack(jnp.where(later, theirs, mine))
    second, second_ends = unpack(jnp.where(later, mine, theirs))
    return first, rows_of(first_ends), second, rows_of(second_ends)


def joined(mine, theirs, bit):
    first, first_ends, second, second_ends = ordered(mine, theirs, bit)
    maps = [after(first[at], chosen(second, first_ends[at])) for at in range(PATCH)]
    return pack(maps, ends_of([chosen(second_ends, at) for at in first_ends]))


def pair_kernel(mine, theirs, packed):
    packed[...] = joined(mine[...], theirs[...], 0)


def group_kernel(mine, theirs, unused, packed):
    packed[...] = joined(mine[...], theirs[...], 1)


def leaving_kernel(mine, theirs, leaving):
    first, first_ends, second, second_ends = ordered(mine[...], theirs[...], 1)
    states = [after(first[at][TRACE:], chosen(second, first_ends[at])) for at in range(PATCH)]
    leaving[...] = pack_states(placed(states, [chosen(second_ends, at) for at in first_ends]))


def prefix_kernel(pair, theirs, prefixes, ends):
    me = lax.axis_index("sweep")
    partner, partner_ends = unpack(pair[...])
    row = lax.broadcasted_iota(jnp.int32, (MAP_ROWS, LANES), 0)
    same = (row == lane_ids(MAP_ROWS)).astype(F32)
    later = (me & 1) == 1
    own = [jnp.where(later, x, same) for x in partner]
    own_ends = [jnp.where(later, x, float(at)) for at, x in enumerate(rows_of(partner_ends))]
    first, first_ends = unpack(theirs[...])
    first_ends = rows_of(first_ends)
    later = (me >> 1 & 1) == 1
    out = []
    for at in range(PATCH):
        whole = after(first[at], chosen(own, first_ends[at]))
        prefixes[at] = jnp.where(later, whole, own[at])
        out.append(jnp.where(later, chosen(own_ends, first_ends[at]), own_ends[at]))
    ends[...] = ends_of(out)


def onward_kernel(entering, packed, leaving):
    maps, ends = unpack(packed[...])
    states = unpack_states(entering[...])
    states = [after(states[at], maps[at]) for at in range(PATCH)]
    leaving[...] = pack_states(placed(states, rows_of(ends)))


def finish_kernel(
    ups, second, fourth, third, before, prefixes, ends, old, solved, sources, weights, passing,
    new, traces, inner, outer, across, below, down, made, operands, rows, sems,
):
    maps, map_ends = unpack(before[...])
    second, fourth, third = [unpack_states(x[...]) for x in (second, fourth, third)]
    states = [after(fourth[at], maps[at]) for at in range(PATCH)]
    last = placed(states, rows_of(map_ends))
    entering = [second[at] + third[at] + last[at] for at in range(PATCH)]
    states = [after(entering[at], prefixes[at]) for at in range(PATCH)]
    current = placed(states, rows_of(ends))
    ups = ups_of(ups)
    for layer in range(LAYERS):
        inflow = [chosen(current, ups[layer][e]) for e in range(PATCH)]
        for e in range(PATCH):
            operands[layer * PATCH + e] = deep_lhs(inflow[e])
        if layer < LAYERS - 1:
            current = [
                sources[layer * PATCH + e] - halves(dot(operands[layer * PATCH + e], passing[layer * PATCH + e]))
                for e in range(PATCH)
            ]
    for at in range(CELLS):
        x = solved[at] - halves(dot(operands[at], weights[at]))
        made[at] = x
        rows[2 * VECS * at : 2 * VECS * (at + 1)] = stacked(old[at] - x)
    copy = pltpu.make_async_copy(made, new, sems.at[0])
    copy.start()
    put_inflows(put_sides(rows, traces, inner, outer, across), ups, down, below)
    copy.wait()


def near_source_kernel(rhs, traces, down, coupling, lift, out, left, right):
    stacks = [near_slots(layer, e, traces, down) for layer in range(LAYERS) for e in range(PATCH)]
    for at, x in enumerate(lift_all(stacks, coupling, lift, left, right)):
        out[at] = rhs[at] - x


def near_residual_kernel(traces, down, coupling, lift, out, left, right):
    stacks = [near_slots(layer, e, traces, down) for layer in range(LAYERS) for e in range(PATCH)]
    for at, x in enumerate(lift_all(stacks, coupling, lift, left, right)):
        out[at] = x


def residual_kernel(near, from_above, outer, inner, from_across, coupling, lift, out, left, right):
    stacks = [
        far_slots(layer, e, from_above, outer, inner, from_across) for layer in range(LAYERS) for e in range(PATCH)
    ]
    for at, x in enumerate(lift_all(stacks, coupling, lift, left, right)):
        out[at] = near[at] + x


VMEM = pl.BlockSpec(memory_space=pltpu.VMEM)
FAR = pl.BlockSpec(memory_space=pl.ANY)


def call(kernel, outs, scratch=(), far_outs=(), micros=1):
    def run(*args):
        return pl.pallas_call(
            kernel,
            in_specs=[VMEM] * len(args),
            out_specs=[FAR if i in far_outs else VMEM for i in range(len(outs))],
            out_shape=[jax.ShapeDtypeStruct(shape, kind) for shape, kind in outs],
            scratch_shapes=list(scratch),
            compiler_params=pltpu.CompilerParams(vmem_limit_bytes=16 * 1024 * 1024),
            cost_estimate=pl.CostEstimate(
                flops=micros * 1_000_000_000, bytes_accessed=micros * 3_600_000, transcendentals=0
            ),
        )(*args)

    return run


SIDE_OUTS = [
    ((CELLS, 2 * VECS, (len(SLOT_FACES) - 1) * LANES), BF16),
    ((LAYERS * EY, VECS, LANES), F32),
    ((LAYERS * EY, VECS, LANES), F32),
    ((LAYERS * EX, VECS, LANES), F32),
]
BELOW = ((LAYERS * EY, VECS, LANES), F32)
DOWN = (((LAYERS - 1) * PATCH, 2 * VECS, LANES), BF16)
ROW_TILE = ((16, LANES), F32)
CELL_ROWS = pltpu.VMEM((CELLS * 2 * VECS, ROWS), BF16)
FLUXES = [pltpu.VMEM((CELLS * 2 * VECS, DEEP), BF16), pltpu.VMEM((CELLS * 2 * VECS, 6 * TRACE - DEEP), BF16)]
FIELD = ((CELLS, VECS, ROWS), F32)
STATES = ((3 * VECS, LANES), F32)
PACKED = ((3 * TRACE + 8, LANES), F32)


def exchange_sides(below, outer, inner, across):
    wide, deep = lax.axis_size("cx"), lax.axis_size("sweep")
    outer = lax.ppermute(outer, "cx", [(i, i + 1 if i % 2 else i - 1) for i in range(1, wide - 1)])
    below = lax.ppermute(below, "sweep", [(i + 1, i) for i in range(deep - 1)])
    inner = lax.ppermute(inner, "cx", [(i, i ^ 1) for i in range(wide)])
    across = lax.ppermute(across, "cy", [(0, 1), (1, 0)])
    return below, outer, inner, across


def swapped(packed, by):
    return lax.ppermute(packed, "sweep", [(i, i ^ by) for i in range(lax.axis_size("sweep"))])


def passed(states, source, target, shift):
    pairs = [(GROUP * source + p, GROUP * target + (p + shift) % GROUP) for p in range(GROUP)]
    return lax.ppermute(states, "sweep", pairs)


def local(rhs_vectors, old_iterate, diag_inverse, coupling, lift_table, upstream):
    old = old_iterate.reshape(CELLS, VECS, ROWS)
    rhs = rhs_vectors.reshape(CELLS, VECS, ROWS)
    diag = diag_inverse.reshape(CELLS, ROWS, ROWS)
    blocks = coupling.reshape(CELLS, TRACE, 6 * TRACE)
    lift = lift_table.T
    traces, inner, outer, across, faces = call(
        open_kernel, SIDE_OUTS + [((CELLS, 2 * VECS, LANES), F32)], [CELL_ROWS], micros=2
    )(old)
    ups, down, below = call(position_kernel, [ROW_TILE, DOWN, BELOW])(upstream.transpose(1, 2, 0), faces)
    halos = exchange_sides(below, outer, inner, across)
    lifted_rows, passing, composed = call(
        transfer_kernel,
        [((CELLS, DEEP, ROWS), BF16), ((CELLS, DEEP, LANES), BF16), ((PATCH, TRACE, LANES), F32)],
        [pltpu.VMEM((CELLS, DEEP, LANES), BF16), pltpu.VMEM((PATCH, TRACE, LANES), F32)],
    )(ups, diag, blocks, lift)
    (rest,) = call(near_source_kernel, [FIELD], FLUXES)(rhs, traces, down, blocks, lift)
    solved, sources, single = call(source_kernel, [FIELD, ((CELLS, VECS, LANES), F32), PACKED], FLUXES)(
        ups, rest, *halos, diag, blocks, lift, passing, composed
    )
    partner = swapped(single, 1)
    (weights,) = call(weight_kernel, [((CELLS, DEEP, ROWS), BF16)])(blocks, lifted_rows, single)
    (pair,) = call(pair_kernel, [PACKED])(single, partner)
    partner_pair = swapped(pair, 2)
    (leaving,) = call(leaving_kernel, [STATES])(pair, partner_pair)
    second = passed(leaving, 0, 1, 2)
    (group,) = call(group_kernel, [PACKED])(pair, partner_pair, leaving)
    before = passed(group, 2, 3, 2)
    (leaving,) = call(onward_kernel, [STATES])(second, group)
    third = passed(leaving, 1, 2, 2)
    fourth = passed(leaving, 1, 3, 0)
    prefixes, ends = call(prefix_kernel, [((PATCH, MAP_ROWS, LANES), F32), ((8, LANES), F32)])(
        partner, partner_pair
    )
    new, traces, inner, outer, across, below, down = call(
        finish_kernel,
        [FIELD] + SIDE_OUTS + [BELOW, DOWN],
        [
            pltpu.VMEM((CELLS, VECS, ROWS), F32),
            pltpu.VMEM((CELLS, 2 * VECS, DEEP), BF16),
            CELL_ROWS,
            pltpu.SemaphoreType.DMA((1,)),
        ],
        far_outs=(0,),
    )(ups, second, fourth, third, before, prefixes, ends, old, solved, sources, weights, passing)
    halos = exchange_sides(below, outer, inner, across)
    (near,) = call(near_residual_kernel, [FIELD], FLUXES)(traces, down, blocks, lift)
    (residual,) = call(residual_kernel, [FIELD], FLUXES)(near, *halos, blocks, lift)
    shape = rhs_vectors.shape
    return new.reshape(shape), residual.reshape(shape)


def solution(mesh):
    field = P("sweep", "cx", "cy", None, None)
    return jax.shard_map(
        local,
        mesh=mesh,
        in_specs=(field, field, field, field, P(), P("sweep", "cx", "cy")),
        out_specs=(field, field),
        check_vma=False,
    )
```

```python
import jax
import jax.numpy as jnp
from jax import lax
from jax.experimental import pallas as pl
from jax.experimental.pallas import tpu as pltpu
from jax.sharding import PartitionSpec as P

NPOINT = 4
ROWS = 320
TRACE = 80
VECS = 16
LAYERS = 3
EX = 2
EY = 2
PATCH = EX * EY
CELLS = LAYERS * PATCH
LANES = 128
DEEP = 2 * LANES
GROUP = 4
NODES = NPOINT**3
MAP_ROWS = TRACE + VECS
BF16 = jnp.bfloat16
F32 = jnp.float32

FACE_ROWS = ((0, 16, 4), (3, 16, 4), (0, 4, 1), (48, 4, 1), (0, 16, 1), (12, 16, 1))
SLOT_FACES = (0, 3, 2, 5, 4)


def split(x):
    high = x.astype(BF16)
    low = (x - high.astype(F32)).astype(BF16)
    return high, low


def stacked(x):
    return jnp.concatenate(split(x), axis=0)


def dot(a, b):
    return jnp.dot(a, b, preferred_element_type=F32)


def dot_rows(a, b):
    return lax.dot_general(a, b, (((1,), (1,)), ((), ())), preferred_element_type=F32)


def halves(x):
    rows = x.shape[0] // 2
    return x[:rows] + x[rows:]


def deep_rows(table):
    high, low = split(table)
    gap = jnp.zeros((LANES - TRACE, table.shape[1]), BF16)
    return jnp.concatenate([high, gap, low, gap], axis=0)


def deep_lhs(x):
    high, low = split(x)
    return jnp.concatenate(
        [jnp.concatenate([high, high], axis=1), jnp.concatenate([low, low], axis=1)], axis=0
    )


def times(x, deep):
    return halves(dot(deep_lhs(x), deep))


def lane_take(x, index):
    return jnp.take_along_axis(x, index, axis=1)


def lane_ids(rows):
    return lax.broadcasted_iota(jnp.int32, (rows, LANES), 1)


def blocks_of(x):
    rest = ROWS - 2 * LANES
    tail = jnp.concatenate([x[:, 2 * LANES :], jnp.zeros((x.shape[0], LANES - rest), x.dtype)], axis=1)
    return x[:, :LANES], x[:, LANES : 2 * LANES], tail


def face_of(blocks, face):
    start, a_step, b_step = FACE_ROWS[face]
    lane = lane_ids(blocks[0].shape[0])
    entry = lane & 15
    index = (lane >> 4 & 1) * NODES + start + (entry >> 2) * a_step + (entry & 3) * b_step
    first, second, third = [lane_take(block, index) for block in blocks]
    third = jnp.where(lane < TRACE, third, 0.0)
    return jnp.where(lane < 32, first, jnp.where(lane < 64, second, third))


def side_table():
    row = lax.broadcasted_iota(jnp.int32, (ROWS, LANES), 0)
    lane = lane_ids(1)
    blocks = []
    for face in SLOT_FACES:
        start, a_step, b_step = FACE_ROWS[face]
        source = (lane >> 4) * NODES + start + (lane >> 2 & 3) * a_step + (lane & 3) * b_step
        source = jnp.where(lane < TRACE, source, -1)
        blocks.append(jnp.where(row == source, 1.0, 0.0).astype(BF16))
    return jnp.concatenate(blocks, axis=1)


def rows_of(ends):
    return [ends[at : at + 1] for at in range(PATCH)]


def ends_of(rows):
    return jnp.concatenate(list(rows) + [jnp.zeros((8 - PATCH, LANES), F32)], axis=0)


def chosen(items, at):
    out = items[0]
    for number in range(1, PATCH):
        out = jnp.where(at == number, items[number], out)
    return out


def placed(states, ends):
    out = []
    for position in range(PATCH):
        total = jnp.where(ends[0] == position, states[0], 0.0)
        for at in range(1, PATCH):
            total = total + jnp.where(ends[at] == position, states[at], 0.0)
        out.append(total)
    return out


def ups_of(ups):
    return [[ups[layer * PATCH + e : layer * PATCH + e + 1] for e in range(PATCH)] for layer in range(LAYERS)]


def position_rows(links):
    found = []
    lane = lax.broadcasted_iota(jnp.int32, (EY, LAYERS), 1)
    for layer in range(LAYERS):
        for a in range(EX):
            value = jnp.sum(jnp.where(lane == layer, links[a], 0).astype(F32), axis=1, keepdims=True)
            found.append(jnp.broadcast_to(value, (EY, LANES)))
    return jnp.concatenate(found + [jnp.zeros((16 - CELLS, LANES), F32)], axis=0)


def put_sides(cells, traces, inner, outer, across):
    core = lax.axis_index("cy")
    even = lax.rem(lax.axis_index("cx"), 2) == 0
    picked = dot(jnp.concatenate([stacked(x) for x in cells], axis=0), side_table())
    pieces = [picked[2 * VECS * at : 2 * VECS * (at + 1)] for at in range(CELLS)]
    whole = [halves(piece[:, LANES:]) for piece in pieces]
    for layer in range(LAYERS):
        block = lambda e, s: whole[layer * PATCH + e][:, (s - 1) * LANES : s * LANES]
        for e in range(PATCH):
            traces[layer * PATCH + e] = pieces[layer * PATCH + e][:, LANES:].astype(BF16)
        for b in range(EY):
            east, west = block(EY + b, 1), block(b, 2)
            inner[layer * EY + b] = jnp.where(even, east, west)
            outer[layer * EY + b] = jnp.where(even, west, east)
        for a in range(EX):
            across[layer * EX + a] = jnp.where(core == 0, block(a * EY + 1, 3), block(a * EY, 4))
    return [piece[:, :LANES] for piece in pieces]


def put_below(pieces, ups, below):
    for e, state in enumerate(placed([halves(pieces[e]) for e in range(PATCH)], ups[0])):
        below[e] = state
    for e in range(PATCH, LAYERS * EY):
        below[e] = jnp.zeros((VECS, LANES), F32)


def put_down(pieces, ups, down):
    for layer in range(1, LAYERS):
        for e, piece in enumerate(placed(pieces[layer * PATCH : (layer + 1) * PATCH], ups[layer])):
            down[(layer - 1) * PATCH + e] = piece.astype(BF16)


def open_kernel(old, traces, inner, outer, across, faces):
    for at, piece in enumerate(put_sides([old[at] for at in range(CELLS)], traces, inner, outer, across)):
        faces[at] = piece


def position_kernel(links, faces, ups, down, below):
    rows = position_rows(links)
    ups[...] = rows
    pieces = [faces[at] for at in range(CELLS)]
    put_below(pieces, ups_of(rows), below)
    put_down(pieces, ups_of(rows), down)


def near_slots(layer, e, traces, down):
    a, b = e // EY, e % EY
    own = lambda cell, s: traces[layer * PATCH + cell, :, (s - 1) * LANES : s * LANES]
    slots = {}
    if layer < LAYERS - 1:
        slots[1] = down[layer * PATCH + e]
    slots[2 if a == 1 else 3] = own(b, 1) if a == 1 else own(EY + b, 2)
    slots[4 if b == 1 else 5] = own(a * EY, 3) if b == 1 else own(a * EY + 1, 4)
    return slots


def far_slots(layer, e, from_above, outer, inner, from_across):
    core = lax.axis_index("cy")
    even = lax.rem(lax.axis_index("cx"), 2) == 0
    a, b = e // EY, e % EY
    close, wide = inner[layer * EY + b], outer[layer * EY + b]
    other = from_across[layer * EX + a]
    slots = {}
    if layer == LAYERS - 1 and from_above is not None:
        slots[1] = stacked(from_above[e])
    slots[2 if a == 0 else 3] = stacked(jnp.where(even, wide, close) if a == 0 else jnp.where(even, close, wide))
    slots[4 if b == 0 else 5] = stacked(jnp.where(core == (1 if b == 0 else 0), other, 0.0))
    return slots


def lift_all(stacks, coupling, lift, left, right):
    lane = lax.broadcasted_iota(jnp.int32, (2 * VECS, DEEP), 1)
    r = 2 * VECS
    for at, slots in enumerate(stacks):
        for begin, numbers, kept_rows in ((0, (1, 2, 3), left), (DEEP, (3, 4, 5), right)):
            present = [slot for slot in numbers if slot in slots]
            y = dot(
                jnp.concatenate([slots[slot] for slot in present], axis=0)[:, :TRACE],
                coupling[at, :, begin : min(begin + DEEP, 6 * TRACE)],
            )
            place = lane[:, : y.shape[1]] + begin
            kept = jnp.zeros((r, y.shape[1]), F32)
            for i, slot in enumerate(present):
                inside = (place >= slot * TRACE) & (place < (slot + 1) * TRACE)
                kept = jnp.where(inside, y[r * i : r * (i + 1)], kept)
            kept_rows[r * at : r * (at + 1)] = stacked(halves(kept))
    out = dot_rows(left[...], lift[:, :DEEP]) + dot_rows(right[...], lift[:, DEEP:])
    return [halves(out[r * at : r * (at + 1)]) for at in range(CELLS)]


def transfer_kernel(ups, diag, coupling, lift, lifted_rows, passing, composed, outflows, first):
    ups = ups_of(ups)
    one = lax.broadcasted_iota(jnp.int32, (TRACE, TRACE), 0)
    two = lax.broadcasted_iota(jnp.int32, (TRACE, TRACE), 1)
    inflow = dot_rows((one == two).astype(F32).astype(BF16), lift[:, :TRACE]).astype(BF16)
    upper, lower = inflow[:NODES, :DEEP], inflow[NODES:, DEEP:]
    for at in range(CELLS):
        lifts = jnp.concatenate([dot(upper, diag[at, :DEEP]), dot(lower, diag[at, DEEP:])], axis=0)
        lifted_rows[at] = deep_rows(lifts)
        outflows[at] = deep_rows(face_of(blocks_of(lifts), 1))
    for at in range(CELLS):
        upwind = coupling[at, :, :LANES]
        passed_on = dot(jnp.concatenate([upwind, upwind], axis=1), outflows[at])
        passing[at] = deep_rows(passed_on)
        if at < PATCH:
            first[at] = passed_on
    source = [first[e] for e in range(PATCH)]
    both = [times(chosen(source, ups[1][e]), passing[PATCH + e]) for e in range(PATCH)]
    for e in range(PATCH):
        composed[e] = -times(chosen(both, ups[2][e]), passing[2 * PATCH + e])


def weight_kernel(coupling, lifted_rows, unused, weights, front):
    for at in range(CELLS):
        upwind = coupling[at, :, :LANES]
        weight = dot(jnp.concatenate([upwind, upwind], axis=1), lifted_rows[at])
        weights[at] = deep_rows(weight)
        if at < PATCH:
            front[at] = face_of(blocks_of(weight), 0)


def turned(x, by):
    return pltpu.roll(x, by % LANES, 1)


def pack(maps, ends):
    lane = lane_ids(TRACE)
    square = [x[:TRACE] for x in maps]
    source = [x[TRACE:] for x in maps]
    all_sources = jnp.concatenate(source, axis=0)
    part = lane_ids(VECS) >> 4
    last = jnp.where(part == 5, turned(source[0], 16), jnp.where(part == 6, turned(source[1], 32), turned(source[2], 48)))
    one = jnp.where(lane < TRACE, square[0], turned(square[3], TRACE))
    rest = jnp.concatenate([turned(all_sources, 64), turned(source[3], 48)], axis=0)
    two = jnp.where(lane < TRACE, square[1], jnp.where(lane < 112, turned(square[3], 32), rest))
    three = jnp.where(lane < TRACE, square[2], jnp.concatenate([turned(all_sources, TRACE), last], axis=0))
    return jnp.concatenate([one, two, three, ends], axis=0)


def unpack(packed):
    lane = lane_ids(TRACE)
    one, two, three = [packed[TRACE * at : TRACE * (at + 1)] for at in range(3)]
    four = jnp.where(lane < 48, turned(one, 48), turned(two, 96))
    square = [jnp.where(lane < TRACE, x, 0.0) for x in (one, two, three, four)]
    lane = lane_ids(PATCH * VECS)
    most = jnp.where(lane < 48, turned(three[: PATCH * VECS], 48), turned(two[: PATCH * VECS], 64))
    ends = [turned(three[PATCH * VECS :], by) for by in (112, 96, 80)] + [turned(two[PATCH * VECS :], 80)]
    lane = lane_ids(VECS)
    maps = []
    for at in range(PATCH):
        source = jnp.where(lane < 64, most[VECS * at : VECS * (at + 1)], jnp.where(lane < TRACE, ends[at], 0.0))
        maps.append(jnp.concatenate([square[at], source], axis=0))
    return maps, packed[3 * TRACE : 3 * TRACE + 8]


def pack_states(states):
    lane = lane_ids(VECS)
    one = jnp.where(lane < TRACE, states[0], turned(states[3], TRACE))
    two = jnp.where(lane < TRACE, states[1], turned(states[3], 32))
    return jnp.concatenate([one, two, states[2]], axis=0)


def unpack_states(packed):
    lane = lane_ids(VECS)
    one, two, three = [packed[VECS * at : VECS * (at + 1)] for at in range(3)]
    four = jnp.where(lane < 48, turned(one, 48), turned(two, 96))
    return [jnp.where(lane < TRACE, x, 0.0) for x in (one, two, three, four)]


def after(first, second):
    nothing = jnp.zeros((TRACE, LANES), F32)
    added = jnp.concatenate([nothing, second[TRACE:]], axis=0) if first.shape[0] > VECS else second[TRACE:]
    return times(first, deep_rows(second[:TRACE])) + added


def source_kernel(
    ups, rhs, traces, down, from_above, outer, inner, from_across, diag, coupling, lift, passing, composed,
    solved, sources, packed, left, right,
):
    ups = ups_of(ups)
    stacks = [
        near_slots(layer, e, traces, down) | far_slots(layer, e, from_above, outer, inner, from_across)
        for layer in range(LAYERS)
        for e in range(PATCH)
    ]
    outflows = []
    for at, x in enumerate(lift_all(stacks, coupling, lift, left, right)):
        y = halves(dot(stacked(rhs[at] - x), diag[at]))
        solved[at] = y
        outflows.append(face_of(blocks_of(y), 1))
        sources[at] = outflows[at]
    current = outflows[:PATCH]
    for layer in range(1, LAYERS):
        current = [
            outflows[layer * PATCH + e] - times(chosen(current, ups[layer][e]), passing[layer * PATCH + e])
            for e in range(PATCH)
        ]
    starts = [chosen(ups[0], chosen(ups[1], ups[2][e])) for e in range(PATCH)]
    maps = placed([jnp.concatenate([composed[e], current[e]], axis=0) for e in range(PATCH)], starts)
    ends = placed([jnp.full((1, LANES), float(e), F32) for e in range(PATCH)], starts)
    packed[...] = pack(maps, ends_of(ends))


def ordered(mine, theirs, bit):
    later = (lax.axis_index("sweep") >> bit & 1) == 1
    first, first_ends = unpack(jnp.where(later, theirs, mine))
    second, second_ends = unpack(jnp.where(later, mine, theirs))
    return first, rows_of(first_ends), second, rows_of(second_ends)


def joined(mine, theirs, bit):
    first, first_ends, second, second_ends = ordered(mine, theirs, bit)
    maps = [after(first[at], chosen(second, first_ends[at])) for at in range(PATCH)]
    return pack(maps, ends_of([chosen(second_ends, at) for at in first_ends]))


def pair_kernel(mine, theirs, packed):
    packed[...] = joined(mine[...], theirs[...], 0)


def group_kernel(mine, theirs, unused, packed):
    packed[...] = joined(mine[...], theirs[...], 1)


def leaving_kernel(mine, theirs, leaving):
    first, first_ends, second, second_ends = ordered(mine[...], theirs[...], 1)
    states = [after(first[at][TRACE:], chosen(second, first_ends[at])) for at in range(PATCH)]
    leaving[...] = pack_states(placed(states, [chosen(second_ends, at) for at in first_ends]))


def prefix_kernel(pair, theirs, prefixes, ends):
    me = lax.axis_index("sweep")
    partner, partner_ends = unpack(pair[...])
    row = lax.broadcasted_iota(jnp.int32, (MAP_ROWS, LANES), 0)
    same = (row == lane_ids(MAP_ROWS)).astype(F32)
    later = (me & 1) == 1
    own = [jnp.where(later, x, same) for x in partner]
    own_ends = [jnp.where(later, x, float(at)) for at, x in enumerate(rows_of(partner_ends))]
    first, first_ends = unpack(theirs[...])
    first_ends = rows_of(first_ends)
    later = (me >> 1 & 1) == 1
    out = []
    for at in range(PATCH):
        whole = after(first[at], chosen(own, first_ends[at]))
        prefixes[at] = jnp.where(later, whole, own[at])
        out.append(jnp.where(later, chosen(own_ends, first_ends[at]), own_ends[at]))
    ends[...] = ends_of(out)


def onward_kernel(entering, packed, leaving):
    maps, ends = unpack(packed[...])
    states = unpack_states(entering[...])
    states = [after(states[at], maps[at]) for at in range(PATCH)]
    leaving[...] = pack_states(placed(states, rows_of(ends)))


def ahead_kernel(ups, front, solved, below, unused, packed):
    maps = [
        jnp.concatenate([front[e], -face_of(blocks_of(solved[e]), 0)], axis=0) for e in range(PATCH)
    ]
    maps = placed(maps, ups_of(ups)[0])
    maps = [jnp.concatenate([x[:TRACE], x[TRACE:] + below[e]], axis=0) for e, x in enumerate(maps)]
    packed[...] = pack(maps, jnp.zeros((8, LANES), F32))


def finish_kernel(
    ups, second, third, fourth, before, prefixes, ends, old, solved, sources, weights, passing,
    new, traces, inner, outer, across, down, leaving, made, sems,
):
    maps, map_ends = unpack(before[...])
    second, fourth, third = [unpack_states(x[...]) for x in (second, fourth, third)]
    states = [after(fourth[at], maps[at]) for at in range(PATCH)]
    last = placed(states, rows_of(map_ends))
    entering = [second[at] + third[at] + last[at] for at in range(PATCH)]
    states = [after(entering[at], prefixes[at]) for at in range(PATCH)]
    current = placed(states, rows_of(ends))
    ups = ups_of(ups)
    changes = []
    for layer in range(LAYERS):
        inflow = [chosen(current, ups[layer][e]) for e in range(PATCH)]
        current = [
            sources[layer * PATCH + e] - times(inflow[e], passing[layer * PATCH + e]) for e in range(PATCH)
        ]
        for e in range(PATCH):
            at = layer * PATCH + e
            x = solved[at] - times(inflow[e], weights[at])
            made[at] = x
            changes.append(old[at] - x)
    copy = pltpu.make_async_copy(made, new, sems.at[0])
    copy.start()
    put_down(put_sides(changes, traces, inner, outer, across), ups, down)
    for e in range(PATCH):
        leaving[e] = current[e]
    copy.wait()


def near_residual_kernel(traces, down, leaving, ahead, coupling, lift, out, left, right):
    stacks = [near_slots(layer, e, traces, down) for layer in range(LAYERS) for e in range(PATCH)]
    maps, unused = unpack(ahead[...])
    for e in range(PATCH):
        stacks[(LAYERS - 1) * PATCH + e][1] = stacked(after(leaving[e], maps[e]))
    for at, x in enumerate(lift_all(stacks, coupling, lift, left, right)):
        out[at] = x


def residual_kernel(near, outer, inner, from_across, coupling, lift, out, left, right):
    stacks = [
        far_slots(layer, e, None, outer, inner, from_across) for layer in range(LAYERS) for e in range(PATCH)
    ]
    for at, x in enumerate(lift_all(stacks, coupling, lift, left, right)):
        out[at] = near[at] + x


VMEM = pl.BlockSpec(memory_space=pltpu.VMEM)
FAR = pl.BlockSpec(memory_space=pl.ANY)


def call(kernel, outs, scratch=(), far_outs=(), micros=1):
    def run(*args):
        return pl.pallas_call(
            kernel,
            in_specs=[VMEM] * len(args),
            out_specs=[FAR if i in far_outs else VMEM for i in range(len(outs))],
            out_shape=[jax.ShapeDtypeStruct(shape, kind) for shape, kind in outs],
            scratch_shapes=list(scratch),
            compiler_params=pltpu.CompilerParams(vmem_limit_bytes=16 * 1024 * 1024),
            cost_estimate=pl.CostEstimate(
                flops=micros * 1_000_000_000, bytes_accessed=micros * 3_600_000, transcendentals=0
            ),
        )(*args)

    return run


SIDE_OUTS = [
    ((CELLS, 2 * VECS, (len(SLOT_FACES) - 1) * LANES), BF16),
    ((LAYERS * EY, VECS, LANES), F32),
    ((LAYERS * EY, VECS, LANES), F32),
    ((LAYERS * EX, VECS, LANES), F32),
]
BELOW = ((LAYERS * EY, VECS, LANES), F32)
DOWN = (((LAYERS - 1) * PATCH, 2 * VECS, LANES), BF16)
ROW_TILE = ((16, LANES), F32)
FLUXES = [pltpu.VMEM((CELLS * 2 * VECS, DEEP), BF16), pltpu.VMEM((CELLS * 2 * VECS, 6 * TRACE - DEEP), BF16)]
FIELD = ((CELLS, VECS, ROWS), F32)
STATES = ((3 * VECS, LANES), F32)
PACKED = ((3 * TRACE + 8, LANES), F32)


def from_next(piece):
    return lax.ppermute(piece, "sweep", [(i + 1, i) for i in range(lax.axis_size("sweep") - 1)])


def exchange_sides(outer, inner, across):
    wide = lax.axis_size("cx")
    outer = lax.ppermute(outer, "cx", [(i, i + 1 if i % 2 else i - 1) for i in range(1, wide - 1)])
    inner = lax.ppermute(inner, "cx", [(i, i ^ 1) for i in range(wide)])
    across = lax.ppermute(across, "cy", [(0, 1), (1, 0)])
    return outer, inner, across


def swapped(packed, by):
    return lax.ppermute(packed, "sweep", [(i, i ^ by) for i in range(lax.axis_size("sweep"))])


def passed(states, source, target, shift):
    pairs = [(GROUP * source + p, GROUP * target + (p + shift) % GROUP) for p in range(GROUP)]
    return lax.ppermute(states, "sweep", pairs)


def local(rhs_vectors, old_iterate, diag_inverse, coupling, lift_table, upstream):
    old = old_iterate.reshape(CELLS, VECS, ROWS)
    rhs = rhs_vectors.reshape(CELLS, VECS, ROWS)
    diag = diag_inverse.reshape(CELLS, ROWS, ROWS)
    blocks = coupling.reshape(CELLS, TRACE, 6 * TRACE)
    lift = lift_table.T
    traces, inner, outer, across, faces = call(
        open_kernel, SIDE_OUTS + [((CELLS, 2 * VECS, LANES), F32)], micros=2
    )(old)
    ups, down, below = call(position_kernel, [ROW_TILE, DOWN, BELOW])(upstream.transpose(1, 2, 0), faces)
    halos = (from_next(below),) + exchange_sides(outer, inner, across)
    lifted_rows, passing, composed = call(
        transfer_kernel,
        [((CELLS, DEEP, ROWS), BF16), ((CELLS, DEEP, LANES), BF16), ((PATCH, TRACE, LANES), F32)],
        [pltpu.VMEM((CELLS, DEEP, LANES), BF16), pltpu.VMEM((PATCH, TRACE, LANES), F32)],
    )(ups, diag, blocks, lift)
    solved, sources, single = call(source_kernel, [FIELD, ((CELLS, VECS, LANES), F32), PACKED], FLUXES)(
        ups, rhs, traces, down, *halos, diag, blocks, lift, passing, composed
    )
    partner = swapped(single, 1)
    weights, front = call(weight_kernel, [((CELLS, DEEP, ROWS), BF16), ((PATCH, TRACE, LANES), F32)])(
        blocks, lifted_rows, single
    )
    (pair,) = call(pair_kernel, [PACKED])(single, partner)
    partner_pair = swapped(pair, 2)
    (leaving,) = call(leaving_kernel, [STATES])(pair, partner_pair)
    second = passed(leaving, 0, 1, 2)
    (group,) = call(group_kernel, [PACKED])(pair, partner_pair, leaving)
    before = passed(group, 2, 3, 2)
    (leaving,) = call(onward_kernel, [STATES])(second, group)
    third = passed(leaving, 1, 2, 2)
    fourth = passed(leaving, 1, 3, 0)
    (ahead,) = call(ahead_kernel, [PACKED])(ups, front, solved, below, leaving)
    ahead = from_next(ahead)
    prefixes, ends = call(prefix_kernel, [((PATCH, MAP_ROWS, LANES), F32), ((8, LANES), F32)])(
        partner, partner_pair
    )
    new, traces, inner, outer, across, down, leaving = call(
        finish_kernel,
        [FIELD] + SIDE_OUTS + [DOWN, ((PATCH, VECS, LANES), F32)],
        [pltpu.VMEM((CELLS, VECS, ROWS), F32), pltpu.SemaphoreType.DMA((1,))],
        far_outs=(0,),
    )(ups, second, third, fourth, before, prefixes, ends, old, solved, sources, weights, passing)
    halos = exchange_sides(outer, inner, across)
    (near,) = call(near_residual_kernel, [FIELD], FLUXES)(traces, down, leaving, ahead, blocks, lift)
    (residual,) = call(residual_kernel, [FIELD], FLUXES)(near, *halos, blocks, lift)
    shape = rhs_vectors.shape
    return new.reshape(shape), residual.reshape(shape)


def solution(mesh):
    field = P("sweep", "cx", "cy", None, None)
    return jax.shard_map(
        local,
        mesh=mesh,
        in_specs=(field, field, field, field, P(), P("sweep", "cx", "cy")),
        out_specs=(field, field),
        check_vma=False,
    )
```

```python
import jax
import jax.numpy as jnp
from jax import lax
from jax.experimental import pallas as pl
from jax.experimental.pallas import tpu as pltpu
from jax.sharding import PartitionSpec as P

NPOINT = 4
ROWS = 320
TRACE = 80
VECS = 16
LAYERS = 3
EX = 2
EY = 2
PATCH = EX * EY
CELLS = LAYERS * PATCH
LANES = 128
DEEP = 2 * LANES
GROUP = 4
NODES = NPOINT**3
MAP_ROWS = TRACE + VECS
BF16 = jnp.bfloat16
F32 = jnp.float32

FACE_ROWS = ((0, 16, 4), (3, 16, 4), (0, 4, 1), (48, 4, 1), (0, 16, 1), (12, 16, 1))
SLOT_FACES = (0, 3, 2, 5, 4)


def split(x):
    high = x.astype(BF16)
    low = (x - high.astype(F32)).astype(BF16)
    return high, low


def stacked(x):
    return jnp.concatenate(split(x), axis=0)


def dot(a, b):
    return jnp.dot(a, b, preferred_element_type=F32)


def dot_rows(a, b):
    return lax.dot_general(a, b, (((1,), (1,)), ((), ())), preferred_element_type=F32)


def halves(x):
    rows = x.shape[0] // 2
    return x[:rows] + x[rows:]


def deep_rows(table):
    high, low = split(table)
    gap = jnp.zeros((LANES - TRACE, table.shape[1]), BF16)
    return jnp.concatenate([high, gap, low, gap], axis=0)


def deep_lhs(x):
    high, low = split(x)
    return jnp.concatenate(
        [jnp.concatenate([high, high], axis=1), jnp.concatenate([low, low], axis=1)], axis=0
    )


def times(x, deep):
    return halves(dot(deep_lhs(x), deep))


def lane_take(x, index):
    return jnp.take_along_axis(x, index, axis=1)


def lane_ids(rows):
    return lax.broadcasted_iota(jnp.int32, (rows, LANES), 1)


def blocks_of(x):
    rest = ROWS - 2 * LANES
    tail = jnp.concatenate([x[:, 2 * LANES :], jnp.zeros((x.shape[0], LANES - rest), x.dtype)], axis=1)
    return x[:, :LANES], x[:, LANES : 2 * LANES], tail


def face_of(blocks, face):
    start, a_step, b_step = FACE_ROWS[face]
    lane = lane_ids(blocks[0].shape[0])
    entry = lane & 15
    index = (lane >> 4 & 1) * NODES + start + (entry >> 2) * a_step + (entry & 3) * b_step
    first, second, third = [lane_take(block, index) for block in blocks]
    third = jnp.where(lane < TRACE, third, 0.0)
    return jnp.where(lane < 32, first, jnp.where(lane < 64, second, third))


def side_table():
    row = lax.broadcasted_iota(jnp.int32, (ROWS, LANES), 0)
    lane = lane_ids(1)
    blocks = []
    for face in SLOT_FACES:
        start, a_step, b_step = FACE_ROWS[face]
        source = (lane >> 4) * NODES + start + (lane >> 2 & 3) * a_step + (lane & 3) * b_step
        source = jnp.where(lane < TRACE, source, -1)
        blocks.append(jnp.where(row == source, 1.0, 0.0).astype(BF16))
    return jnp.concatenate(blocks, axis=1)


def rows_of(ends):
    return [ends[at : at + 1] for at in range(PATCH)]


def ends_of(rows):
    return jnp.concatenate(list(rows) + [jnp.zeros((8 - PATCH, LANES), F32)], axis=0)


def chosen(items, at):
    out = items[0]
    for number in range(1, PATCH):
        out = jnp.where(at == number, items[number], out)
    return out


def placed(states, ends):
    out = []
    for position in range(PATCH):
        total = jnp.where(ends[0] == position, states[0], 0.0)
        for at in range(1, PATCH):
            total = total + jnp.where(ends[at] == position, states[at], 0.0)
        out.append(total)
    return out


def ups_of(ups):
    return [[ups[layer * PATCH + e : layer * PATCH + e + 1] for e in range(PATCH)] for layer in range(LAYERS)]


def position_rows(links):
    found = []
    lane = lax.broadcasted_iota(jnp.int32, (EY, LAYERS), 1)
    for layer in range(LAYERS):
        for a in range(EX):
            value = jnp.sum(jnp.where(lane == layer, links[a], 0).astype(F32), axis=1, keepdims=True)
            found.append(jnp.broadcast_to(value, (EY, LANES)))
    return jnp.concatenate(found + [jnp.zeros((16 - CELLS, LANES), F32)], axis=0)


def put_sides(cells, traces, inner, outer, across):
    core = lax.axis_index("cy")
    even = lax.rem(lax.axis_index("cx"), 2) == 0
    picked = dot(jnp.concatenate([stacked(x) for x in cells], axis=0), side_table())
    pieces = [picked[2 * VECS * at : 2 * VECS * (at + 1)] for at in range(CELLS)]
    whole = [halves(piece[:, LANES:]) for piece in pieces]
    for layer in range(LAYERS):
        block = lambda e, s: whole[layer * PATCH + e][:, (s - 1) * LANES : s * LANES]
        for e in range(PATCH):
            traces[layer * PATCH + e] = pieces[layer * PATCH + e][:, LANES:].astype(BF16)
        for b in range(EY):
            east, west = block(EY + b, 1), block(b, 2)
            inner[layer * EY + b] = jnp.where(even, east, west)
            outer[layer * EY + b] = jnp.where(even, west, east)
        for a in range(EX):
            across[layer * EX + a] = jnp.where(core == 0, block(a * EY + 1, 3), block(a * EY, 4))
    return [piece[:, :LANES] for piece in pieces]


def put_below(pieces, ups, below):
    for e, state in enumerate(placed([halves(pieces[e]) for e in range(PATCH)], ups[0])):
        below[e] = state
    for e in range(PATCH, LAYERS * EY):
        below[e] = jnp.zeros((VECS, LANES), F32)


def put_down(pieces, ups, down):
    for layer in range(1, LAYERS):
        for e, piece in enumerate(placed(pieces[layer * PATCH : (layer + 1) * PATCH], ups[layer])):
            down[(layer - 1) * PATCH + e] = piece.astype(BF16)


def open_kernel(old, traces, inner, outer, across, faces):
    for at, piece in enumerate(put_sides([old[at] for at in range(CELLS)], traces, inner, outer, across)):
        faces[at] = piece


def position_kernel(links, faces, ups, down, below):
    rows = position_rows(links)
    ups[...] = rows
    pieces = [faces[at] for at in range(CELLS)]
    put_below(pieces, ups_of(rows), below)
    put_down(pieces, ups_of(rows), down)


def near_slots(layer, e, traces, down):
    a, b = e // EY, e % EY
    own = lambda cell, s: traces[layer * PATCH + cell, :, (s - 1) * LANES : s * LANES]
    slots = {}
    if layer < LAYERS - 1:
        slots[1] = down[layer * PATCH + e]
    slots[2 if a == 1 else 3] = own(b, 1) if a == 1 else own(EY + b, 2)
    slots[4 if b == 1 else 5] = own(a * EY, 3) if b == 1 else own(a * EY + 1, 4)
    return slots


def far_slots(layer, e, from_above, outer, inner, from_across):
    core = lax.axis_index("cy")
    even = lax.rem(lax.axis_index("cx"), 2) == 0
    a, b = e // EY, e % EY
    close, wide = inner[layer * EY + b], outer[layer * EY + b]
    other = from_across[layer * EX + a]
    slots = {}
    if layer == LAYERS - 1 and from_above is not None:
        slots[1] = stacked(from_above[e])
    slots[2 if a == 0 else 3] = stacked(jnp.where(even, wide, close) if a == 0 else jnp.where(even, close, wide))
    slots[4 if b == 0 else 5] = stacked(jnp.where(core == (1 if b == 0 else 0), other, 0.0))
    return slots


def lift_all(stacks, coupling, lift, left, right):
    lane = lax.broadcasted_iota(jnp.int32, (2 * VECS, DEEP), 1)
    r = 2 * VECS
    for at, slots in enumerate(stacks):
        for begin, numbers, kept_rows in ((0, (1, 2, 3), left), (DEEP, (3, 4, 5), right)):
            present = [slot for slot in numbers if slot in slots]
            y = dot(
                jnp.concatenate([slots[slot] for slot in present], axis=0)[:, :TRACE],
                coupling[at, :, begin : min(begin + DEEP, 6 * TRACE)],
            )
            place = lane[:, : y.shape[1]] + begin
            kept = jnp.zeros((r, y.shape[1]), F32)
            for i, slot in enumerate(present):
                inside = (place >= slot * TRACE) & (place < (slot + 1) * TRACE)
                kept = jnp.where(inside, y[r * i : r * (i + 1)], kept)
            kept_rows[r * at : r * (at + 1)] = stacked(halves(kept))
    out = dot_rows(left[...], lift[:, :DEEP]) + dot_rows(right[...], lift[:, DEEP:])
    return [halves(out[r * at : r * (at + 1)]) for at in range(CELLS)]


def transfer_kernel(ups, diag, coupling, lift, lifted_rows, passing, composed, outflows, first):
    ups = ups_of(ups)
    one = lax.broadcasted_iota(jnp.int32, (TRACE, TRACE), 0)
    two = lax.broadcasted_iota(jnp.int32, (TRACE, TRACE), 1)
    inflow = dot_rows((one == two).astype(F32).astype(BF16), lift[:, :TRACE]).astype(BF16)
    upper, lower = inflow[:NODES, :DEEP], inflow[NODES:, DEEP:]
    for at in range(CELLS):
        lifts = jnp.concatenate([dot(upper, diag[at, :DEEP]), dot(lower, diag[at, DEEP:])], axis=0)
        lifted_rows[at] = deep_rows(lifts)
        outflows[at] = deep_rows(face_of(blocks_of(lifts), 1))
    for at in range(CELLS):
        upwind = coupling[at, :, :LANES]
        passed_on = dot(jnp.concatenate([upwind, upwind], axis=1), outflows[at])
        passing[at] = deep_rows(passed_on)
        if at < PATCH:
            first[at] = passed_on
    source = [first[e] for e in range(PATCH)]
    both = [times(chosen(source, ups[1][e]), passing[PATCH + e]) for e in range(PATCH)]
    for e in range(PATCH):
        composed[e] = -times(chosen(both, ups[2][e]), passing[2 * PATCH + e])


def weight_kernel(coupling, lifted_rows, unused, weights, front):
    for at in range(CELLS):
        upwind = coupling[at, :, :LANES]
        weight = dot(jnp.concatenate([upwind, upwind], axis=1), lifted_rows[at])
        weights[at] = deep_rows(weight)
        if at < PATCH:
            front[at] = face_of(blocks_of(weight), 0)


def turned(x, by):
    return pltpu.roll(x, by % LANES, 1)


def pack(maps, ends):
    lane = lane_ids(TRACE)
    square = [x[:TRACE] for x in maps]
    source = [x[TRACE:] for x in maps]
    all_sources = jnp.concatenate(source, axis=0)
    part = lane_ids(VECS) >> 4
    last = jnp.where(part == 5, turned(source[0], 16), jnp.where(part == 6, turned(source[1], 32), turned(source[2], 48)))
    one = jnp.where(lane < TRACE, square[0], turned(square[3], TRACE))
    rest = jnp.concatenate([turned(all_sources, 64), turned(source[3], 48)], axis=0)
    two = jnp.where(lane < TRACE, square[1], jnp.where(lane < 112, turned(square[3], 32), rest))
    three = jnp.where(lane < TRACE, square[2], jnp.concatenate([turned(all_sources, TRACE), last], axis=0))
    return jnp.concatenate([one, two, three, ends], axis=0)


def unpack(packed):
    lane = lane_ids(TRACE)
    one, two, three = [packed[TRACE * at : TRACE * (at + 1)] for at in range(3)]
    four = jnp.where(lane < 48, turned(one, 48), turned(two, 96))
    square = [jnp.where(lane < TRACE, x, 0.0) for x in (one, two, three, four)]
    lane = lane_ids(PATCH * VECS)
    most = jnp.where(lane < 48, turned(three[: PATCH * VECS], 48), turned(two[: PATCH * VECS], 64))
    ends = [turned(three[PATCH * VECS :], by) for by in (112, 96, 80)] + [turned(two[PATCH * VECS :], 80)]
    lane = lane_ids(VECS)
    maps = []
    for at in range(PATCH):
        source = jnp.where(lane < 64, most[VECS * at : VECS * (at + 1)], jnp.where(lane < TRACE, ends[at], 0.0))
        maps.append(jnp.concatenate([square[at], source], axis=0))
    return maps, packed[3 * TRACE : 3 * TRACE + 8]


def pack_states(states):
    lane = lane_ids(VECS)
    one = jnp.where(lane < TRACE, states[0], turned(states[3], TRACE))
    two = jnp.where(lane < TRACE, states[1], turned(states[3], 32))
    return jnp.concatenate([one, two, states[2]], axis=0)


def unpack_states(packed):
    lane = lane_ids(VECS)
    one, two, three = [packed[VECS * at : VECS * (at + 1)] for at in range(3)]
    four = jnp.where(lane < 48, turned(one, 48), turned(two, 96))
    return [jnp.where(lane < TRACE, x, 0.0) for x in (one, two, three, four)]


def after(first, second):
    nothing = jnp.zeros((TRACE, LANES), F32)
    added = jnp.concatenate([nothing, second[TRACE:]], axis=0) if first.shape[0] > VECS else second[TRACE:]
    return times(first, deep_rows(second[:TRACE])) + added


def source_kernel(
    ups, rhs, traces, down, from_above, outer, inner, from_across, diag, coupling, lift, passing, composed,
    solved, sources, packed, left, right,
):
    ups = ups_of(ups)
    stacks = [
        near_slots(layer, e, traces, down) | far_slots(layer, e, from_above, outer, inner, from_across)
        for layer in range(LAYERS)
        for e in range(PATCH)
    ]
    outflows = []
    for at, x in enumerate(lift_all(stacks, coupling, lift, left, right)):
        y = halves(dot(stacked(rhs[at] - x), diag[at]))
        solved[at] = y
        outflows.append(face_of(blocks_of(y), 1))
        sources[at] = outflows[at]
    current = outflows[:PATCH]
    for layer in range(1, LAYERS):
        current = [
            outflows[layer * PATCH + e] - times(chosen(current, ups[layer][e]), passing[layer * PATCH + e])
            for e in range(PATCH)
        ]
    starts = [chosen(ups[0], chosen(ups[1], ups[2][e])) for e in range(PATCH)]
    maps = placed([jnp.concatenate([composed[e], current[e]], axis=0) for e in range(PATCH)], starts)
    ends = placed([jnp.full((1, LANES), float(e), F32) for e in range(PATCH)], starts)
    packed[...] = pack(maps, ends_of(ends))


def ordered(mine, theirs, bit):
    later = (lax.axis_index("sweep") >> bit & 1) == 1
    first, first_ends = unpack(jnp.where(later, theirs, mine))
    second, second_ends = unpack(jnp.where(later, mine, theirs))
    return first, rows_of(first_ends), second, rows_of(second_ends)


def joined(mine, theirs, bit):
    first, first_ends, second, second_ends = ordered(mine, theirs, bit)
    maps = [after(first[at], chosen(second, first_ends[at])) for at in range(PATCH)]
    return pack(maps, ends_of([chosen(second_ends, at) for at in first_ends]))


def pair_kernel(mine, theirs, packed):
    packed[...] = joined(mine[...], theirs[...], 0)


def group_kernel(mine, theirs, unused, packed):
    packed[...] = joined(mine[...], theirs[...], 1)


def leaving_kernel(mine, theirs, leaving):
    first, first_ends, second, second_ends = ordered(mine[...], theirs[...], 1)
    states = [after(first[at][TRACE:], chosen(second, first_ends[at])) for at in range(PATCH)]
    leaving[...] = pack_states(placed(states, [chosen(second_ends, at) for at in first_ends]))


def prefix_kernel(pair, theirs, prefixes, ends):
    me = lax.axis_index("sweep")
    partner, partner_ends = unpack(pair[...])
    row = lax.broadcasted_iota(jnp.int32, (MAP_ROWS, LANES), 0)
    same = (row == lane_ids(MAP_ROWS)).astype(F32)
    later = (me & 1) == 1
    own = [jnp.where(later, x, same) for x in partner]
    own_ends = [jnp.where(later, x, float(at)) for at, x in enumerate(rows_of(partner_ends))]
    first, first_ends = unpack(theirs[...])
    first_ends = rows_of(first_ends)
    later = (me >> 1 & 1) == 1
    out = []
    for at in range(PATCH):
        whole = after(first[at], chosen(own, first_ends[at]))
        prefixes[at] = jnp.where(later, whole, own[at])
        out.append(jnp.where(later, chosen(own_ends, first_ends[at]), own_ends[at]))
    ends[...] = ends_of(out)


def onward_kernel(entering, packed, leaving):
    maps, ends = unpack(packed[...])
    states = unpack_states(entering[...])
    states = [after(states[at], maps[at]) for at in range(PATCH)]
    leaving[...] = pack_states(placed(states, rows_of(ends)))


def ahead_kernel(ups, front, solved, below, packed):
    maps = [
        jnp.concatenate([front[e], -face_of(blocks_of(solved[e]), 0)], axis=0) for e in range(PATCH)
    ]
    maps = placed(maps, ups_of(ups)[0])
    maps = [jnp.concatenate([x[:TRACE], x[TRACE:] + below[e]], axis=0) for e, x in enumerate(maps)]
    packed[...] = pack(maps, jnp.zeros((8, LANES), F32))


def finish_kernel(
    ups, second, third, fourth, before, prefixes, ends, old, solved, sources, weights, passing,
    new, traces, inner, outer, across, down, leaving, made, sems,
):
    maps, map_ends = unpack(before[...])
    second, fourth, third = [unpack_states(x[...]) for x in (second, fourth, third)]
    states = [after(fourth[at], maps[at]) for at in range(PATCH)]
    last = placed(states, rows_of(map_ends))
    entering = [second[at] + third[at] + last[at] for at in range(PATCH)]
    states = [after(entering[at], prefixes[at]) for at in range(PATCH)]
    current = placed(states, rows_of(ends))
    ups = ups_of(ups)
    changes = []
    for layer in range(LAYERS):
        inflow = [chosen(current, ups[layer][e]) for e in range(PATCH)]
        current = [
            sources[layer * PATCH + e] - times(inflow[e], passing[layer * PATCH + e]) for e in range(PATCH)
        ]
        for e in range(PATCH):
            at = layer * PATCH + e
            x = solved[at] - times(inflow[e], weights[at])
            made[at] = x
            changes.append(old[at] - x)
    copy = pltpu.make_async_copy(made, new, sems.at[0])
    copy.start()
    put_down(put_sides(changes, traces, inner, outer, across), ups, down)
    for e in range(PATCH):
        leaving[e] = current[e]
    copy.wait()


def near_residual_kernel(traces, down, leaving, ahead, coupling, lift, out, left, right):
    stacks = [near_slots(layer, e, traces, down) for layer in range(LAYERS) for e in range(PATCH)]
    maps, unused = unpack(ahead[...])
    for e in range(PATCH):
        stacks[(LAYERS - 1) * PATCH + e][1] = stacked(after(leaving[e], maps[e]))
    for at, x in enumerate(lift_all(stacks, coupling, lift, left, right)):
        out[at] = x


def residual_kernel(near, outer, inner, from_across, coupling, lift, out, left, right):
    stacks = [
        far_slots(layer, e, None, outer, inner, from_across) for layer in range(LAYERS) for e in range(PATCH)
    ]
    for at, x in enumerate(lift_all(stacks, coupling, lift, left, right)):
        out[at] = near[at] + x


VMEM = pl.BlockSpec(memory_space=pltpu.VMEM)
FAR = pl.BlockSpec(memory_space=pl.ANY)


def call(kernel, outs, scratch=(), far_outs=(), micros=1):
    def run(*args):
        return pl.pallas_call(
            kernel,
            in_specs=[VMEM] * len(args),
            out_specs=[FAR if i in far_outs else VMEM for i in range(len(outs))],
            out_shape=[jax.ShapeDtypeStruct(shape, kind) for shape, kind in outs],
            scratch_shapes=list(scratch),
            compiler_params=pltpu.CompilerParams(vmem_limit_bytes=16 * 1024 * 1024),
            cost_estimate=pl.CostEstimate(
                flops=micros * 1_000_000_000, bytes_accessed=micros * 3_600_000, transcendentals=0
            ),
        )(*args)

    return run


SIDE_OUTS = [
    ((CELLS, 2 * VECS, (len(SLOT_FACES) - 1) * LANES), BF16),
    ((LAYERS * EY, VECS, LANES), F32),
    ((LAYERS * EY, VECS, LANES), F32),
    ((LAYERS * EX, VECS, LANES), F32),
]
BELOW = ((LAYERS * EY, VECS, LANES), F32)
DOWN = (((LAYERS - 1) * PATCH, 2 * VECS, LANES), BF16)
ROW_TILE = ((16, LANES), F32)
FLUXES = [pltpu.VMEM((CELLS * 2 * VECS, DEEP), BF16), pltpu.VMEM((CELLS * 2 * VECS, 6 * TRACE - DEEP), BF16)]
FIELD = ((CELLS, VECS, ROWS), F32)
STATES = ((3 * VECS, LANES), F32)
PACKED = ((3 * TRACE + 8, LANES), F32)


def from_next(piece):
    return lax.ppermute(piece, "sweep", [(i + 1, i) for i in range(lax.axis_size("sweep") - 1)])


def exchange_sides(outer, inner, across):
    wide = lax.axis_size("cx")
    outer = lax.ppermute(outer, "cx", [(i, i + 1 if i % 2 else i - 1) for i in range(1, wide - 1)])
    inner = lax.ppermute(inner, "cx", [(i, i ^ 1) for i in range(wide)])
    across = lax.ppermute(across, "cy", [(0, 1), (1, 0)])
    return outer, inner, across


def swapped(packed, by):
    return lax.ppermute(packed, "sweep", [(i, i ^ by) for i in range(lax.axis_size("sweep"))])


def passed(states, source, target, shift):
    pairs = [(GROUP * source + p, GROUP * target + (p + shift) % GROUP) for p in range(GROUP)]
    return lax.ppermute(states, "sweep", pairs)


def local(rhs_vectors, old_iterate, diag_inverse, coupling, lift_table, upstream):
    old = old_iterate.reshape(CELLS, VECS, ROWS)
    rhs = rhs_vectors.reshape(CELLS, VECS, ROWS)
    diag = diag_inverse.reshape(CELLS, ROWS, ROWS)
    blocks = coupling.reshape(CELLS, TRACE, 6 * TRACE)
    lift = lift_table.T
    traces, inner, outer, across, faces = call(
        open_kernel, SIDE_OUTS + [((CELLS, 2 * VECS, LANES), F32)], micros=2
    )(old)
    ups, down, below = call(position_kernel, [ROW_TILE, DOWN, BELOW])(upstream.transpose(1, 2, 0), faces)
    halos = (from_next(below),) + exchange_sides(outer, inner, across)
    lifted_rows, passing, composed = call(
        transfer_kernel,
        [((CELLS, DEEP, ROWS), BF16), ((CELLS, DEEP, LANES), BF16), ((PATCH, TRACE, LANES), F32)],
        [pltpu.VMEM((CELLS, DEEP, LANES), BF16), pltpu.VMEM((PATCH, TRACE, LANES), F32)],
    )(ups, diag, blocks, lift)
    solved, sources, single = call(source_kernel, [FIELD, ((CELLS, VECS, LANES), F32), PACKED], FLUXES)(
        ups, rhs, traces, down, *halos, diag, blocks, lift, passing, composed
    )
    partner = swapped(single, 1)
    (pair,) = call(pair_kernel, [PACKED])(single, partner)
    partner_pair = swapped(pair, 2)
    weights, front = call(weight_kernel, [((CELLS, DEEP, ROWS), BF16), ((PATCH, TRACE, LANES), F32)])(
        blocks, lifted_rows, pair
    )
    (ahead,) = call(ahead_kernel, [PACKED])(ups, front, solved, below)
    ahead = from_next(ahead)
    (leaving,) = call(leaving_kernel, [STATES])(pair, partner_pair)
    second = passed(leaving, 0, 1, 2)
    (group,) = call(group_kernel, [PACKED])(pair, partner_pair, leaving)
    before = passed(group, 2, 3, 2)
    (leaving,) = call(onward_kernel, [STATES])(second, group)
    third = passed(leaving, 1, 2, 2)
    fourth = passed(leaving, 1, 3, 0)
    prefixes, ends = call(prefix_kernel, [((PATCH, MAP_ROWS, LANES), F32), ((8, LANES), F32)])(
        partner, partner_pair
    )
    new, traces, inner, outer, across, down, leaving = call(
        finish_kernel,
        [FIELD] + SIDE_OUTS + [DOWN, ((PATCH, VECS, LANES), F32)],
        [pltpu.VMEM((CELLS, VECS, ROWS), F32), pltpu.SemaphoreType.DMA((1,))],
        far_outs=(0,),
    )(ups, second, third, fourth, before, prefixes, ends, old, solved, sources, weights, passing)
    halos = exchange_sides(outer, inner, across)
    (near,) = call(near_residual_kernel, [FIELD], FLUXES)(traces, down, leaving, ahead, blocks, lift)
    (residual,) = call(residual_kernel, [FIELD], FLUXES)(near, *halos, blocks, lift)
    shape = rhs_vectors.shape
    return new.reshape(shape), residual.reshape(shape)


def solution(mesh):
    field = P("sweep", "cx", "cy", None, None)
    return jax.shard_map(
        local,
        mesh=mesh,
        in_specs=(field, field, field, field, P(), P("sweep", "cx", "cy")),
        out_specs=(field, field),
        check_vma=False,
    )
```

```python
import jax
import jax.numpy as jnp
from jax import lax
from jax.experimental import pallas as pl
from jax.experimental.pallas import tpu as pltpu
from jax.sharding import PartitionSpec as P

NPOINT = 4
ROWS = 320
TRACE = 80
VECS = 16
LAYERS = 3
EX = 2
EY = 2
PATCH = EX * EY
CELLS = LAYERS * PATCH
LANES = 128
DEEP = 2 * LANES
GROUP = 4
NODES = NPOINT**3
MAP_ROWS = TRACE + VECS
BF16 = jnp.bfloat16
F32 = jnp.float32

FACE_ROWS = ((0, 16, 4), (3, 16, 4), (0, 4, 1), (48, 4, 1), (0, 16, 1), (12, 16, 1))
SLOT_FACES = (0, 3, 2, 5, 4)


def split(x):
    high = x.astype(BF16)
    low = (x - high.astype(F32)).astype(BF16)
    return high, low


def stacked(x):
    return jnp.concatenate(split(x), axis=0)


def dot(a, b):
    return jnp.dot(a, b, preferred_element_type=F32)


def dot_rows(a, b):
    return lax.dot_general(a, b, (((1,), (1,)), ((), ())), preferred_element_type=F32)


def halves(x):
    rows = x.shape[0] // 2
    return x[:rows] + x[rows:]


def deep_rows(table):
    high, low = split(table)
    gap = jnp.zeros((LANES - TRACE, table.shape[1]), BF16)
    return jnp.concatenate([high, gap, low, gap], axis=0)


def deep_lhs(x):
    high, low = split(x)
    return jnp.concatenate(
        [jnp.concatenate([high, high], axis=1), jnp.concatenate([low, low], axis=1)], axis=0
    )


def times(x, deep):
    return halves(dot(deep_lhs(x), deep))


def lane_take(x, index):
    return jnp.take_along_axis(x, index, axis=1)


def lane_ids(rows):
    return lax.broadcasted_iota(jnp.int32, (rows, LANES), 1)


def blocks_of(x):
    rest = ROWS - 2 * LANES
    tail = jnp.concatenate([x[:, 2 * LANES :], jnp.zeros((x.shape[0], LANES - rest), x.dtype)], axis=1)
    return x[:, :LANES], x[:, LANES : 2 * LANES], tail


def face_of(blocks, face):
    start, a_step, b_step = FACE_ROWS[face]
    lane = lane_ids(blocks[0].shape[0])
    entry = lane & 15
    index = (lane >> 4 & 1) * NODES + start + (entry >> 2) * a_step + (entry & 3) * b_step
    first, second, third = [lane_take(block, index) for block in blocks]
    third = jnp.where(lane < TRACE, third, 0.0)
    return jnp.where(lane < 32, first, jnp.where(lane < 64, second, third))


def side_table():
    row = lax.broadcasted_iota(jnp.int32, (ROWS, LANES), 0)
    lane = lane_ids(1)
    blocks = []
    for face in SLOT_FACES:
        start, a_step, b_step = FACE_ROWS[face]
        source = (lane >> 4) * NODES + start + (lane >> 2 & 3) * a_step + (lane & 3) * b_step
        source = jnp.where(lane < TRACE, source, -1)
        blocks.append(jnp.where(row == source, 1.0, 0.0).astype(BF16))
    return jnp.concatenate(blocks, axis=1)


def rows_of(ends):
    return [ends[at : at + 1] for at in range(PATCH)]


def ends_of(rows):
    return jnp.concatenate(list(rows) + [jnp.zeros((8 - PATCH, LANES), F32)], axis=0)


def chosen(items, at):
    out = items[0]
    for number in range(1, PATCH):
        out = jnp.where(at == number, items[number], out)
    return out


def placed(states, ends):
    out = []
    for position in range(PATCH):
        total = jnp.where(ends[0] == position, states[0], 0.0)
        for at in range(1, PATCH):
            total = total + jnp.where(ends[at] == position, states[at], 0.0)
        out.append(total)
    return out


def ups_of(ups):
    return [[ups[layer * PATCH + e : layer * PATCH + e + 1] for e in range(PATCH)] for layer in range(LAYERS)]


def position_rows(links):
    found = []
    lane = lax.broadcasted_iota(jnp.int32, (EY, LAYERS), 1)
    for layer in range(LAYERS):
        for a in range(EX):
            value = jnp.sum(jnp.where(lane == layer, links[a], 0).astype(F32), axis=1, keepdims=True)
            found.append(jnp.broadcast_to(value, (EY, LANES)))
    return jnp.concatenate(found + [jnp.zeros((16 - CELLS, LANES), F32)], axis=0)


def put_sides(cells, traces, inner, outer, across):
    core = lax.axis_index("cy")
    even = lax.rem(lax.axis_index("cx"), 2) == 0
    picked = dot(jnp.concatenate([stacked(x) for x in cells], axis=0), side_table())
    pieces = [picked[2 * VECS * at : 2 * VECS * (at + 1)] for at in range(CELLS)]
    whole = [halves(piece[:, LANES:]) for piece in pieces]
    for layer in range(LAYERS):
        block = lambda e, s: whole[layer * PATCH + e][:, (s - 1) * LANES : s * LANES]
        for e in range(PATCH):
            traces[layer * PATCH + e] = pieces[layer * PATCH + e][:, LANES:].astype(BF16)
        for b in range(EY):
            east, west = block(EY + b, 1), block(b, 2)
            inner[layer * EY + b] = jnp.where(even, east, west)
            outer[layer * EY + b] = jnp.where(even, west, east)
        for a in range(EX):
            across[layer * EX + a] = jnp.where(core == 0, block(a * EY + 1, 3), block(a * EY, 4))
    return [piece[:, :LANES] for piece in pieces]


def put_below(pieces, ups, below):
    for e, state in enumerate(placed([halves(pieces[e]) for e in range(PATCH)], ups[0])):
        below[e] = state
    for e in range(PATCH, LAYERS * EY):
        below[e] = jnp.zeros((VECS, LANES), F32)


def put_down(pieces, ups, down):
    for layer in range(1, LAYERS):
        for e, piece in enumerate(placed(pieces[layer * PATCH : (layer + 1) * PATCH], ups[layer])):
            down[(layer - 1) * PATCH + e] = piece.astype(BF16)


def open_kernel(old, traces, inner, outer, across, faces):
    for at, piece in enumerate(put_sides([old[at] for at in range(CELLS)], traces, inner, outer, across)):
        faces[at] = piece


def position_kernel(links, faces, ups, down, below):
    rows = position_rows(links)
    ups[...] = rows
    pieces = [faces[at] for at in range(CELLS)]
    put_below(pieces, ups_of(rows), below)
    put_down(pieces, ups_of(rows), down)


def near_slots(layer, e, traces, down):
    a, b = e // EY, e % EY
    own = lambda cell, s: traces[layer * PATCH + cell, :, (s - 1) * LANES : s * LANES]
    slots = {}
    if layer < LAYERS - 1:
        slots[1] = down[layer * PATCH + e]
    slots[2 if a == 1 else 3] = own(b, 1) if a == 1 else own(EY + b, 2)
    slots[4 if b == 1 else 5] = own(a * EY, 3) if b == 1 else own(a * EY + 1, 4)
    return slots


def far_slots(layer, e, from_above, outer, inner, from_across):
    core = lax.axis_index("cy")
    even = lax.rem(lax.axis_index("cx"), 2) == 0
    a, b = e // EY, e % EY
    close, wide = inner[layer * EY + b], outer[layer * EY + b]
    other = from_across[layer * EX + a]
    slots = {}
    if layer == LAYERS - 1 and from_above is not None:
        slots[1] = stacked(from_above[e])
    slots[2 if a == 0 else 3] = stacked(jnp.where(even, wide, close) if a == 0 else jnp.where(even, close, wide))
    slots[4 if b == 0 else 5] = stacked(jnp.where(core == (1 if b == 0 else 0), other, 0.0))
    return slots


def lift_all(stacks, coupling, lift, left, right):
    lane = lax.broadcasted_iota(jnp.int32, (2 * VECS, DEEP), 1)
    r = 2 * VECS
    for at, slots in enumerate(stacks):
        for begin, numbers, kept_rows in ((0, (1, 2, 3), left), (DEEP, (3, 4, 5), right)):
            present = [slot for slot in numbers if slot in slots]
            y = dot(
                jnp.concatenate([slots[slot] for slot in present], axis=0)[:, :TRACE],
                coupling[at, :, begin : min(begin + DEEP, 6 * TRACE)],
            )
            place = lane[:, : y.shape[1]] + begin
            kept = jnp.zeros((r, y.shape[1]), F32)
            for i, slot in enumerate(present):
                inside = (place >= slot * TRACE) & (place < (slot + 1) * TRACE)
                kept = jnp.where(inside, y[r * i : r * (i + 1)], kept)
            kept_rows[r * at : r * (at + 1)] = stacked(halves(kept))
    out = dot_rows(left[...], lift[:, :DEEP]) + dot_rows(right[...], lift[:, DEEP:])
    return [halves(out[r * at : r * (at + 1)]) for at in range(CELLS)]


def transfer_kernel(ups, diag, coupling, lift, lifted_rows, passing, composed, outflows, first):
    ups = ups_of(ups)
    one = lax.broadcasted_iota(jnp.int32, (TRACE, TRACE), 0)
    two = lax.broadcasted_iota(jnp.int32, (TRACE, TRACE), 1)
    inflow = dot_rows((one == two).astype(F32).astype(BF16), lift[:, :TRACE]).astype(BF16)
    upper, lower = inflow[:NODES, :DEEP], inflow[NODES:, DEEP:]
    for at in range(CELLS):
        lifts = jnp.concatenate([dot(upper, diag[at, :DEEP]), dot(lower, diag[at, DEEP:])], axis=0)
        lifted_rows[at] = deep_rows(lifts)
        outflows[at] = deep_rows(face_of(blocks_of(lifts), 1))
    for at in range(CELLS):
        upwind = coupling[at, :, :LANES]
        passed_on = dot(jnp.concatenate([upwind, upwind], axis=1), outflows[at])
        passing[at] = deep_rows(passed_on)
        if at < PATCH:
            first[at] = passed_on
    source = [first[e] for e in range(PATCH)]
    both = [times(chosen(source, ups[1][e]), passing[PATCH + e]) for e in range(PATCH)]
    for e in range(PATCH):
        composed[e] = -times(chosen(both, ups[2][e]), passing[2 * PATCH + e])


def weight_kernel(coupling, lifted_rows, unused, weights, front):
    for at in range(CELLS):
        upwind = coupling[at, :, :LANES]
        weight = dot(jnp.concatenate([upwind, upwind], axis=1), lifted_rows[at])
        weights[at] = deep_rows(weight)
        if at < PATCH:
            front[at] = face_of(blocks_of(weight), 0)


def turned(x, by):
    return pltpu.roll(x, by % LANES, 1)


def pack(maps, ends):
    lane = lane_ids(TRACE)
    square = [x[:TRACE] for x in maps]
    source = [x[TRACE:] for x in maps]
    all_sources = jnp.concatenate(source, axis=0)
    part = lane_ids(VECS) >> 4
    last = jnp.where(part == 5, turned(source[0], 16), jnp.where(part == 6, turned(source[1], 32), turned(source[2], 48)))
    one = jnp.where(lane < TRACE, square[0], turned(square[3], TRACE))
    rest = jnp.concatenate([turned(all_sources, 64), turned(source[3], 48)], axis=0)
    two = jnp.where(lane < TRACE, square[1], jnp.where(lane < 112, turned(square[3], 32), rest))
    three = jnp.where(lane < TRACE, square[2], jnp.concatenate([turned(all_sources, TRACE), last], axis=0))
    return jnp.concatenate([one, two, three, ends], axis=0)


def unpack(packed):
    lane = lane_ids(TRACE)
    one, two, three = [packed[TRACE * at : TRACE * (at + 1)] for at in range(3)]
    four = jnp.where(lane < 48, turned(one, 48), turned(two, 96))
    square = [jnp.where(lane < TRACE, x, 0.0) for x in (one, two, three, four)]
    lane = lane_ids(PATCH * VECS)
    most = jnp.where(lane < 48, turned(three[: PATCH * VECS], 48), turned(two[: PATCH * VECS], 64))
    ends = [turned(three[PATCH * VECS :], by) for by in (112, 96, 80)] + [turned(two[PATCH * VECS :], 80)]
    lane = lane_ids(VECS)
    maps = []
    for at in range(PATCH):
        source = jnp.where(lane < 64, most[VECS * at : VECS * (at + 1)], jnp.where(lane < TRACE, ends[at], 0.0))
        maps.append(jnp.concatenate([square[at], source], axis=0))
    return maps, packed[3 * TRACE : 3 * TRACE + 8]


def pack_states(states):
    lane = lane_ids(VECS)
    one = jnp.where(lane < TRACE, states[0], turned(states[3], TRACE))
    two = jnp.where(lane < TRACE, states[1], turned(states[3], 32))
    return jnp.concatenate([one, two, states[2]], axis=0)


def unpack_states(packed):
    lane = lane_ids(VECS)
    one, two, three = [packed[VECS * at : VECS * (at + 1)] for at in range(3)]
    four = jnp.where(lane < 48, turned(one, 48), turned(two, 96))
    return [jnp.where(lane < TRACE, x, 0.0) for x in (one, two, three, four)]


def after(first, second):
    nothing = jnp.zeros((TRACE, LANES), F32)
    added = jnp.concatenate([nothing, second[TRACE:]], axis=0) if first.shape[0] > VECS else second[TRACE:]
    return times(first, deep_rows(second[:TRACE])) + added


def source_kernel(
    ups, rhs, traces, down, from_above, outer, inner, from_across, diag, coupling, lift, passing, composed,
    solved, sources, packed, left, right,
):
    ups = ups_of(ups)
    stacks = [
        near_slots(layer, e, traces, down) | far_slots(layer, e, from_above, outer, inner, from_across)
        for layer in range(LAYERS)
        for e in range(PATCH)
    ]
    outflows = []
    for at, x in enumerate(lift_all(stacks, coupling, lift, left, right)):
        y = halves(dot(stacked(rhs[at] - x), diag[at]))
        solved[at] = y
        outflows.append(face_of(blocks_of(y), 1))
        sources[at] = outflows[at]
    current = outflows[:PATCH]
    for layer in range(1, LAYERS):
        current = [
            outflows[layer * PATCH + e] - times(chosen(current, ups[layer][e]), passing[layer * PATCH + e])
            for e in range(PATCH)
        ]
    starts = [chosen(ups[0], chosen(ups[1], ups[2][e])) for e in range(PATCH)]
    maps = placed([jnp.concatenate([composed[e], current[e]], axis=0) for e in range(PATCH)], starts)
    ends = placed([jnp.full((1, LANES), float(e), F32) for e in range(PATCH)], starts)
    packed[...] = pack(maps, ends_of(ends))


def ordered(mine, theirs, bit):
    later = (lax.axis_index("sweep") >> bit & 1) == 1
    first, first_ends = unpack(jnp.where(later, theirs, mine))
    second, second_ends = unpack(jnp.where(later, mine, theirs))
    return first, rows_of(first_ends), second, rows_of(second_ends)


def joined(mine, theirs, bit):
    first, first_ends, second, second_ends = ordered(mine, theirs, bit)
    maps = [after(first[at], chosen(second, first_ends[at])) for at in range(PATCH)]
    return pack(maps, ends_of([chosen(second_ends, at) for at in first_ends]))


def pair_kernel(mine, theirs, packed):
    packed[...] = joined(mine[...], theirs[...], 0)


def group_kernel(mine, theirs, unused, packed):
    packed[...] = joined(mine[...], theirs[...], 1)


def leaving_kernel(mine, theirs, leaving):
    first, first_ends, second, second_ends = ordered(mine[...], theirs[...], 1)
    states = [after(first[at][TRACE:], chosen(second, first_ends[at])) for at in range(PATCH)]
    leaving[...] = pack_states(placed(states, [chosen(second_ends, at) for at in first_ends]))


def entry_kernel(
    pair, theirs, ups, passing, sources, weights, solved, tables, base, out_tables, out_added, starts
):
    me = lax.axis_index("sweep")
    partner, partner_ends = unpack(pair[...])
    row = lax.broadcasted_iota(jnp.int32, (MAP_ROWS, LANES), 0)
    same = (row == lane_ids(MAP_ROWS)).astype(F32)
    later = (me & 1) == 1
    own = [jnp.where(later, x, same) for x in partner]
    own_ends = [jnp.where(later, x, float(at)) for at, x in enumerate(rows_of(partner_ends))]
    first, first_ends = unpack(theirs[...])
    first_ends = rows_of(first_ends)
    later = (me >> 1 & 1) == 1
    maps, ends = [], []
    for at in range(PATCH):
        whole = after(first[at], chosen(own, first_ends[at]))
        maps.append(jnp.where(later, whole, own[at]))
        ends.append(jnp.where(later, chosen(own_ends, first_ends[at]), own_ends[at]))
    maps = placed(maps, ends)
    begin = placed([jnp.full((1, LANES), float(at), F32) for at in range(PATCH)], ends)
    ups = ups_of(ups)
    found, every = [], []
    nothing = jnp.zeros((TRACE, LANES), F32)
    for layer in range(LAYERS):
        begin = [chosen(begin, ups[layer][e]) for e in range(PATCH)]
        maps = [chosen(maps, ups[layer][e]) for e in range(PATCH)]
        found += begin
        every += maps
        maps = [
            jnp.concatenate([nothing, sources[layer * PATCH + e]], axis=0)
            - times(maps[e], passing[layer * PATCH + e])
            for e in range(PATCH)
        ]
    for e in range(PATCH):
        out_tables[e] = deep_rows(maps[e][:TRACE])
        out_added[e] = maps[e][TRACE:]
    for at in range(CELLS):
        product = times(every[at], weights[at])
        tables[at] = deep_rows(product[:TRACE])
        base[at] = solved[at] - product[TRACE:]
    starts[...] = jnp.concatenate(found + [jnp.zeros((16 - CELLS, LANES), F32)], axis=0)


def onward_kernel(entering, packed, leaving):
    maps, ends = unpack(packed[...])
    states = unpack_states(entering[...])
    states = [after(states[at], maps[at]) for at in range(PATCH)]
    leaving[...] = pack_states(placed(states, rows_of(ends)))


def ahead_kernel(ups, front, solved, below, packed):
    maps = [
        jnp.concatenate([front[e], -face_of(blocks_of(solved[e]), 0)], axis=0) for e in range(PATCH)
    ]
    maps = placed(maps, ups_of(ups)[0])
    maps = [jnp.concatenate([x[:TRACE], x[TRACE:] + below[e]], axis=0) for e, x in enumerate(maps)]
    packed[...] = pack(maps, jnp.zeros((8, LANES), F32))


def finish_kernel(
    ups, second, third, fourth, before, tables, base, out_tables, out_added, starts, old,
    new, traces, inner, outer, across, down, leaving, made, sems,
):
    maps, map_ends = unpack(before[...])
    second, fourth, third = [unpack_states(x[...]) for x in (second, fourth, third)]
    states = [after(fourth[at], maps[at]) for at in range(PATCH)]
    last = placed(states, rows_of(map_ends))
    entering = [second[at] + third[at] + last[at] for at in range(PATCH)]
    inflows = [deep_lhs(chosen(entering, starts[at : at + 1])) for at in range(CELLS)]
    products = [halves(dot(inflows[at], tables[at])) for at in range(CELLS)]
    found = [base[at] - products[at] for at in range(CELLS)]
    for at in range(CELLS):
        made[at] = found[at]
    copy = pltpu.make_async_copy(made, new, sems.at[0])
    copy.start()
    changes = [old[at] - found[at] for at in range(CELLS)]
    put_down(put_sides(changes, traces, inner, outer, across), ups_of(ups), down)
    for e in range(PATCH):
        leaving[e] = halves(dot(inflows[(LAYERS - 1) * PATCH + e], out_tables[e])) + out_added[e]
    copy.wait()


def near_residual_kernel(traces, down, leaving, ahead, coupling, lift, out, left, right):
    stacks = [near_slots(layer, e, traces, down) for layer in range(LAYERS) for e in range(PATCH)]
    maps, unused = unpack(ahead[...])
    for e in range(PATCH):
        stacks[(LAYERS - 1) * PATCH + e][1] = stacked(after(leaving[e], maps[e]))
    for at, x in enumerate(lift_all(stacks, coupling, lift, left, right)):
        out[at] = x


def residual_kernel(near, outer, inner, from_across, coupling, lift, out, left, right):
    stacks = [
        far_slots(layer, e, None, outer, inner, from_across) for layer in range(LAYERS) for e in range(PATCH)
    ]
    for at, x in enumerate(lift_all(stacks, coupling, lift, left, right)):
        out[at] = near[at] + x


VMEM = pl.BlockSpec(memory_space=pltpu.VMEM)
FAR = pl.BlockSpec(memory_space=pl.ANY)


def call(kernel, outs, scratch=(), far_outs=(), micros=1):
    def run(*args):
        return pl.pallas_call(
            kernel,
            in_specs=[VMEM] * len(args),
            out_specs=[FAR if i in far_outs else VMEM for i in range(len(outs))],
            out_shape=[jax.ShapeDtypeStruct(shape, kind) for shape, kind in outs],
            scratch_shapes=list(scratch),
            compiler_params=pltpu.CompilerParams(vmem_limit_bytes=16 * 1024 * 1024),
            cost_estimate=pl.CostEstimate(
                flops=micros * 1_000_000_000, bytes_accessed=micros * 3_600_000, transcendentals=0
            ),
        )(*args)

    return run


SIDE_OUTS = [
    ((CELLS, 2 * VECS, (len(SLOT_FACES) - 1) * LANES), BF16),
    ((LAYERS * EY, VECS, LANES), F32),
    ((LAYERS * EY, VECS, LANES), F32),
    ((LAYERS * EX, VECS, LANES), F32),
]
BELOW = ((LAYERS * EY, VECS, LANES), F32)
DOWN = (((LAYERS - 1) * PATCH, 2 * VECS, LANES), BF16)
ROW_TILE = ((16, LANES), F32)
FLUXES = [pltpu.VMEM((CELLS * 2 * VECS, DEEP), BF16), pltpu.VMEM((CELLS * 2 * VECS, 6 * TRACE - DEEP), BF16)]
FIELD = ((CELLS, VECS, ROWS), F32)
STATES = ((3 * VECS, LANES), F32)
PACKED = ((3 * TRACE + 8, LANES), F32)


def from_next(piece):
    return lax.ppermute(piece, "sweep", [(i + 1, i) for i in range(lax.axis_size("sweep") - 1)])


def exchange_sides(outer, inner, across):
    wide = lax.axis_size("cx")
    outer = lax.ppermute(outer, "cx", [(i, i + 1 if i % 2 else i - 1) for i in range(1, wide - 1)])
    inner = lax.ppermute(inner, "cx", [(i, i ^ 1) for i in range(wide)])
    across = lax.ppermute(across, "cy", [(0, 1), (1, 0)])
    return outer, inner, across


def swapped(packed, by):
    return lax.ppermute(packed, "sweep", [(i, i ^ by) for i in range(lax.axis_size("sweep"))])


def passed(states, source, target, shift):
    pairs = [(GROUP * source + p, GROUP * target + (p + shift) % GROUP) for p in range(GROUP)]
    return lax.ppermute(states, "sweep", pairs)


def local(rhs_vectors, old_iterate, diag_inverse, coupling, lift_table, upstream):
    old = old_iterate.reshape(CELLS, VECS, ROWS)
    rhs = rhs_vectors.reshape(CELLS, VECS, ROWS)
    diag = diag_inverse.reshape(CELLS, ROWS, ROWS)
    blocks = coupling.reshape(CELLS, TRACE, 6 * TRACE)
    lift = lift_table.T
    traces, inner, outer, across, faces = call(
        open_kernel, SIDE_OUTS + [((CELLS, 2 * VECS, LANES), F32)], micros=2
    )(old)
    ups, down, below = call(position_kernel, [ROW_TILE, DOWN, BELOW])(upstream.transpose(1, 2, 0), faces)
    halos = (from_next(below),) + exchange_sides(outer, inner, across)
    lifted_rows, passing, composed = call(
        transfer_kernel,
        [((CELLS, DEEP, ROWS), BF16), ((CELLS, DEEP, LANES), BF16), ((PATCH, TRACE, LANES), F32)],
        [pltpu.VMEM((CELLS, DEEP, LANES), BF16), pltpu.VMEM((PATCH, TRACE, LANES), F32)],
    )(ups, diag, blocks, lift)
    solved, sources, single = call(source_kernel, [FIELD, ((CELLS, VECS, LANES), F32), PACKED], FLUXES)(
        ups, rhs, traces, down, *halos, diag, blocks, lift, passing, composed
    )
    partner = swapped(single, 1)
    (pair,) = call(pair_kernel, [PACKED])(single, partner)
    partner_pair = swapped(pair, 2)
    weights, front = call(weight_kernel, [((CELLS, DEEP, ROWS), BF16), ((PATCH, TRACE, LANES), F32)])(
        blocks, lifted_rows, pair
    )
    (ahead,) = call(ahead_kernel, [PACKED])(ups, front, solved, below)
    ahead = from_next(ahead)
    (leaving,) = call(leaving_kernel, [STATES])(pair, partner_pair)
    second = passed(leaving, 0, 1, 2)
    (group,) = call(group_kernel, [PACKED])(pair, partner_pair, leaving)
    before = passed(group, 2, 3, 2)
    (leaving,) = call(onward_kernel, [STATES])(second, group)
    third = passed(leaving, 1, 2, 2)
    fourth = passed(leaving, 1, 3, 0)
    maps = call(
        entry_kernel,
        [
            ((CELLS, DEEP, ROWS), BF16),
            FIELD,
            ((PATCH, DEEP, LANES), BF16),
            ((PATCH, VECS, LANES), F32),
            ROW_TILE,
        ],
    )(partner, partner_pair, ups, passing, sources, weights, solved)
    new, traces, inner, outer, across, down, leaving = call(
        finish_kernel,
        [FIELD] + SIDE_OUTS + [DOWN, ((PATCH, VECS, LANES), F32)],
        [pltpu.VMEM((CELLS, VECS, ROWS), F32), pltpu.SemaphoreType.DMA((1,))],
        far_outs=(0,),
    )(ups, second, third, fourth, before, *maps, old)
    halos = exchange_sides(outer, inner, across)
    (near,) = call(near_residual_kernel, [FIELD], FLUXES)(traces, down, leaving, ahead, blocks, lift)
    (residual,) = call(residual_kernel, [FIELD], FLUXES)(near, *halos, blocks, lift)
    shape = rhs_vectors.shape
    return new.reshape(shape), residual.reshape(shape)


def solution(mesh):
    field = P("sweep", "cx", "cy", None, None)
    return jax.shard_map(
        local,
        mesh=mesh,
        in_specs=(field, field, field, field, P(), P("sweep", "cx", "cy")),
        out_specs=(field, field),
        check_vma=False,
    )
```

```python
import jax
import jax.numpy as jnp
from jax import lax
from jax.experimental import pallas as pl
from jax.experimental.pallas import tpu as pltpu
from jax.sharding import PartitionSpec as P

NPOINT = 4
ROWS = 320
TRACE = 80
VECS = 16
LAYERS = 3
EX = 2
EY = 2
PATCH = EX * EY
CELLS = LAYERS * PATCH
LANES = 128
DEEP = 2 * LANES
GROUP = 4
NODES = NPOINT**3
MAP_ROWS = TRACE + VECS
BF16 = jnp.bfloat16
F32 = jnp.float32

FACE_ROWS = ((0, 16, 4), (3, 16, 4), (0, 4, 1), (48, 4, 1), (0, 16, 1), (12, 16, 1))
SLOT_FACES = (0, 3, 2, 5, 4)


def split(x):
    high = x.astype(BF16)
    low = (x - high.astype(F32)).astype(BF16)
    return high, low


def stacked(x):
    return jnp.concatenate(split(x), axis=0)


def dot(a, b):
    return jnp.dot(a, b, preferred_element_type=F32)


def dot_rows(a, b):
    return lax.dot_general(a, b, (((1,), (1,)), ((), ())), preferred_element_type=F32)


def halves(x):
    rows = x.shape[0] // 2
    return x[:rows] + x[rows:]


def deep_rows(table):
    high, low = split(table)
    gap = jnp.zeros((LANES - TRACE, table.shape[1]), BF16)
    return jnp.concatenate([high, gap, low, gap], axis=0)


def deep_lhs(x):
    high, low = split(x)
    return jnp.concatenate(
        [jnp.concatenate([high, high], axis=1), jnp.concatenate([low, low], axis=1)], axis=0
    )


def times(x, deep):
    return halves(dot(deep_lhs(x), deep))


def times_all(items, deeps):
    operands = [deep_lhs(x) for x in items]
    products = [dot(x, deep) for x, deep in zip(operands, deeps)]
    return [halves(x) for x in products]


def lane_take(x, index):
    return jnp.take_along_axis(x, index, axis=1)


def lane_ids(rows):
    return lax.broadcasted_iota(jnp.int32, (rows, LANES), 1)


def blocks_of(x):
    rest = ROWS - 2 * LANES
    tail = jnp.concatenate([x[:, 2 * LANES :], jnp.zeros((x.shape[0], LANES - rest), x.dtype)], axis=1)
    return x[:, :LANES], x[:, LANES : 2 * LANES], tail


def face_of(blocks, face):
    start, a_step, b_step = FACE_ROWS[face]
    lane = lane_ids(blocks[0].shape[0])
    entry = lane & 15
    index = (lane >> 4 & 1) * NODES + start + (entry >> 2) * a_step + (entry & 3) * b_step
    first, second, third = [lane_take(block, index) for block in blocks]
    third = jnp.where(lane < TRACE, third, 0.0)
    return jnp.where(lane < 32, first, jnp.where(lane < 64, second, third))


def side_table():
    row = lax.broadcasted_iota(jnp.int32, (ROWS, LANES), 0)
    lane = lane_ids(1)
    blocks = []
    for face in SLOT_FACES:
        start, a_step, b_step = FACE_ROWS[face]
        source = (lane >> 4) * NODES + start + (lane >> 2 & 3) * a_step + (lane & 3) * b_step
        source = jnp.where(lane < TRACE, source, -1)
        blocks.append(jnp.where(row == source, 1.0, 0.0).astype(BF16))
    return jnp.concatenate(blocks, axis=1)


def rows_of(ends):
    return [ends[at : at + 1] for at in range(PATCH)]


def ends_of(rows):
    return jnp.concatenate(list(rows) + [jnp.zeros((8 - PATCH, LANES), F32)], axis=0)


def chosen(items, at):
    out = items[0]
    for number in range(1, PATCH):
        out = jnp.where(at == number, items[number], out)
    return out


def placed(states, ends):
    out = []
    for position in range(PATCH):
        total = jnp.where(ends[0] == position, states[0], 0.0)
        for at in range(1, PATCH):
            total = total + jnp.where(ends[at] == position, states[at], 0.0)
        out.append(total)
    return out


def ups_of(ups):
    return [[ups[layer * PATCH + e : layer * PATCH + e + 1] for e in range(PATCH)] for layer in range(LAYERS)]


def position_rows(links):
    found = []
    lane = lax.broadcasted_iota(jnp.int32, (EY, LAYERS), 1)
    for layer in range(LAYERS):
        for a in range(EX):
            value = jnp.sum(jnp.where(lane == layer, links[a], 0).astype(F32), axis=1, keepdims=True)
            found.append(jnp.broadcast_to(value, (EY, LANES)))
    return jnp.concatenate(found + [jnp.zeros((16 - CELLS, LANES), F32)], axis=0)


def put_sides(cells, traces, inner, outer, across):
    core = lax.axis_index("cy")
    even = lax.rem(lax.axis_index("cx"), 2) == 0
    picked = dot(jnp.concatenate([stacked(x) for x in cells], axis=0), side_table())
    pieces = [picked[2 * VECS * at : 2 * VECS * (at + 1)] for at in range(CELLS)]
    whole = [halves(piece[:, LANES:]) for piece in pieces]
    for layer in range(LAYERS):
        block = lambda e, s: whole[layer * PATCH + e][:, (s - 1) * LANES : s * LANES]
        for e in range(PATCH):
            traces[layer * PATCH + e] = pieces[layer * PATCH + e][:, LANES:].astype(BF16)
        for b in range(EY):
            east, west = block(EY + b, 1), block(b, 2)
            inner[layer * EY + b] = jnp.where(even, east, west)
            outer[layer * EY + b] = jnp.where(even, west, east)
        for a in range(EX):
            across[layer * EX + a] = jnp.where(core == 0, block(a * EY + 1, 3), block(a * EY, 4))
    return [piece[:, :LANES] for piece in pieces]


def put_below(pieces, ups, below):
    for e, state in enumerate(placed([halves(pieces[e]) for e in range(PATCH)], ups[0])):
        below[e] = state
    for e in range(PATCH, LAYERS * EY):
        below[e] = jnp.zeros((VECS, LANES), F32)


def put_down(pieces, ups, down):
    for layer in range(1, LAYERS):
        for e, piece in enumerate(placed(pieces[layer * PATCH : (layer + 1) * PATCH], ups[layer])):
            down[(layer - 1) * PATCH + e] = piece.astype(BF16)


def open_kernel(old, traces, inner, outer, across, faces):
    for at, piece in enumerate(put_sides([old[at] for at in range(CELLS)], traces, inner, outer, across)):
        faces[at] = piece


def position_kernel(links, faces, ups, down, below):
    rows = position_rows(links)
    ups[...] = rows
    pieces = [faces[at] for at in range(CELLS)]
    put_below(pieces, ups_of(rows), below)
    put_down(pieces, ups_of(rows), down)


def near_slots(layer, e, traces, down):
    a, b = e // EY, e % EY
    own = lambda cell, s: traces[layer * PATCH + cell, :, (s - 1) * LANES : s * LANES]
    slots = {}
    if layer < LAYERS - 1:
        slots[1] = down[layer * PATCH + e]
    slots[2 if a == 1 else 3] = own(b, 1) if a == 1 else own(EY + b, 2)
    slots[4 if b == 1 else 5] = own(a * EY, 3) if b == 1 else own(a * EY + 1, 4)
    return slots


def far_slots(layer, e, from_above, outer, inner, from_across):
    core = lax.axis_index("cy")
    even = lax.rem(lax.axis_index("cx"), 2) == 0
    a, b = e // EY, e % EY
    close, wide = inner[layer * EY + b], outer[layer * EY + b]
    other = from_across[layer * EX + a]
    slots = {}
    if layer == LAYERS - 1 and from_above is not None:
        slots[1] = stacked(from_above[e])
    slots[2 if a == 0 else 3] = stacked(jnp.where(even, wide, close) if a == 0 else jnp.where(even, close, wide))
    slots[4 if b == 0 else 5] = stacked(jnp.where(core == (1 if b == 0 else 0), other, 0.0))
    return slots


def lift_all(stacks, coupling, lift, left, right):
    lane = lax.broadcasted_iota(jnp.int32, (2 * VECS, DEEP), 1)
    r = 2 * VECS
    for at, slots in enumerate(stacks):
        for begin, numbers, kept_rows in ((0, (1, 2, 3), left), (DEEP, (3, 4, 5), right)):
            present = [slot for slot in numbers if slot in slots]
            y = dot(
                jnp.concatenate([slots[slot] for slot in present], axis=0)[:, :TRACE],
                coupling[at, :, begin : min(begin + DEEP, 6 * TRACE)],
            )
            place = lane[:, : y.shape[1]] + begin
            kept = jnp.zeros((r, y.shape[1]), F32)
            for i, slot in enumerate(present):
                inside = (place >= slot * TRACE) & (place < (slot + 1) * TRACE)
                kept = jnp.where(inside, y[r * i : r * (i + 1)], kept)
            kept_rows[r * at : r * (at + 1)] = stacked(halves(kept))
    out = dot_rows(left[...], lift[:, :DEEP]) + dot_rows(right[...], lift[:, DEEP:])
    return [halves(out[r * at : r * (at + 1)]) for at in range(CELLS)]


def transfer_kernel(ups, diag, coupling, lift, lifted_rows, passing, composed, outflows, first):
    ups = ups_of(ups)
    one = lax.broadcasted_iota(jnp.int32, (TRACE, TRACE), 0)
    two = lax.broadcasted_iota(jnp.int32, (TRACE, TRACE), 1)
    inflow = dot_rows((one == two).astype(F32).astype(BF16), lift[:, :TRACE]).astype(BF16)
    upper, lower = inflow[:NODES, :DEEP], inflow[NODES:, DEEP:]
    for at in range(CELLS):
        lifts = jnp.concatenate([dot(upper, diag[at, :DEEP]), dot(lower, diag[at, DEEP:])], axis=0)
        lifted_rows[at] = deep_rows(lifts)
        outflows[at] = deep_rows(face_of(blocks_of(lifts), 1))
    for at in range(CELLS):
        upwind = coupling[at, :, :LANES]
        passed_on = dot(jnp.concatenate([upwind, upwind], axis=1), outflows[at])
        passing[at] = deep_rows(passed_on)
        if at < PATCH:
            first[at] = passed_on
    source = [first[e] for e in range(PATCH)]
    both = times_all([chosen(source, at) for at in ups[1]], [passing[PATCH + e] for e in range(PATCH)])
    both = times_all([chosen(both, at) for at in ups[2]], [passing[2 * PATCH + e] for e in range(PATCH)])
    for e in range(PATCH):
        composed[e] = -both[e]


def weight_kernel(coupling, lifted_rows, unused, weights, front):
    for at in range(CELLS):
        upwind = coupling[at, :, :LANES]
        weight = dot(jnp.concatenate([upwind, upwind], axis=1), lifted_rows[at])
        weights[at] = deep_rows(weight)
        if at < PATCH:
            front[at] = face_of(blocks_of(weight), 0)


def turned(x, by):
    return pltpu.roll(x, by % LANES, 1)


def pack(maps, ends):
    lane = lane_ids(TRACE)
    square = [x[:TRACE] for x in maps]
    source = [x[TRACE:] for x in maps]
    all_sources = jnp.concatenate(source, axis=0)
    part = lane_ids(VECS) >> 4
    last = jnp.where(part == 5, turned(source[0], 16), jnp.where(part == 6, turned(source[1], 32), turned(source[2], 48)))
    one = jnp.where(lane < TRACE, square[0], turned(square[3], TRACE))
    rest = jnp.concatenate([turned(all_sources, 64), turned(source[3], 48)], axis=0)
    two = jnp.where(lane < TRACE, square[1], jnp.where(lane < 112, turned(square[3], 32), rest))
    three = jnp.where(lane < TRACE, square[2], jnp.concatenate([turned(all_sources, TRACE), last], axis=0))
    return jnp.concatenate([one, two, three, ends], axis=0)


def unpack(packed):
    lane = lane_ids(TRACE)
    one, two, three = [packed[TRACE * at : TRACE * (at + 1)] for at in range(3)]
    four = jnp.where(lane < 48, turned(one, 48), turned(two, 96))
    square = [jnp.where(lane < TRACE, x, 0.0) for x in (one, two, three, four)]
    lane = lane_ids(PATCH * VECS)
    most = jnp.where(lane < 48, turned(three[: PATCH * VECS], 48), turned(two[: PATCH * VECS], 64))
    ends = [turned(three[PATCH * VECS :], by) for by in (112, 96, 80)] + [turned(two[PATCH * VECS :], 80)]
    lane = lane_ids(VECS)
    maps = []
    for at in range(PATCH):
        source = jnp.where(lane < 64, most[VECS * at : VECS * (at + 1)], jnp.where(lane < TRACE, ends[at], 0.0))
        maps.append(jnp.concatenate([square[at], source], axis=0))
    return maps, packed[3 * TRACE : 3 * TRACE + 8]


def pack_states(states):
    lane = lane_ids(VECS)
    one = jnp.where(lane < TRACE, states[0], turned(states[3], TRACE))
    two = jnp.where(lane < TRACE, states[1], turned(states[3], 32))
    return jnp.concatenate([one, two, states[2]], axis=0)


def unpack_states(packed):
    lane = lane_ids(VECS)
    one, two, three = [packed[VECS * at : VECS * (at + 1)] for at in range(3)]
    four = jnp.where(lane < 48, turned(one, 48), turned(two, 96))
    return [jnp.where(lane < TRACE, x, 0.0) for x in (one, two, three, four)]


def after(first, second):
    nothing = jnp.zeros((TRACE, LANES), F32)
    added = jnp.concatenate([nothing, second[TRACE:]], axis=0) if first.shape[0] > VECS else second[TRACE:]
    return times(first, deep_rows(second[:TRACE])) + added


def source_kernel(
    ups, rhs, traces, down, from_above, outer, inner, from_across, diag, coupling, lift, passing, composed,
    solved, sources, packed, left, right,
):
    ups = ups_of(ups)
    stacks = [
        near_slots(layer, e, traces, down) | far_slots(layer, e, from_above, outer, inner, from_across)
        for layer in range(LAYERS)
        for e in range(PATCH)
    ]
    outflows = []
    lifts = lift_all(stacks, coupling, lift, left, right)
    for layer in range(LAYERS):
        own = range(layer * PATCH, (layer + 1) * PATCH)
        operands = [stacked(rhs[at] - lifts[at]) for at in own]
        results = [halves(dot(x, diag[at])) for x, at in zip(operands, own)]
        for at, y in zip(own, results):
            solved[at] = y
        outflows += [face_of(blocks_of(y), 1) for y in results]
        for at in own:
            sources[at] = outflows[at]
    current = outflows[:PATCH]
    for layer in range(1, LAYERS):
        moved = times_all(
            [chosen(current, ups[layer][e]) for e in range(PATCH)],
            [passing[layer * PATCH + e] for e in range(PATCH)],
        )
        current = [outflows[layer * PATCH + e] - moved[e] for e in range(PATCH)]
    starts = [chosen(ups[0], chosen(ups[1], ups[2][e])) for e in range(PATCH)]
    maps = placed([jnp.concatenate([composed[e], current[e]], axis=0) for e in range(PATCH)], starts)
    ends = placed([jnp.full((1, LANES), float(e), F32) for e in range(PATCH)], starts)
    packed[...] = pack(maps, ends_of(ends))


def after_all(firsts, seconds):
    tables = [deep_rows(x[:TRACE]) for x in seconds]
    added = [x[TRACE:] for x in seconds]
    if firsts[0].shape[0] > VECS:
        nothing = jnp.zeros((TRACE, LANES), F32)
        added = [jnp.concatenate([nothing, x], axis=0) for x in added]
    return [x + y for x, y in zip(times_all(firsts, tables), added)]


def ordered(mine, theirs, bit):
    later = (lax.axis_index("sweep") >> bit & 1) == 1
    first, first_ends = unpack(jnp.where(later, theirs, mine))
    second, second_ends = unpack(jnp.where(later, mine, theirs))
    return first, rows_of(first_ends), second, rows_of(second_ends)


def joined(mine, theirs, bit):
    first, first_ends, second, second_ends = ordered(mine, theirs, bit)
    maps = after_all(first, [chosen(second, at) for at in first_ends])
    return pack(maps, ends_of([chosen(second_ends, at) for at in first_ends]))


def pair_kernel(mine, theirs, packed):
    packed[...] = joined(mine[...], theirs[...], 0)


def group_kernel(mine, theirs, unused, packed):
    packed[...] = joined(mine[...], theirs[...], 1)


def leaving_kernel(mine, theirs, leaving):
    first, first_ends, second, second_ends = ordered(mine[...], theirs[...], 1)
    states = after_all([x[TRACE:] for x in first], [chosen(second, at) for at in first_ends])
    leaving[...] = pack_states(placed(states, [chosen(second_ends, at) for at in first_ends]))


def entry_kernel(
    pair, theirs, ups, passing, sources, weights, solved, tables, base, out_tables, out_added, starts
):
    me = lax.axis_index("sweep")
    partner, partner_ends = unpack(pair[...])
    row = lax.broadcasted_iota(jnp.int32, (MAP_ROWS, LANES), 0)
    same = (row == lane_ids(MAP_ROWS)).astype(F32)
    later = (me & 1) == 1
    own = [jnp.where(later, x, same) for x in partner]
    own_ends = [jnp.where(later, x, float(at)) for at, x in enumerate(rows_of(partner_ends))]
    first, first_ends = unpack(theirs[...])
    first_ends = rows_of(first_ends)
    later = (me >> 1 & 1) == 1
    maps, ends = [], []
    for at in range(PATCH):
        whole = after(first[at], chosen(own, first_ends[at]))
        maps.append(jnp.where(later, whole, own[at]))
        ends.append(jnp.where(later, chosen(own_ends, first_ends[at]), own_ends[at]))
    maps = placed(maps, ends)
    begin = placed([jnp.full((1, LANES), float(at), F32) for at in range(PATCH)], ends)
    ups = ups_of(ups)
    found, every = [], []
    nothing = jnp.zeros((TRACE, LANES), F32)
    for layer in range(LAYERS):
        begin = [chosen(begin, ups[layer][e]) for e in range(PATCH)]
        maps = [chosen(maps, ups[layer][e]) for e in range(PATCH)]
        found += begin
        every += maps
        maps = [
            jnp.concatenate([nothing, sources[layer * PATCH + e]], axis=0)
            - times(maps[e], passing[layer * PATCH + e])
            for e in range(PATCH)
        ]
    for e in range(PATCH):
        out_tables[e] = deep_rows(maps[e][:TRACE])
        out_added[e] = maps[e][TRACE:]
    for at in range(CELLS):
        product = times(every[at], weights[at])
        tables[at] = deep_rows(product[:TRACE])
        base[at] = solved[at] - product[TRACE:]
    starts[...] = jnp.concatenate(found + [jnp.zeros((16 - CELLS, LANES), F32)], axis=0)


def onward_kernel(entering, packed, leaving):
    maps, ends = unpack(packed[...])
    states = unpack_states(entering[...])
    states = after_all(states, maps)
    leaving[...] = pack_states(placed(states, rows_of(ends)))


def ahead_kernel(ups, front, solved, below, packed):
    maps = [
        jnp.concatenate([front[e], -face_of(blocks_of(solved[e]), 0)], axis=0) for e in range(PATCH)
    ]
    maps = placed(maps, ups_of(ups)[0])
    maps = [jnp.concatenate([x[:TRACE], x[TRACE:] + below[e]], axis=0) for e, x in enumerate(maps)]
    packed[...] = pack(maps, jnp.zeros((8, LANES), F32))


def finish_kernel(
    ups, second, third, fourth, before, tables, base, out_tables, out_added, starts, old,
    new, traces, inner, outer, across, down, leaving, made, sems,
):
    maps, map_ends = unpack(before[...])
    second, fourth, third = [unpack_states(x[...]) for x in (second, fourth, third)]
    states = after_all(fourth, maps)
    last = placed(states, rows_of(map_ends))
    entering = [second[at] + third[at] + last[at] for at in range(PATCH)]
    inflows = [deep_lhs(chosen(entering, starts[at : at + 1])) for at in range(CELLS)]
    products = [halves(dot(inflows[at], tables[at])) for at in range(CELLS)]
    found = [base[at] - products[at] for at in range(CELLS)]
    for at in range(CELLS):
        made[at] = found[at]
    copy = pltpu.make_async_copy(made, new, sems.at[0])
    copy.start()
    changes = [old[at] - found[at] for at in range(CELLS)]
    put_down(put_sides(changes, traces, inner, outer, across), ups_of(ups), down)
    for e in range(PATCH):
        leaving[e] = halves(dot(inflows[(LAYERS - 1) * PATCH + e], out_tables[e])) + out_added[e]
    copy.wait()


def near_residual_kernel(traces, down, leaving, ahead, coupling, lift, out, left, right):
    stacks = [near_slots(layer, e, traces, down) for layer in range(LAYERS) for e in range(PATCH)]
    maps, unused = unpack(ahead[...])
    for e in range(PATCH):
        stacks[(LAYERS - 1) * PATCH + e][1] = stacked(after(leaving[e], maps[e]))
    for at, x in enumerate(lift_all(stacks, coupling, lift, left, right)):
        out[at] = x


def residual_kernel(near, outer, inner, from_across, coupling, lift, out, left, right):
    stacks = [
        far_slots(layer, e, None, outer, inner, from_across) for layer in range(LAYERS) for e in range(PATCH)
    ]
    for at, x in enumerate(lift_all(stacks, coupling, lift, left, right)):
        out[at] = near[at] + x


VMEM = pl.BlockSpec(memory_space=pltpu.VMEM)
FAR = pl.BlockSpec(memory_space=pl.ANY)


def call(kernel, outs, scratch=(), far_outs=(), micros=1):
    def run(*args):
        return pl.pallas_call(
            kernel,
            in_specs=[VMEM] * len(args),
            out_specs=[FAR if i in far_outs else VMEM for i in range(len(outs))],
            out_shape=[jax.ShapeDtypeStruct(shape, kind) for shape, kind in outs],
            scratch_shapes=list(scratch),
            compiler_params=pltpu.CompilerParams(vmem_limit_bytes=16 * 1024 * 1024),
            cost_estimate=pl.CostEstimate(
                flops=micros * 1_000_000_000, bytes_accessed=micros * 3_600_000, transcendentals=0
            ),
        )(*args)

    return run


SIDE_OUTS = [
    ((CELLS, 2 * VECS, (len(SLOT_FACES) - 1) * LANES), BF16),
    ((LAYERS * EY, VECS, LANES), F32),
    ((LAYERS * EY, VECS, LANES), F32),
    ((LAYERS * EX, VECS, LANES), F32),
]
BELOW = ((LAYERS * EY, VECS, LANES), F32)
DOWN = (((LAYERS - 1) * PATCH, 2 * VECS, LANES), BF16)
ROW_TILE = ((16, LANES), F32)
FLUXES = [pltpu.VMEM((CELLS * 2 * VECS, DEEP), BF16), pltpu.VMEM((CELLS * 2 * VECS, 6 * TRACE - DEEP), BF16)]
FIELD = ((CELLS, VECS, ROWS), F32)
STATES = ((3 * VECS, LANES), F32)
PACKED = ((3 * TRACE + 8, LANES), F32)


def from_next(piece):
    return lax.ppermute(piece, "sweep", [(i + 1, i) for i in range(lax.axis_size("sweep") - 1)])


def exchange_sides(outer, inner, across):
    wide = lax.axis_size("cx")
    outer = lax.ppermute(outer, "cx", [(i, i + 1 if i % 2 else i - 1) for i in range(1, wide - 1)])
    inner = lax.ppermute(inner, "cx", [(i, i ^ 1) for i in range(wide)])
    across = lax.ppermute(across, "cy", [(0, 1), (1, 0)])
    return outer, inner, across


def swapped(packed, by):
    return lax.ppermute(packed, "sweep", [(i, i ^ by) for i in range(lax.axis_size("sweep"))])


def passed(states, source, target, shift):
    pairs = [(GROUP * source + p, GROUP * target + (p + shift) % GROUP) for p in range(GROUP)]
    return lax.ppermute(states, "sweep", pairs)


def local(rhs_vectors, old_iterate, diag_inverse, coupling, lift_table, upstream):
    old = old_iterate.reshape(CELLS, VECS, ROWS)
    rhs = rhs_vectors.reshape(CELLS, VECS, ROWS)
    diag = diag_inverse.reshape(CELLS, ROWS, ROWS)
    blocks = coupling.reshape(CELLS, TRACE, 6 * TRACE)
    lift = lift_table.T
    traces, inner, outer, across, faces = call(
        open_kernel, SIDE_OUTS + [((CELLS, 2 * VECS, LANES), F32)], micros=2
    )(old)
    ups, down, below = call(position_kernel, [ROW_TILE, DOWN, BELOW])(upstream.transpose(1, 2, 0), faces)
    halos = (from_next(below),) + exchange_sides(outer, inner, across)
    lifted_rows, passing, composed = call(
        transfer_kernel,
        [((CELLS, DEEP, ROWS), BF16), ((CELLS, DEEP, LANES), BF16), ((PATCH, TRACE, LANES), F32)],
        [pltpu.VMEM((CELLS, DEEP, LANES), BF16), pltpu.VMEM((PATCH, TRACE, LANES), F32)],
    )(ups, diag, blocks, lift)
    solved, sources, single = call(source_kernel, [FIELD, ((CELLS, VECS, LANES), F32), PACKED], FLUXES)(
        ups, rhs, traces, down, *halos, diag, blocks, lift, passing, composed
    )
    partner = swapped(single, 1)
    (pair,) = call(pair_kernel, [PACKED])(single, partner)
    partner_pair = swapped(pair, 2)
    weights, front = call(weight_kernel, [((CELLS, DEEP, ROWS), BF16), ((PATCH, TRACE, LANES), F32)])(
        blocks, lifted_rows, pair
    )
    (ahead,) = call(ahead_kernel, [PACKED])(ups, front, solved, below)
    ahead = from_next(ahead)
    (leaving,) = call(leaving_kernel, [STATES])(pair, partner_pair)
    second = passed(leaving, 0, 1, 2)
    (group,) = call(group_kernel, [PACKED])(pair, partner_pair, leaving)
    before = passed(group, 2, 3, 2)
    (leaving,) = call(onward_kernel, [STATES])(second, group)
    third = passed(leaving, 1, 2, 2)
    fourth = passed(leaving, 1, 3, 0)
    maps = call(
        entry_kernel,
        [
            ((CELLS, DEEP, ROWS), BF16),
            FIELD,
            ((PATCH, DEEP, LANES), BF16),
            ((PATCH, VECS, LANES), F32),
            ROW_TILE,
        ],
    )(partner, partner_pair, ups, passing, sources, weights, solved)
    new, traces, inner, outer, across, down, leaving = call(
        finish_kernel,
        [FIELD] + SIDE_OUTS + [DOWN, ((PATCH, VECS, LANES), F32)],
        [pltpu.VMEM((CELLS, VECS, ROWS), F32), pltpu.SemaphoreType.DMA((1,))],
        far_outs=(0,),
    )(ups, second, third, fourth, before, *maps, old)
    halos = exchange_sides(outer, inner, across)
    (near,) = call(near_residual_kernel, [FIELD], FLUXES)(traces, down, leaving, ahead, blocks, lift)
    (residual,) = call(residual_kernel, [FIELD], FLUXES)(near, *halos, blocks, lift)
    shape = rhs_vectors.shape
    return new.reshape(shape), residual.reshape(shape)


def solution(mesh):
    field = P("sweep", "cx", "cy", None, None)
    return jax.shard_map(
        local,
        mesh=mesh,
        in_specs=(field, field, field, field, P(), P("sweep", "cx", "cy")),
        out_specs=(field, field),
        check_vma=False,
    )
```

```python
import jax
import jax.numpy as jnp
from jax import lax
from jax.experimental import pallas as pl
from jax.experimental.pallas import tpu as pltpu
from jax.sharding import PartitionSpec as P

NPOINT = 4
ROWS = 320
TRACE = 80
VECS = 16
LAYERS = 3
EX = 2
EY = 2
PATCH = EX * EY
CELLS = LAYERS * PATCH
LANES = 128
DEEP = 2 * LANES
GROUP = 4
NODES = NPOINT**3
MAP_ROWS = TRACE + VECS
BF16 = jnp.bfloat16
F32 = jnp.float32

FACE_ROWS = ((0, 16, 4), (3, 16, 4), (0, 4, 1), (48, 4, 1), (0, 16, 1), (12, 16, 1))
SLOT_FACES = (0, 3, 2, 5, 4)


def split(x):
    high = x.astype(BF16)
    low = (x - high.astype(F32)).astype(BF16)
    return high, low


def stacked(x):
    return jnp.concatenate(split(x), axis=0)


def dot(a, b):
    return jnp.dot(a, b, preferred_element_type=F32)


def dot_rows(a, b):
    return lax.dot_general(a, b, (((1,), (1,)), ((), ())), preferred_element_type=F32)


def halves(x):
    rows = x.shape[0] // 2
    return x[:rows] + x[rows:]


def deep_rows(table):
    high, low = split(table)
    gap = jnp.zeros((LANES - TRACE, table.shape[1]), BF16)
    return jnp.concatenate([high, gap, low, gap], axis=0)


def deep_lhs(x):
    high, low = split(x)
    return jnp.concatenate(
        [jnp.concatenate([high, high], axis=1), jnp.concatenate([low, low], axis=1)], axis=0
    )


def times(x, deep):
    return halves(dot(deep_lhs(x), deep))


def lane_take(x, index):
    return jnp.take_along_axis(x, index, axis=1)


def lane_ids(rows):
    return lax.broadcasted_iota(jnp.int32, (rows, LANES), 1)


def blocks_of(x):
    rest = ROWS - 2 * LANES
    tail = jnp.concatenate([x[:, 2 * LANES :], jnp.zeros((x.shape[0], LANES - rest), x.dtype)], axis=1)
    return x[:, :LANES], x[:, LANES : 2 * LANES], tail


def face_of(blocks, face):
    start, a_step, b_step = FACE_ROWS[face]
    lane = lane_ids(blocks[0].shape[0])
    entry = lane & 15
    index = (lane >> 4 & 1) * NODES + start + (entry >> 2) * a_step + (entry & 3) * b_step
    first, second, third = [lane_take(block, index) for block in blocks]
    third = jnp.where(lane < TRACE, third, 0.0)
    return jnp.where(lane < 32, first, jnp.where(lane < 64, second, third))


def side_table():
    row = lax.broadcasted_iota(jnp.int32, (ROWS, LANES), 0)
    lane = lane_ids(1)
    blocks = []
    for face in SLOT_FACES:
        start, a_step, b_step = FACE_ROWS[face]
        source = (lane >> 4) * NODES + start + (lane >> 2 & 3) * a_step + (lane & 3) * b_step
        source = jnp.where(lane < TRACE, source, -1)
        blocks.append(jnp.where(row == source, 1.0, 0.0).astype(BF16))
    return jnp.concatenate(blocks, axis=1)


def rows_of(ends):
    return [ends[at : at + 1] for at in range(PATCH)]


def ends_of(rows):
    return jnp.concatenate(list(rows) + [jnp.zeros((8 - PATCH, LANES), F32)], axis=0)


def chosen(items, at):
    out = items[0]
    for number in range(1, PATCH):
        out = jnp.where(at == number, items[number], out)
    return out


def placed(states, ends):
    out = []
    for position in range(PATCH):
        total = jnp.where(ends[0] == position, states[0], 0.0)
        for at in range(1, PATCH):
            total = total + jnp.where(ends[at] == position, states[at], 0.0)
        out.append(total)
    return out


def ups_of(ups):
    return [[ups[layer * PATCH + e : layer * PATCH + e + 1] for e in range(PATCH)] for layer in range(LAYERS)]


def position_rows(links):
    found = []
    lane = lax.broadcasted_iota(jnp.int32, (EY, LAYERS), 1)
    for layer in range(LAYERS):
        for a in range(EX):
            value = jnp.sum(jnp.where(lane == layer, links[a], 0).astype(F32), axis=1, keepdims=True)
            found.append(jnp.broadcast_to(value, (EY, LANES)))
    return jnp.concatenate(found + [jnp.zeros((16 - CELLS, LANES), F32)], axis=0)


def put_sides(cells, traces, inner, outer, across):
    core = lax.axis_index("cy")
    even = lax.rem(lax.axis_index("cx"), 2) == 0
    picked = dot(jnp.concatenate([stacked(x) for x in cells], axis=0), side_table())
    pieces = [picked[2 * VECS * at : 2 * VECS * (at + 1)] for at in range(CELLS)]
    whole = [halves(piece[:, LANES:]) for piece in pieces]
    for layer in range(LAYERS):
        block = lambda e, s: whole[layer * PATCH + e][:, (s - 1) * LANES : s * LANES]
        for e in range(PATCH):
            traces[layer * PATCH + e] = pieces[layer * PATCH + e][:, LANES:].astype(BF16)
        for b in range(EY):
            east, west = block(EY + b, 1), block(b, 2)
            inner[layer * EY + b] = jnp.where(even, east, west)
            outer[layer * EY + b] = jnp.where(even, west, east)
        for a in range(EX):
            across[layer * EX + a] = jnp.where(core == 0, block(a * EY + 1, 3), block(a * EY, 4))
    return [piece[:, :LANES] for piece in pieces]


def put_below(pieces, ups, below):
    for e, state in enumerate(placed([halves(pieces[e]) for e in range(PATCH)], ups[0])):
        below[e] = state
    for e in range(PATCH, LAYERS * EY):
        below[e] = jnp.zeros((VECS, LANES), F32)


def put_down(pieces, ups, down):
    for layer in range(1, LAYERS):
        for e, piece in enumerate(placed(pieces[layer * PATCH : (layer + 1) * PATCH], ups[layer])):
            down[(layer - 1) * PATCH + e] = piece.astype(BF16)


def open_kernel(old, traces, inner, outer, across, faces):
    for at, piece in enumerate(put_sides([old[at] for at in range(CELLS)], traces, inner, outer, across)):
        faces[at] = piece


def position_kernel(links, faces, ups, down, below):
    rows = position_rows(links)
    ups[...] = rows
    pieces = [faces[at] for at in range(CELLS)]
    put_below(pieces, ups_of(rows), below)
    put_down(pieces, ups_of(rows), down)


def near_slots(layer, e, traces, down):
    a, b = e // EY, e % EY
    own = lambda cell, s: traces[layer * PATCH + cell, :, (s - 1) * LANES : s * LANES]
    slots = {}
    if layer < LAYERS - 1:
        slots[1] = down[layer * PATCH + e]
    slots[2 if a == 1 else 3] = own(b, 1) if a == 1 else own(EY + b, 2)
    slots[4 if b == 1 else 5] = own(a * EY, 3) if b == 1 else own(a * EY + 1, 4)
    return slots


def far_slots(layer, e, from_above, outer, inner, from_across):
    core = lax.axis_index("cy")
    even = lax.rem(lax.axis_index("cx"), 2) == 0
    a, b = e // EY, e % EY
    close, wide = inner[layer * EY + b], outer[layer * EY + b]
    other = from_across[layer * EX + a]
    slots = {}
    if layer == LAYERS - 1 and from_above is not None:
        slots[1] = stacked(from_above[e])
    slots[2 if a == 0 else 3] = stacked(jnp.where(even, wide, close) if a == 0 else jnp.where(even, close, wide))
    slots[4 if b == 0 else 5] = stacked(jnp.where(core == (1 if b == 0 else 0), other, 0.0))
    return slots


def lift_all(stacks, coupling, lift, left, right):
    lane = lax.broadcasted_iota(jnp.int32, (2 * VECS, DEEP), 1)
    r = 2 * VECS
    for at, slots in enumerate(stacks):
        for begin, numbers, kept_rows in ((0, (1, 2, 3), left), (DEEP, (3, 4, 5), right)):
            present = [slot for slot in numbers if slot in slots]
            y = dot(
                jnp.concatenate([slots[slot] for slot in present], axis=0)[:, :TRACE],
                coupling[at, :, begin : min(begin + DEEP, 6 * TRACE)],
            )
            place = lane[:, : y.shape[1]] + begin
            kept = jnp.zeros((r, y.shape[1]), F32)
            for i, slot in enumerate(present):
                inside = (place >= slot * TRACE) & (place < (slot + 1) * TRACE)
                kept = jnp.where(inside, y[r * i : r * (i + 1)], kept)
            kept_rows[r * at : r * (at + 1)] = stacked(halves(kept))
    out = dot_rows(left[...], lift[:, :DEEP]) + dot_rows(right[...], lift[:, DEEP:])
    return [halves(out[r * at : r * (at + 1)]) for at in range(CELLS)]


def transfer_kernel(ups, diag, coupling, lift, lifted_rows, passing, composed, outflows, first):
    ups = ups_of(ups)
    one = lax.broadcasted_iota(jnp.int32, (TRACE, TRACE), 0)
    two = lax.broadcasted_iota(jnp.int32, (TRACE, TRACE), 1)
    inflow = dot_rows((one == two).astype(F32).astype(BF16), lift[:, :TRACE]).astype(BF16)
    upper, lower = inflow[:NODES, :DEEP], inflow[NODES:, DEEP:]
    for at in range(CELLS):
        lifts = jnp.concatenate([dot(upper, diag[at, :DEEP]), dot(lower, diag[at, DEEP:])], axis=0)
        lifted_rows[at] = deep_rows(lifts)
        outflows[at] = deep_rows(face_of(blocks_of(lifts), 1))
    for at in range(CELLS):
        upwind = coupling[at, :, :LANES]
        passed_on = dot(jnp.concatenate([upwind, upwind], axis=1), outflows[at])
        passing[at] = deep_rows(passed_on)
        if at < PATCH:
            first[at] = passed_on
    source = [first[e] for e in range(PATCH)]
    both = [times(chosen(source, ups[1][e]), passing[PATCH + e]) for e in range(PATCH)]
    for e in range(PATCH):
        composed[e] = -times(chosen(both, ups[2][e]), passing[2 * PATCH + e])


def weight_kernel(coupling, lifted_rows, unused, weights, front):
    for at in range(CELLS):
        upwind = coupling[at, :, :LANES]
        weight = dot(jnp.concatenate([upwind, upwind], axis=1), lifted_rows[at])
        weights[at] = deep_rows(weight)
        if at < PATCH:
            front[at] = face_of(blocks_of(weight), 0)


def turned(x, by):
    return pltpu.roll(x, by % LANES, 1)


def pack(maps, ends):
    lane = lane_ids(TRACE)
    square = [x[:TRACE] for x in maps]
    source = [x[TRACE:] for x in maps]
    all_sources = jnp.concatenate(source, axis=0)
    part = lane_ids(VECS) >> 4
    last = jnp.where(part == 5, turned(source[0], 16), jnp.where(part == 6, turned(source[1], 32), turned(source[2], 48)))
    one = jnp.where(lane < TRACE, square[0], turned(square[3], TRACE))
    rest = jnp.concatenate([turned(all_sources, 64), turned(source[3], 48)], axis=0)
    two = jnp.where(lane < TRACE, square[1], jnp.where(lane < 112, turned(square[3], 32), rest))
    three = jnp.where(lane < TRACE, square[2], jnp.concatenate([turned(all_sources, TRACE), last], axis=0))
    return jnp.concatenate([one, two, three, ends], axis=0)


def unpack(packed):
    lane = lane_ids(TRACE)
    one, two, three = [packed[TRACE * at : TRACE * (at + 1)] for at in range(3)]
    four = jnp.where(lane < 48, turned(one, 48), turned(two, 96))
    square = [jnp.where(lane < TRACE, x, 0.0) for x in (one, two, three, four)]
    lane = lane_ids(PATCH * VECS)
    most = jnp.where(lane < 48, turned(three[: PATCH * VECS], 48), turned(two[: PATCH * VECS], 64))
    ends = [turned(three[PATCH * VECS :], by) for by in (112, 96, 80)] + [turned(two[PATCH * VECS :], 80)]
    lane = lane_ids(VECS)
    maps = []
    for at in range(PATCH):
        source = jnp.where(lane < 64, most[VECS * at : VECS * (at + 1)], jnp.where(lane < TRACE, ends[at], 0.0))
        maps.append(jnp.concatenate([square[at], source], axis=0))
    return maps, packed[3 * TRACE : 3 * TRACE + 8]


def pack_states(states):
    lane = lane_ids(VECS)
    one = jnp.where(lane < TRACE, states[0], turned(states[3], TRACE))
    two = jnp.where(lane < TRACE, states[1], turned(states[3], 32))
    return jnp.concatenate([one, two, states[2]], axis=0)


def unpack_states(packed):
    lane = lane_ids(VECS)
    one, two, three = [packed[VECS * at : VECS * (at + 1)] for at in range(3)]
    four = jnp.where(lane < 48, turned(one, 48), turned(two, 96))
    return [jnp.where(lane < TRACE, x, 0.0) for x in (one, two, three, four)]


def after(first, second):
    nothing = jnp.zeros((TRACE, LANES), F32)
    added = jnp.concatenate([nothing, second[TRACE:]], axis=0) if first.shape[0] > VECS else second[TRACE:]
    return times(first, deep_rows(second[:TRACE])) + added


def source_kernel(
    ups, rest, from_above, outer, inner, from_across, diag, coupling, lift, passing, composed,
    solved, sources, packed, left, right,
):
    ups = ups_of(ups)
    stacks = [
        far_slots(layer, e, from_above, outer, inner, from_across) for layer in range(LAYERS) for e in range(PATCH)
    ]
    outflows = []
    for at, x in enumerate(lift_all(stacks, coupling, lift, left, right)):
        y = halves(dot(stacked(rest[at] - x), diag[at]))
        solved[at] = y
        outflows.append(face_of(blocks_of(y), 1))
        sources[at] = outflows[at]
    current = outflows[:PATCH]
    for layer in range(1, LAYERS):
        current = [
            outflows[layer * PATCH + e] - times(chosen(current, ups[layer][e]), passing[layer * PATCH + e])
            for e in range(PATCH)
        ]
    starts = [chosen(ups[0], chosen(ups[1], ups[2][e])) for e in range(PATCH)]
    maps = placed([jnp.concatenate([composed[e], current[e]], axis=0) for e in range(PATCH)], starts)
    ends = placed([jnp.full((1, LANES), float(e), F32) for e in range(PATCH)], starts)
    packed[...] = pack(maps, ends_of(ends))


def ordered(mine, theirs, bit):
    later = (lax.axis_index("sweep") >> bit & 1) == 1
    first, first_ends = unpack(jnp.where(later, theirs, mine))
    second, second_ends = unpack(jnp.where(later, mine, theirs))
    return first, rows_of(first_ends), second, rows_of(second_ends)


def joined(mine, theirs, bit):
    first, first_ends, second, second_ends = ordered(mine, theirs, bit)
    maps = [after(first[at], chosen(second, first_ends[at])) for at in range(PATCH)]
    return pack(maps, ends_of([chosen(second_ends, at) for at in first_ends]))


def pair_kernel(mine, theirs, packed):
    packed[...] = joined(mine[...], theirs[...], 0)


def group_kernel(mine, theirs, unused, packed):
    packed[...] = joined(mine[...], theirs[...], 1)


def leaving_kernel(mine, theirs, leaving):
    first, first_ends, second, second_ends = ordered(mine[...], theirs[...], 1)
    states = [after(first[at][TRACE:], chosen(second, first_ends[at])) for at in range(PATCH)]
    leaving[...] = pack_states(placed(states, [chosen(second_ends, at) for at in first_ends]))


def entry_kernel(
    pair, theirs, ups, passing, sources, weights, solved, tables, base, out_tables, out_added, starts
):
    me = lax.axis_index("sweep")
    partner, partner_ends = unpack(pair[...])
    row = lax.broadcasted_iota(jnp.int32, (MAP_ROWS, LANES), 0)
    same = (row == lane_ids(MAP_ROWS)).astype(F32)
    later = (me & 1) == 1
    own = [jnp.where(later, x, same) for x in partner]
    own_ends = [jnp.where(later, x, float(at)) for at, x in enumerate(rows_of(partner_ends))]
    first, first_ends = unpack(theirs[...])
    first_ends = rows_of(first_ends)
    later = (me >> 1 & 1) == 1
    maps, ends = [], []
    for at in range(PATCH):
        whole = after(first[at], chosen(own, first_ends[at]))
        maps.append(jnp.where(later, whole, own[at]))
        ends.append(jnp.where(later, chosen(own_ends, first_ends[at]), own_ends[at]))
    maps = placed(maps, ends)
    begin = placed([jnp.full((1, LANES), float(at), F32) for at in range(PATCH)], ends)
    ups = ups_of(ups)
    found, every = [], []
    nothing = jnp.zeros((TRACE, LANES), F32)
    for layer in range(LAYERS):
        begin = [chosen(begin, ups[layer][e]) for e in range(PATCH)]
        maps = [chosen(maps, ups[layer][e]) for e in range(PATCH)]
        found += begin
        every += maps
        maps = [
            jnp.concatenate([nothing, sources[layer * PATCH + e]], axis=0)
            - times(maps[e], passing[layer * PATCH + e])
            for e in range(PATCH)
        ]
    for e in range(PATCH):
        out_tables[e] = deep_rows(maps[e][:TRACE])
        out_added[e] = maps[e][TRACE:]
    for at in range(CELLS):
        product = times(every[at], weights[at])
        tables[at] = deep_rows(product[:TRACE])
        base[at] = solved[at] - product[TRACE:]
    starts[...] = jnp.concatenate(found + [jnp.zeros((16 - CELLS, LANES), F32)], axis=0)


def onward_kernel(entering, packed, leaving):
    maps, ends = unpack(packed[...])
    states = unpack_states(entering[...])
    states = [after(states[at], maps[at]) for at in range(PATCH)]
    leaving[...] = pack_states(placed(states, rows_of(ends)))


def ahead_kernel(ups, front, solved, below, packed):
    maps = [
        jnp.concatenate([front[e], -face_of(blocks_of(solved[e]), 0)], axis=0) for e in range(PATCH)
    ]
    maps = placed(maps, ups_of(ups)[0])
    maps = [jnp.concatenate([x[:TRACE], x[TRACE:] + below[e]], axis=0) for e, x in enumerate(maps)]
    packed[...] = pack(maps, jnp.zeros((8, LANES), F32))


def finish_kernel(
    ups, second, third, fourth, before, tables, base, out_tables, out_added, starts, old,
    new, traces, inner, outer, across, down, leaving, made, sems,
):
    maps, map_ends = unpack(before[...])
    second, fourth, third = [unpack_states(x[...]) for x in (second, fourth, third)]
    states = [after(fourth[at], maps[at]) for at in range(PATCH)]
    last = placed(states, rows_of(map_ends))
    entering = [second[at] + third[at] + last[at] for at in range(PATCH)]
    inflows = [deep_lhs(chosen(entering, starts[at : at + 1])) for at in range(CELLS)]
    products = [halves(dot(inflows[at], tables[at])) for at in range(CELLS)]
    found = [base[at] - products[at] for at in range(CELLS)]
    for at in range(CELLS):
        made[at] = found[at]
    copy = pltpu.make_async_copy(made, new, sems.at[0])
    copy.start()
    changes = [old[at] - found[at] for at in range(CELLS)]
    put_down(put_sides(changes, traces, inner, outer, across), ups_of(ups), down)
    for e in range(PATCH):
        leaving[e] = halves(dot(inflows[(LAYERS - 1) * PATCH + e], out_tables[e])) + out_added[e]
    copy.wait()


def near_source_kernel(rhs, traces, down, coupling, lift, out, left, right):
    stacks = [near_slots(layer, e, traces, down) for layer in range(LAYERS) for e in range(PATCH)]
    for at, x in enumerate(lift_all(stacks, coupling, lift, left, right)):
        out[at] = rhs[at] - x


def near_residual_kernel(traces, down, leaving, ahead, coupling, lift, out, left, right):
    stacks = [near_slots(layer, e, traces, down) for layer in range(LAYERS) for e in range(PATCH)]
    maps, unused = unpack(ahead[...])
    for e in range(PATCH):
        stacks[(LAYERS - 1) * PATCH + e][1] = stacked(after(leaving[e], maps[e]))
    for at, x in enumerate(lift_all(stacks, coupling, lift, left, right)):
        out[at] = x


def residual_kernel(near, outer, inner, from_across, coupling, lift, out, left, right):
    stacks = [
        far_slots(layer, e, None, outer, inner, from_across) for layer in range(LAYERS) for e in range(PATCH)
    ]
    for at, x in enumerate(lift_all(stacks, coupling, lift, left, right)):
        out[at] = near[at] + x


VMEM = pl.BlockSpec(memory_space=pltpu.VMEM)
FAR = pl.BlockSpec(memory_space=pl.ANY)


def call(kernel, outs, scratch=(), far_outs=(), micros=1):
    def run(*args):
        return pl.pallas_call(
            kernel,
            in_specs=[VMEM] * len(args),
            out_specs=[FAR if i in far_outs else VMEM for i in range(len(outs))],
            out_shape=[jax.ShapeDtypeStruct(shape, kind) for shape, kind in outs],
            scratch_shapes=list(scratch),
            compiler_params=pltpu.CompilerParams(vmem_limit_bytes=16 * 1024 * 1024),
            cost_estimate=pl.CostEstimate(
                flops=micros * 1_000_000_000, bytes_accessed=micros * 3_600_000, transcendentals=0
            ),
        )(*args)

    return run


SIDE_OUTS = [
    ((CELLS, 2 * VECS, (len(SLOT_FACES) - 1) * LANES), BF16),
    ((LAYERS * EY, VECS, LANES), F32),
    ((LAYERS * EY, VECS, LANES), F32),
    ((LAYERS * EX, VECS, LANES), F32),
]
BELOW = ((LAYERS * EY, VECS, LANES), F32)
DOWN = (((LAYERS - 1) * PATCH, 2 * VECS, LANES), BF16)
ROW_TILE = ((16, LANES), F32)
FLUXES = [pltpu.VMEM((CELLS * 2 * VECS, DEEP), BF16), pltpu.VMEM((CELLS * 2 * VECS, 6 * TRACE - DEEP), BF16)]
FIELD = ((CELLS, VECS, ROWS), F32)
STATES = ((3 * VECS, LANES), F32)
PACKED = ((3 * TRACE + 8, LANES), F32)


def from_next(piece):
    return lax.ppermute(piece, "sweep", [(i + 1, i) for i in range(lax.axis_size("sweep") - 1)])


def exchange_sides(outer, inner, across):
    wide = lax.axis_size("cx")
    outer = lax.ppermute(outer, "cx", [(i, i + 1 if i % 2 else i - 1) for i in range(1, wide - 1)])
    inner = lax.ppermute(inner, "cx", [(i, i ^ 1) for i in range(wide)])
    across = lax.ppermute(across, "cy", [(0, 1), (1, 0)])
    return outer, inner, across


def swapped(packed, by):
    return lax.ppermute(packed, "sweep", [(i, i ^ by) for i in range(lax.axis_size("sweep"))])


def passed(states, source, target, shift):
    pairs = [(GROUP * source + p, GROUP * target + (p + shift) % GROUP) for p in range(GROUP)]
    return lax.ppermute(states, "sweep", pairs)


def local(rhs_vectors, old_iterate, diag_inverse, coupling, lift_table, upstream):
    old = old_iterate.reshape(CELLS, VECS, ROWS)
    rhs = rhs_vectors.reshape(CELLS, VECS, ROWS)
    diag = diag_inverse.reshape(CELLS, ROWS, ROWS)
    blocks = coupling.reshape(CELLS, TRACE, 6 * TRACE)
    lift = lift_table.T
    traces, inner, outer, across, faces = call(
        open_kernel, SIDE_OUTS + [((CELLS, 2 * VECS, LANES), F32)], micros=2
    )(old)
    ups, down, below = call(position_kernel, [ROW_TILE, DOWN, BELOW])(upstream.transpose(1, 2, 0), faces)
    halos = (from_next(below),) + exchange_sides(outer, inner, across)
    lifted_rows, passing, composed = call(
        transfer_kernel,
        [((CELLS, DEEP, ROWS), BF16), ((CELLS, DEEP, LANES), BF16), ((PATCH, TRACE, LANES), F32)],
        [pltpu.VMEM((CELLS, DEEP, LANES), BF16), pltpu.VMEM((PATCH, TRACE, LANES), F32)],
    )(ups, diag, blocks, lift)
    (rest,) = call(near_source_kernel, [FIELD], FLUXES)(rhs, traces, down, blocks, lift)
    solved, sources, single = call(source_kernel, [FIELD, ((CELLS, VECS, LANES), F32), PACKED], FLUXES)(
        ups, rest, *halos, diag, blocks, lift, passing, composed
    )
    partner = swapped(single, 1)
    (pair,) = call(pair_kernel, [PACKED])(single, partner)
    partner_pair = swapped(pair, 2)
    weights, front = call(weight_kernel, [((CELLS, DEEP, ROWS), BF16), ((PATCH, TRACE, LANES), F32)])(
        blocks, lifted_rows, pair
    )
    (ahead,) = call(ahead_kernel, [PACKED])(ups, front, solved, below)
    ahead = from_next(ahead)
    (leaving,) = call(leaving_kernel, [STATES])(pair, partner_pair)
    second = passed(leaving, 0, 1, 2)
    (group,) = call(group_kernel, [PACKED])(pair, partner_pair, leaving)
    before = passed(group, 2, 3, 2)
    (leaving,) = call(onward_kernel, [STATES])(second, group)
    third = passed(leaving, 1, 2, 2)
    fourth = passed(leaving, 1, 3, 0)
    maps = call(
        entry_kernel,
        [
            ((CELLS, DEEP, ROWS), BF16),
            FIELD,
            ((PATCH, DEEP, LANES), BF16),
            ((PATCH, VECS, LANES), F32),
            ROW_TILE,
        ],
    )(partner, partner_pair, ups, passing, sources, weights, solved)
    new, traces, inner, outer, across, down, leaving = call(
        finish_kernel,
        [FIELD] + SIDE_OUTS + [DOWN, ((PATCH, VECS, LANES), F32)],
        [pltpu.VMEM((CELLS, VECS, ROWS), F32), pltpu.SemaphoreType.DMA((1,))],
        far_outs=(0,),
    )(ups, second, third, fourth, before, *maps, old)
    halos = exchange_sides(outer, inner, across)
    (near,) = call(near_residual_kernel, [FIELD], FLUXES)(traces, down, leaving, ahead, blocks, lift)
    (residual,) = call(residual_kernel, [FIELD], FLUXES)(near, *halos, blocks, lift)
    shape = rhs_vectors.shape
    return new.reshape(shape), residual.reshape(shape)


def solution(mesh):
    field = P("sweep", "cx", "cy", None, None)
    return jax.shard_map(
        local,
        mesh=mesh,
        in_specs=(field, field, field, field, P(), P("sweep", "cx", "cy")),
        out_specs=(field, field),
        check_vma=False,
    )
```
